256 devices in a mesh: gx: 16 (over z, core), gy: 16 (over y, x).
Axes of the slice: x: 4, y: 4, z: 8, core: 2. Of those that a mesh axis runs over, the one named last changes fastest.
Arguments:
- material: int32 [256, 256, 128], P('gx', 'gy'), may hold values from 0 to 7
- velocity: float32 [8], replicated, may hold values from 1.5 to 4.5
- density: float32 [8], replicated, may hold values from 1 to 2.2
- right_side: float32 [256, 256, 128], P('gx', 'gy'), may hold values from -24 to 24
Outputs:
- fine_solution: float32 [256, 256, 128], P('gx', 'gy')
- mid_solution: float32 [128, 128, 64], P('gx', 'gy')
- coarse_solution: float32 [64, 64, 32], P('gx', 'gy')
The draws below stay inside these ranges and needn't reach their ends.
Inputs may be any that keep to these rules, and one draw needn't show every extreme that they name: Each cell's material selects its row of the velocity and density tables.
All inputs are finite; a program needn't handle non-finite values.
Results may differ from the reference program's by a relative error of at most 0.0003.
Values sent between devices are 32-bit elements; how exact they have to be, the bound alone decides.
No kernel may reach another device: no remote copies, remote signals or barrier semaphores. Data moves between devices by JAX's collectives and lax.ppermute only.
A program may use at most 128 MiB of HBM per device.

```python
import jax
import jax.numpy as jnp
from jax import lax

MATS = 8
SWEEPS_FINE = 2
SWEEPS_MID = 2
SWEEPS_COARSE = 4
NX = 256
NY = 256
NZ = 128


def place_ends(array, own_key, low, top_value):
    longest = array.shape.index(max(array.shape))
    spots = []
    for shift in (0, 1):
        where = [jax.random.randint(jax.random.fold_in(own_key, axis), (), 0, length) for axis, length in enumerate(array.shape)]
        where[longest] = (where[longest] + shift) % array.shape[longest]
        spots.append(tuple(where))
    return array.at[spots[0]].set(low).at[spots[1]].set(top_value)


def steps_of(key, extent, pieces, least, top_value):
    loudness, own = 1.0, jax.random.fold_in(key, 6)
    for dim, shards_of in pieces:
        heights = jnp.exp(jax.random.uniform(jax.random.fold_in(own, dim), (shards_of,), jnp.float32, least / len(pieces), top_value / len(pieces)))
        loudness = loudness * jnp.repeat(heights, extent[dim] // shards_of).reshape([-1 if axis == dim else 1 for axis in range(len(extent))])
    return loudness


def centred(stream_key, shape, width, bound, split=(), held_as=jnp.bfloat16):
    entries = jax.random.normal(stream_key, shape, jnp.float32) * width
    if len(split) > 0:
        entries = steps_of(stream_key, shape, split, -0.22, 0.18) * entries
    return jnp.clip(entries, min=-bound, max=bound).astype(held_as)


def setup_inputs(seed: int = 0) -> dict:
    key_list = jax.random.split(jax.random.key(seed), 5)
    material = place_ends(jax.random.randint(key_list[0], (NX, NY, NZ), 0, MATS), jax.random.fold_in(key_list[0], 1), 0, MATS - 1).astype(jnp.int32)
    velocity = jnp.clip(jax.random.uniform(key_list[1], (MATS,), jnp.float32, 1.5, 4.5), 1.5, 4.5)
    density = jnp.clip(jax.random.uniform(key_list[2], (MATS,), jnp.float32, 1.0, 2.2), 1.0, 2.2)
    right_side = centred(key_list[3], (NX, NY, NZ), 4.0, 24.0, ((0, 16), (1, 16)), jnp.float32)
    return {"material": material, "velocity": velocity, "density": density, "right_side": right_side}


SHIFT_SCALE = 3.0
DAMPING = 0.7


def harmonic(former, latter):
    return 2.0 * former * latter / (former + latter)


def look_up(material, table):
    picked = jnp.zeros(material.shape, table.dtype)
    for number in range(table.shape[0]):
        picked = jnp.where(material == number, table[number], picked)
    return picked


def face_values(padded, shape):
    size_x, size_y, size_z = shape
    return [padded[0:size_x, 1:size_y + 1, 1:size_z + 1], padded[2:size_x + 2, 1:size_y + 1, 1:size_z + 1],
            padded[1:size_x + 1, 0:size_y, 1:size_z + 1], padded[1:size_x + 1, 2:size_y + 2, 1:size_z + 1],
            padded[1:size_x + 1, 1:size_y + 1, 0:size_z], padded[1:size_x + 1, 1:size_y + 1, 2:size_z + 2]]


def apply_fine(current, couplings, diagonal):
    values = face_values(jnp.pad(current, 1), current.shape)
    summed = couplings[0] * values[0]
    for number in range(1, 6):
        summed = summed + couplings[number] * values[number]
    return diagonal * current - summed


def apply_stencil(current, stencil):
    padded = jnp.pad(current, 1)
    size_x, size_y, size_z = current.shape
    result = jnp.zeros(current.shape, current.dtype)
    for offset in range(27):
        step_x, step_y, step_z = offset // 9, (offset // 3) % 3, offset % 3
        result = result + stencil[offset] * padded[step_x:step_x + size_x, step_y:step_y + size_y, step_z:step_z + size_z]
    return result


def line_weights(conductivity, dimension):
    moved = jnp.moveaxis(conductivity, dimension, 0)
    even_cells = moved[0::2]
    odd_cells = moved[1::2]
    previous = jnp.concatenate([jnp.zeros_like(odd_cells[:1]), odd_cells[:-1]], 0)
    below = harmonic(even_cells, previous)
    above = harmonic(even_cells, odd_cells)
    summed = below + above
    return jnp.moveaxis(below / summed, 0, dimension), jnp.moveaxis(above / summed, 0, dimension)


def level_weights(conductivity):
    return [line_weights(conductivity[:, 1::2, 1::2], 0), line_weights(conductivity[:, :, 1::2], 1),
            line_weights(conductivity, 2)]


def prolong(coarse, low_weight, high_weight, dimension):
    moved = jnp.moveaxis(coarse, dimension, 0)
    low_moved = jnp.moveaxis(low_weight, dimension, 0)
    high_moved = jnp.moveaxis(high_weight, dimension, 0)
    previous = jnp.concatenate([jnp.zeros_like(moved[:1]), moved[:-1]], 0)
    between = low_moved * previous + high_moved * moved
    finer = jnp.stack([between, moved], 1).reshape((2 * moved.shape[0],) + moved.shape[1:])
    return jnp.moveaxis(finer, 0, dimension)


def restrict(finer, low_weight, high_weight, dimension):
    moved = jnp.moveaxis(finer, dimension, 0)
    low_moved = jnp.moveaxis(low_weight, dimension, 0)
    high_moved = jnp.moveaxis(high_weight, dimension, 0)
    pairs = moved.reshape((moved.shape[0] // 2, 2) + moved.shape[1:])
    between = pairs[:, 0]
    centres = pairs[:, 1]
    carried = low_moved * between
    following = jnp.concatenate([carried[1:], jnp.zeros_like(carried[:1])], 0)
    return jnp.moveaxis(centres + high_moved * between + following, 0, dimension)


def prolong_all(coarse, weights):
    for dimension in range(3):
        coarse = prolong(coarse, weights[dimension][0], weights[dimension][1], dimension)
    return coarse


def restrict_all(finer, weights):
    for dimension in (2, 1, 0):
        finer = restrict(finer, weights[dimension][0], weights[dimension][1], dimension)
    return finer


def coarsen(conductivity):
    size_x, size_y, size_z = conductivity.shape
    blocks = conductivity.reshape(size_x // 2, 2, size_y // 2, 2, size_z // 2, 2)
    return jnp.mean(blocks, axis=(1, 3, 5))


def colour_masks(position, dtype):
    return jnp.stack([jnp.stack([((position + offset - 1) % 3 == colour) for colour in range(3)])
                      for offset in range(3)]).astype(dtype)


def assemble(stacked, index_x, index_y, index_z):
    shape = stacked.shape[1:]
    blocks = stacked.reshape((3, 3, 3) + shape)
    mask_x = colour_masks(index_x, stacked.dtype)
    mask_y = colour_masks(index_y, stacked.dtype)
    mask_z = colour_masks(index_z, stacked.dtype)
    along_x = mask_x[:, 0][:, None, None, :, None, None] * blocks[0][None]
    for colour in (1, 2):
        along_x = along_x + mask_x[:, colour][:, None, None, :, None, None] * blocks[colour][None]
    along_y = mask_y[:, 0][None, :, None, None, :, None] * along_x[:, 0][:, None]
    for colour in (1, 2):
        along_y = along_y + mask_y[:, colour][None, :, None, None, :, None] * along_x[:, colour][:, None]
    along_z = mask_z[:, 0][None, None, :, None, None, :] * along_y[:, :, 0][:, :, None]
    for colour in (1, 2):
        along_z = along_z + mask_z[:, colour][None, None, :, None, None, :] * along_y[:, :, colour][:, :, None]
    return along_z.reshape((27,) + shape)


def galerkin(operate, weights, shape):
    index_x = jnp.arange(shape[0], dtype=jnp.int32)
    index_y = jnp.arange(shape[1], dtype=jnp.int32)
    index_z = jnp.arange(shape[2], dtype=jnp.int32)
    dtype = weights[0][0].dtype

    def probe(colour):
        hits = ((index_x % 3 == colour // 9)[:, None, None] & (index_y % 3 == (colour // 3) % 3)[None, :, None]
                & (index_z % 3 == colour % 3)[None, None, :])
        return restrict_all(operate(prolong_all(hits.astype(dtype), weights)), weights)

    stacked = lax.map(probe, jnp.arange(27, dtype=jnp.int32))
    return assemble(stacked, index_x, index_y, index_z)


def smooth(operate, diagonal, source, sweeps):
    current = jnp.zeros_like(source)
    for repeat in range(sweeps):
        current = current + DAMPING * ((source - operate(current)) / diagonal)
    return current


def reference(material, velocity, density, right_side):
    density_cell = look_up(material, density)
    velocity_cell = look_up(material, velocity)
    conductivity = 1.0 / density_cell
    shift_field = SHIFT_SCALE / (density_cell * velocity_cell * velocity_cell)
    couplings = [harmonic(conductivity, other) for other in face_values(jnp.pad(conductivity, 1), conductivity.shape)]
    diagonal = shift_field
    for coupling in couplings:
        diagonal = diagonal + coupling
    weights_fine = level_weights(conductivity)
    conductivity_mid = coarsen(conductivity)
    weights_mid = level_weights(conductivity_mid)
    shape_mid = conductivity_mid.shape
    shape_low = (shape_mid[0] // 2, shape_mid[1] // 2, shape_mid[2] // 2)

    def fine_operator(current):
        return apply_fine(current, couplings, diagonal)

    stencil_mid = galerkin(fine_operator, weights_fine, shape_mid)

    def mid_operator(current):
        return apply_stencil(current, stencil_mid)

    stencil_low = galerkin(mid_operator, weights_mid, shape_low)

    def low_operator(current):
        return apply_stencil(current, stencil_low)

    fine_solution = smooth(fine_operator, diagonal, right_side, SWEEPS_FINE)
    source_mid = restrict_all(right_side - fine_operator(fine_solution), weights_fine)
    mid_solution = smooth(mid_operator, stencil_mid[13], source_mid, SWEEPS_MID)
    source_low = restrict_all(source_mid - mid_operator(mid_solution), weights_mid)
    coarse_solution = smooth(low_operator, stencil_low[13], source_low, SWEEPS_COARSE)
    return fine_solution, mid_solution, coarse_solution
```

```python
import jax
import jax.numpy as jnp
from jax import lax
from jax.experimental import pallas as pl
from jax.experimental.pallas import tpu as pltpu
from jax.sharding import PartitionSpec as P

DAMP = 0.7
F32 = jnp.float32
LOW, HIGH = 7, 10
X0 = LOW
ROWS = LOW + 16 + HIGH
HALF = ((0, 0), (0, 1), (1, -1), (1, 0), (1, 1))
FULL = tuple((dy, dz) for dy in (-1, 0, 1) for dz in (-1, 0, 1))
HI = lax.Precision.HIGHEST


def neg(s):
    return (-s[0], -s[1])


def shift(v, dy, dz, sy=1, sz=1):
    rows, lanes = v.shape
    if dy:
        v = pltpu.roll(v, (-dy * sy) % rows, 0)
    if dz:
        v = pltpu.roll(v, (-dz * sz) % lanes, 1)
    return v


def iota(shape, dim):
    return lax.broadcasted_iota(jnp.int32, shape, dim)


def depth_order(transposed):
    z = iota((128, 128), 1 if transposed else 0)
    c = iota((128, 128), 0 if transposed else 1)
    source = jnp.where(c < 64, 2 * c, 2 * c - 127)
    return jnp.where(z == source, 1.0, 0.0).astype(F32)


def pack_kernel(mat_ref, rhs_ref, mid_ref, low_ref, high_ref, fl_ref):
    fl_ref[...] = mat_ref[...].astype(F32)
    order = depth_order(False)
    for q, ref in ((0, fl_ref), (2, rhs_ref)):
        for parity in range(2):
            part = ref[:, pl.ds(parity, 8, stride=2), :].reshape(128, 128)
            part = jnp.dot(part, order, precision=HI, preferred_element_type=F32)
            part = part.reshape(16, 8, 128)
            mid_ref[:, q + parity] = part
            low_ref[:, q + parity] = part[16 - LOW :]
            high_ref[:, q + parity] = part[:HIGH]


def pick(index, table):
    b0 = (index & 1) == 1
    b1 = (index & 2) == 2
    b2 = (index & 4) == 4
    q = [jnp.where(b0, table[2 * n + 1], table[2 * n]) for n in range(4)]
    q = [jnp.where(b1, q[2 * n + 1], q[2 * n]) for n in range(2)]
    return jnp.where(b2, q[1], q[0])


def collapse_line(tm, t0, tp, l, lc, move, want):
    h, hc = 1.0 - l, 1.0 - lc
    out = {}
    hcp = move(hc, 1)
    lcm = move(lc, -1)
    if 0 in want:
        low = move(h * (hc * t0 + tp), -1)
        high = move(l * (lc * t0 + tm), 1)
        out[0] = t0 + low + high + tm * move(hc, -1) + tp * move(lc, 1)
    if 1 in want:
        out[1] = move(l * (hc * t0 + tp), 1) + tp * hcp
    if -1 in want:
        out[-1] = move(h * (lc * t0 + tm), -1) + tm * lcm
    return out


def collapse_rows(d0, d1, d2, c0, c1, c2, a0, a2, sy, sz, upper):
    h0 = 1.0 - a0
    diag, up = {}, {}
    for s in HALF:
        a2s = shift(a2, *s, sy, sz)
        h0s = 1.0 - shift(a0, *s, sy, sz)
        t10 = shift(c0[neg(s)], *s, sy, sz)
        t21 = shift(c1[neg(s)], *s, sy, sz)
        diag[s] = (
            d1[s]
            + h0 * (h0s * d0[s] + c0[s])
            + h0s * t10
            + a2 * (a2s * d2[s] + t21)
            + a2s * c1[s]
        )
    if upper:
        for s in FULL:
            h2s = 1.0 - shift(a2, *s, sy, sz)
            d2s = d2[s] if s in HALF else shift(d2[neg(s)], *s, sy, sz)
            up[s] = a2 * (h2s * d2s + c2[s]) + h2s * c1[s]
    return diag, up


def apply27(e0, e1, e1_before, u_before, u, u_after):
    total = e0[(0, 0)] * u
    back = {}
    for dy in (-1, 0, 1):
        for dz in (-1, 0, 1):
            s = (dy, dz)
            total = total + e1[s] * shift(u_after, dy, dz)
            if s in HALF and s != (0, 0):
                total = total + e0[s] * shift(u, dy, dz)
    for dy in (-1, 0, 1):
        row = None
        for dz in (-1, 0, 1):
            s = (dy, dz)
            product = e1_before[s] * u_before
            if s in HALF and s != (0, 0):
                product = product + e0[s] * u
            product = shift(product, 0, -dz)
            row = product if row is None else row + product
        total = total + shift(row, -dy, 0)
    return total


def halves(n, shape):
    return iota(shape, 1) < n


def main_kernel(tab_ref, pos_ref, *refs):
    ins = refs[:9]
    fine_ref, mid_ref, low_ref = refs[9:12]
    (D, S, B, OP, CX, CYE, CYO, CZL, CZU, WZ, WY, DG, DI, U1, U2, T, AL, SM, CM,
     WZP, WYP, C0, C1, E0, E1, UM, UN, Z0, Z1, L15, CMP) = refs[12:]
    sh = (16, 128)
    lane = iota(sh, 1)
    subl = iota(sh, 0)
    lt64 = lane < 64
    x_first = pos_ref[0] == 0
    x_last = pos_ref[1] == 1
    y_first = pos_ref[2] == 0
    y_last = pos_ref[3] == 1
    yc = jnp.where(y_first, 0, -1)
    yd = jnp.where(y_last, 8, -1)
    keep_y = jnp.where((subl == yc) | (subl == yd), 0.0, 1.0)
    keep_zl = jnp.where(lane == 0, 0.0, 1.0)
    keep_zu = jnp.where(lane == 127, 0.0, 1.0)
    keep_wz = jnp.where((lane == 0) | (lane >= 64), 0.0, 1.0)

    def keep_x(x):
        cut = (x_first & (x == 0)) | (x_last & (x == 16))
        return jnp.where(cut, 0.0, 1.0).astype(F32)

    def r64(v):
        return pltpu.roll(v, 64, 1)

    def z_lower(v):
        return jnp.where(lt64, pltpu.roll(v, 65, 1), r64(v))

    def z_upper(v):
        return jnp.where(lt64, r64(v), pltpu.roll(v, 63, 1))

    def y_next(v):
        return pltpu.roll(v, 15, 0)

    def y_prev(v):
        return pltpu.roll(v, 1, 0)

    tsh = (8, 128)
    den = [jnp.full(tsh, tab_ref[n], F32) for n in range(8)]
    vel = [jnp.full(tsh, tab_ref[8 + n], F32) for n in range(8)]
    sft = [3.0 / (d * v * v) for d, v in zip(den, vel)]
    s8 = iota(tsh, 0)

    def segment(first, count, own, above, below):
        def body(i, _):
            r = first + i
            for p in range(2):
                m0 = own[i, p].astype(jnp.int32)
                mb = below[i, p].astype(jnp.int32)
                m1 = jnp.where(s8 < 5, above[i, p].astype(jnp.int32), mb)
                d0, d1 = pick(m0, den), pick(m1, den)
                D[r, p, 0:8] = d0
                D[r, p, 8:16] = d1
                S[r, p, 0:8] = pick(m0, sft)
                S[r, p, 8:16] = pick(m1, sft)
                B[r, p, 0:8] = own[i, 2 + p]
                B[r, p, 8:16] = jnp.where(s8 < 5, above[i, 2 + p], below[i, 2 + p])
                if p == 1:
                    dd = y_prev(jnp.concatenate([d0, d1], 0))
                    OP[r, 0:8] = dd[0:8]
                    OP[r, 8:16] = jnp.where(s8 == 5, pltpu.roll(pick(mb, den), 1, 0), dd[8:16])
            return 0

        lax.fori_loop(0, count, body, 0)

    segment(0, LOW, ins[0], ins[1], ins[2])
    segment(LOW, 16, ins[3], ins[4], ins[5])
    segment(LOW + 16, HIGH, ins[6], ins[7], ins[8])

    def x_coupling(r, p):
        return keep_x(r - X0) * 2.0 / (D[r, p] + D[r - 1, p])

    for p in range(2):
        CX[1, p] = x_coupling(1, p)

    def coefficients(r, _):
        de, do, op = D[r, 0], D[r, 1], OP[r]
        sy_m, sy_p = de + op, de + do
        cye = keep_y * 2.0 / sy_m
        cyo = 2.0 / sy_p
        CYE[r] = cye
        CYO[r] = cyo
        WY[r] = keep_y * sy_p / (sy_m + sy_p)
        for p in range(2):
            d = D[r, p]
            lo, up = d + z_lower(d), d + z_upper(d)
            czl = keep_zl * 2.0 / lo
            czu = keep_zu * 2.0 / up
            CZL[r, p] = czl
            CZU[r, p] = czu
            WZ[r, p] = keep_wz * up / (lo + up)
            cxu = x_coupling(r + 1, p)
            CX[r + 1, p] = cxu
            ylo, yup = (cye, cyo) if p == 0 else (cyo, y_next(cye))
            diag = S[r, p] + CX[r, p] + cxu + ylo + yup + czl + czu
            DG[r, p] = diag
            di = DAMP / diag
            DI[r, p] = di
            U1[r, p] = di * B[r, p]
        return 0

    lax.fori_loop(1, ROWS - 1, coefficients, 0)

    def neighbours(U, r):
        e, o = U[r, 0], U[r, 1]
        cye, cyo = CYE[r], CYO[r]
        out = []
        for p in range(2):
            u = (e, o)[p]
            if p == 0:
                along_y = cye * y_prev(o) + cyo * o
            else:
                along_y = cyo * e + y_next(cye * e)
            out.append(
                CX[r, p] * U[r - 1, p]
                + CX[r + 1, p] * U[r + 1, p]
                + along_y
                + CZL[r, p] * z_lower(u)
                + CZU[r, p] * z_upper(u)
            )
        return out

    def second(r, _):
        around = neighbours(U1, r)
        for p in range(2):
            U2[r, p] = U1[r, p] + DI[r, p] * ((1.0 - DAMP) * B[r, p] + around[p])
        return 0

    lax.fori_loop(2, ROWS - 2, second, 0)
    order = depth_order(True)
    for p in range(2):
        part = U2[X0 : X0 + 16, p, 0:8].reshape(128, 128)
        part = jnp.dot(part, order, precision=HI, preferred_element_type=F32)
        fine_ref[:, pl.ds(p, 8, stride=2), :] = part.reshape(16, 8, 128)

    def residual(r, _):
        around = neighbours(U2, r)
        t = []
        for p in range(2):
            v = B[r, p] - DG[r, p] * U2[r, p] + around[p]
            wl = WZ[r, p]
            lowered = wl * v
            t.append(v + r64(v - lowered) + pltpu.roll(lowered, 63, 1))
        wy = WY[r]
        te = t[0] * wy
        T[r] = t[1] + (t[0] - te) + y_next(te)
        return 0

    lax.fori_loop(3, ROWS - 3, residual, 0)

    def x_weights(n, _):
        r = 3 + 2 * n
        d = D[r, 1]
        lo, up = d + D[r - 1, 1], d + D[r + 1, 1]
        AL[n] = keep_x(r - X0) * up / (lo + up)
        return 0

    lax.fori_loop(0, 14, x_weights, 0)

    def restrict_x(n, _):
        r = 3 + 2 * n
        SM[n] = T[r + 1] + (1.0 - AL[n]) * T[r] + AL[n + 1] * T[r + 2]
        return 0

    lax.fori_loop(0, 13, restrict_x, 0)

    def mean_mid(n, _):
        r = 3 + 2 * n
        total = 1.0 / D[r, 0] + 1.0 / D[r, 1] + 1.0 / D[r + 1, 0] + 1.0 / D[r + 1, 1]
        CM[n] = 0.125 * (total + r64(total))
        return 0

    lax.fori_loop(0, 13, mean_mid, 0)

    def even_part(qa, qb):
        return jnp.where(lt64, qa, r64(qb))

    def odd_part(qa, qb):
        return jnp.where(lt64, r64(qa), qb)

    def pair_weights(n, _):
        r = 3 + n
        for p in range(2):
            WZP[n, p] = even_part(WZ[r, p], WZ[r + 12, p])
        WYP[n] = odd_part(WY[r], WY[r + 12])
        return 0

    lax.fori_loop(0, 16, pair_weights, 0)

    def z1(v):
        return pltpu.roll(v, 127, 1)

    def z_collapse_lateral(c_e, c_o, wa, wb):
        ha, hb = 1.0 - wa, 1.0 - wb
        wc = wa * c_e
        return {
            0: c_o + ha * hb * c_e + z1(wc * wb),
            1: z1(wc * hb),
            -1: (c_e - wc) * wb,
        }

    def build(n, _):
        r = 3 + n
        q = r + 12
        cen, xup = [], []
        for p in range(2):
            wl = WZP[n, p]
            wh = 1.0 - wl
            dge, dgo = even_part(DG[r, p], DG[q, p]), odd_part(DG[r, p], DG[q, p])
            cze, czo = -even_part(CZL[r, p], CZL[q, p]), -odd_part(CZL[r, p], CZL[q, p])
            wd = wl * dge
            c = dgo + wh * (wh * dge + 2.0 * czo) + z1(wl * (wd + 2.0 * cze))
            m = wh * (wd + cze) + wl * czo
            cen.append({-1: m, 0: c, 1: z1(m)})
            cxe = -even_part(CX[r + 1, p], CX[q + 1, p])
            cxo = -odd_part(CX[r + 1, p], CX[q + 1, p])
            xup.append(z_collapse_lateral(cxe, cxo, wl, WZP[n + 1, p]))
        we, wo = WZP[n, 0], WZP[n, 1]
        F = z_collapse_lateral(-even_part(CYO[r], CYO[q]), -odd_part(CYO[r], CYO[q]), we, wo)
        H = z_collapse_lateral(-even_part(CYE[r], CYE[q]), -odd_part(CYE[r], CYE[q]), we, y_prev(wo))
        vl = WYP[n]
        vh = 1.0 - vl
        ul = WYP[n + 1]
        be, bo = cen
        vls = {d: shift(vl, 0, d) for d in (-1, 0, 1)}
        vhs = {d: 1.0 - vls[d] for d in (-1, 0, 1)}
        uls = {d: shift(ul, 0, d) for d in (-1, 0, 1)}
        uhs = {d: 1.0 - uls[d] for d in (-1, 0, 1)}
        Ht = {d: shift(H[-d], 0, d) for d in (-1, 0, 1)}
        Ft = {d: shift(F[-d], 0, d) for d in (0, 1)}
        for d in (0, 1):
            C0[n, HALF.index((0, d))] = (
                bo[d]
                + vh * (vhs[d] * be[d] + F[d])
                + vhs[d] * Ft[d]
                + y_next(vl * (vls[d] * be[d] + H[d]) + vls[d] * Ht[d])
            )
        for d in (-1, 0, 1):
            C0[n, HALF.index((1, d))] = y_next(vl * (vhs[d] * be[d] + F[d]) + vhs[d] * Ht[d])
        xe, xo = xup
        for d in (-1, 0, 1):
            lx = vl * xe[d]
            hx = xe[d] - lx
            C1[n, FULL.index((0, d))] = xo[d] + hx * uhs[d] + y_next(lx * uls[d])
            C1[n, FULL.index((1, d))] = y_next(lx * uhs[d])
            C1[n, FULL.index((-1, d))] = hx * uls[d]
        return 0

    lax.fori_loop(0, 15, build, 0)

    def half_of(ref, n):
        return {s: ref[n, j] for j, s in enumerate(HALF)}

    def full_of(ref, n):
        return {s: ref[n, j] for j, s in enumerate(FULL)}

    def join6(n, ref):
        return odd_part(ref[n], ref[n + 6])

    def first_dim(a, _):
        n = 2 * a
        diag, up = collapse_rows(
            half_of(C0, n), half_of(C0, n + 1), half_of(C0, n + 2),
            full_of(C1, n), full_of(C1, n + 1), full_of(C1, n + 2),
            join6(a, AL), join6(a + 1, AL), 1, 1, True,
        )
        for j, s in enumerate(HALF):
            E0[a, j] = diag[s]
        for j, s in enumerate(FULL):
            E1[a + 1, j] = up[s]
        return 0

    for j in range(9):
        C1[15, j] = jnp.zeros(sh, F32)
        C1[14, j] = jnp.zeros(sh, F32)
    lax.fori_loop(0, 7, first_dim, 0)
    for j in range(9):
        E1[0, j] = r64(E1[6, j])
        E1[7, j] = r64(E1[1, j])

    def mid_first(a, _):
        UM[a + 1] = DAMP * join6(a, SM) / E0[a, 0]
        return 0

    lax.fori_loop(0, 7, mid_first, 0)
    UM[0] = r64(UM[6])
    UM[8] = r64(UM[2])

    def a1(U, a):
        return apply27(half_of(E0, a), full_of(E1, a + 1), full_of(E1, a), U[a], U[a + 1], U[a + 2])

    def mid_second(a, _):
        UN[a + 1] = UM[a + 1] + DAMP * ((join6(a, SM) - a1(UM, a)) / E0[a, 0])
        return 0

    lax.fori_loop(0, 7, mid_second, 0)
    UN[0] = r64(UN[6])
    UN[8] = r64(UN[2])
    for i in range(4):
        mid_ref[i] = UN[i + 3, 0:8, 0:64]
        mid_ref[i + 4] = r64(UN[i + 1])[0:8, 0:64]

    def mid_residual(a, _):
        UM[a + 1] = join6(a, SM) - a1(UN, a)
        return 0

    lax.fori_loop(0, 7, mid_residual, 0)

    def at(b, ref, j=None):
        if j is None:
            return jnp.where(lt64, ref[b + 2], ref[b])
        return jnp.where(lt64, ref[b + 2, j], ref[b, j])

    def at1(b, j=None):
        if j is None:
            return jnp.where(lt64, UM[b + 3], UM[b + 1])
        return jnp.where(lt64, E1[b + 3, j], E1[b + 1, j])

    def cm(b):
        return jnp.where(lt64, CM[b + 2], CM[b + 6])

    edge_z = jnp.where((lane == 0) | (lane == 64), 0.0, 1.0)

    def weight(g, before, after, keep):
        lo, up = before * (g + after), after * (g + before)
        return keep * lo / (lo + up)

    def mid_z(b):
        g = cm(b)
        return weight(g, pltpu.roll(g, 1, 1), pltpu.roll(g, 127, 1), edge_z)

    def mid_y(b):
        g = cm(b)
        return weight(g, y_prev(g), y_next(g), keep_y)

    def mid_x(b):
        ka = jnp.where(x_first & (b == 0), 0.0, 1.0).astype(F32)
        kb = jnp.where(x_last & (b == 4), 0.0, 1.0).astype(F32)
        return weight(cm(b), cm(b - 1), cm(b + 1), jnp.where(lt64, ka, kb))

    def move_z(v, n):
        return shift(v, 0, n)

    def move_y(v, n):
        return shift(v, n, 0)

    def build_low(b, _):
        e0 = {s: at(b, E0, j) for j, s in enumerate(HALF)}
        e1 = {s: at1(b, j) for j, s in enumerate(FULL)}
        lz = (mid_z(b), mid_z(b + 1))
        z0, zz1 = {}, {}
        for dx in (0, 1):
            source, out = ((e0, z0), (e1, zz1))[dx]
            for dy in (-1, 0, 1):
                if dx == 0 and dy == -1:
                    continue
                lc = move_y(lz[dx], dy)
                if dx == 0 and dy == 0:
                    t0, tp = source[(0, 0)], source[(0, 1)]
                    tm = move_z(tp, -1)
                    want = (0, 1)
                else:
                    tm, t0, tp = (source[(dy, d)] for d in (-1, 0, 1))
                    want = (-1, 0, 1)
                for d, v in collapse_line(tm, t0, tp, lz[0], lc, move_z, want).items():
                    out[(dy, d)] = v
        ly = (mid_y(b), mid_y(b + 1))
        for d in (-1, 0, 1):
            lc = shift(ly[0], 0, d, 1, 2)
            want = (0, 1) if d >= 0 else (1,)
            t0 = z0[(0, d)] if d >= 0 else shift(z0[(0, 1)], 0, -1, 1, 2)
            tp = z0[(1, d)]
            tm = shift(z0[(1, -d)], -1, d, 1, 2)
            for dy, v in collapse_line(tm, t0, tp, ly[0], lc, move_y, want).items():
                Z0[b, HALF.index((dy, d))] = v
            lc = shift(ly[1], 0, d, 1, 2)
            tm, t0, tp = (zz1[(dy, d)] for dy in (-1, 0, 1))
            for dy, v in collapse_line(tm, t0, tp, ly[0], lc, move_y, (-1, 0, 1)).items():
                Z1[b, FULL.index((dy, d))] = v
        v = at1(b)
        lv = lz[0] * v
        v = v + move_z(v - lv, -1) + move_z(lv, 1)
        lv = ly[0] * v
        UN[b] = v + move_y(v - lv, -1) + move_y(lv, 1)
        return 0

    lax.fori_loop(0, 5, build_low, 0)

    def low_rows(i, _):
        b = 2 * i
        w0, w2 = mid_x(b), mid_x(b + 2)
        diag, up = collapse_rows(
            half_of(Z0, b), half_of(Z0, b + 1), half_of(Z0, b + 2),
            full_of(Z1, b), full_of(Z1, b + 1), full_of(Z1, b + 2),
            w0, w2, 1, 2, True,
        )
        del diag, up
        return 0

    for i in range(2):
        b = 2 * i
        w0, w2 = mid_x(b), mid_x(b + 2)
        diag, up = collapse_rows(
            half_of(Z0, b), half_of(Z0, b + 1), half_of(Z0, b + 2),
            full_of(Z1, b), full_of(Z1, b + 1), full_of(Z1, b + 2),
            w0, w2, 2, 2, True,
        )
        for j, s in enumerate(HALF):
            L15[i, j] = diag[s][0:8]
        for j, s in enumerate(FULL):
            L15[i, 5 + j] = up[s][0:8]
        L15[i, 14] = (UN[b + 1] + (1.0 - w0) * UN[b] + w2 * UN[b + 2])[0:8]
    src, dst = iota((128, 128), 0), iota((128, 128), 1)
    total = None
    for i in range(2):
        row, z = dst // 32, dst % 32
        hit = (src // 64 == row // 2) & (row % 2 == i) & (src % 64 == 2 * z + 1)
        part = jnp.dot(L15[i].reshape(120, 128), jnp.where(hit, 1.0, 0.0).astype(F32),
                       precision=HI, preferred_element_type=F32)
        total = part if total is None else total + part
    CMP[...] = total
    low_ref[0:60] = CMP[pl.ds(1, 60, stride=2), :]
    low_ref[60:64] = jnp.zeros((4, 128), F32)


def low_kernel(*refs):
    ins, out_ref, E, SRC, UA, UB = refs[:9], refs[9], refs[10], refs[11], refs[12], refs[13]
    for b in range(3):
        own, above, below = ins[3 * b : 3 * b + 3]
        for j in range(15):
            rows = pl.ds(4 * j, 4)
            mine = own[rows, :]
            v = jnp.concatenate([mine, above[rows, :], mine, below[rows, :]], 0)
            if j < 14:
                E[b, j] = v
            else:
                SRC[b] = v
    lane = iota((16, 128), 1)
    last = lane >= 96
    first = lane < 32

    def after(get, b):
        here = pltpu.roll(get(b), 96, 1)
        there = pltpu.roll(get(min(b + 1, 2)), 96, 1)
        return jnp.where(last, there, here)

    def before(get, b):
        here = pltpu.roll(get(b), 32, 1)
        there = pltpu.roll(get(max(b - 1, 0)), 32, 1)
        return jnp.where(first, there, here)

    zlane = lane % 32
    keep = {-1: jnp.where(zlane == 0, 0.0, 1.0), 1: jnp.where(zlane == 31, 0.0, 1.0)}
    del keep
    for b in range(3):
        UA[b] = DAMP * SRC[b] / E[b, 0]
    cur, nxt = UA, UB
    for sweep in range(3):
        blocks = (0, 1, 2) if sweep < 2 else (1,)
        for b in blocks:
            u_after = after(lambda c: cur[c], b)
            e0 = {s: E[b, j] for j, s in enumerate(HALF)}
            u = cur[b]
            total = e0[(0, 0)] * u
            for s in FULL:
                total = total + E[b, 5 + FULL.index(s)] * shift(u_after, *s)
                if s in HALF and s != (0, 0):
                    total = total + e0[s] * shift(u, *s)
            for dy in (-1, 0, 1):
                row = None
                for dz in (-1, 0, 1):
                    s = (dy, dz)
                    j = 5 + FULL.index(s)
                    product = before(lambda c: E[c, j] * cur[c], b)
                    if s in HALF and s != (0, 0):
                        product = product + e0[s] * u
                    product = shift(product, 0, -dz)
                    row = product if row is None else row + product
                total = total + shift(row, -dy, 0)
            nxt[b] = u + DAMP * ((SRC[b] - total) / e0[(0, 0)])
        if sweep < 2:
            cur, nxt = nxt, cur
    result = nxt[1]
    for i in range(4):
        out_ref[i] = pltpu.roll(result, (128 - 32 * i) % 128, 1)[0:4, 0:32] if i else result[0:4, 0:32]


def around(pieces):
    nx, ny = lax.axis_size("gx"), lax.axis_size("gy")

    def fetch(value, fx, fy):
        if fx == 0 and fy == 0:
            return value
        route = [
            (((i + fx) % nx) * ny + (j + fy) % ny, i * ny + j) for i in range(nx) for j in range(ny)
        ]
        return lax.ppermute(value, ("gx", "gy"), route)

    return [fetch(pieces[fx], fx, fy) for fx in (-1, 0, 1) for fy in (0, 1, -1)]


def per_device(material, velocity, density, right_side):
    shape = jax.ShapeDtypeStruct
    params = pltpu.CompilerParams(vmem_limit_bytes=48 * 1024 * 1024)
    own, low, high = pl.pallas_call(
        pack_kernel,
        out_shape=(
            shape((16, 4, 8, 128), F32),
            shape((LOW, 4, 8, 128), F32),
            shape((HIGH, 4, 8, 128), F32),
        ),
        scratch_shapes=[pltpu.VMEM((16, 16, 128), F32)],
        compiler_params=params,
        name="pack",
    )(material, right_side)
    row_x, row_y = lax.axis_index("gx"), lax.axis_index("gy")
    position = jnp.stack(
        [
            row_x,
            (row_x == lax.axis_size("gx") - 1).astype(jnp.int32),
            row_y,
            (row_y == lax.axis_size("gy") - 1).astype(jnp.int32),
        ]
    ).astype(jnp.int32)
    tables = jnp.concatenate([density, velocity])
    blocks = around({-1: low, 0: own, 1: high})
    vm = lambda *s: pltpu.VMEM(s, F32)
    smem, vmem = pl.BlockSpec(memory_space=pltpu.SMEM), pl.BlockSpec(memory_space=pltpu.VMEM)
    two, one = (ROWS, 2, 16, 128), (ROWS, 16, 128)
    fine, mid, sent = pl.pallas_call(
        main_kernel,
        in_specs=[smem, smem] + [vmem] * 9,
        out_specs=[vmem] * 3,
        out_shape=(
            shape((16, 16, 128), F32),
            shape((8, 8, 64), F32),
            shape((64, 128), F32),
        ),
        scratch_shapes=[
            vm(*two), vm(*two), vm(*two), vm(*one), vm(*two), vm(*one), vm(*one), vm(*two), vm(*two),
            vm(*two), vm(*one), vm(*two), vm(*two), vm(*two), vm(*two), vm(*one),
            vm(14, 16, 128), vm(13, 16, 128), vm(13, 16, 128),
            vm(16, 2, 16, 128), vm(16, 16, 128), vm(16, 5, 16, 128), vm(16, 9, 16, 128),
            vm(7, 5, 16, 128), vm(8, 9, 16, 128), vm(9, 16, 128), vm(9, 16, 128),
            vm(5, 5, 16, 128), vm(5, 9, 16, 128), vm(2, 15, 8, 128), vm(120, 128),
        ],
        compiler_params=params,
        name="levels",
    )(tables, position, *blocks)
    lows = around({-1: sent, 0: sent, 1: sent})
    coarse = pl.pallas_call(
        low_kernel,
        in_specs=[vmem] * 9,
        out_specs=vmem,
        out_shape=shape((4, 4, 32), F32),
        scratch_shapes=[vm(3, 14, 16, 128), vm(3, 16, 128), vm(3, 16, 128), vm(3, 16, 128)],
        compiler_params=params,
        name="coarse",
    )(*lows)
    return fine, mid, coarse


def solution(mesh):
    return jax.shard_map(
        per_device,
        mesh=mesh,
        in_specs=(P("gx", "gy", None), P(), P(), P("gx", "gy", None)),
        out_specs=(P("gx", "gy", None), P("gx", "gy", None), P("gx", "gy", None)),
        check_vma=False,
    )
```

```python
import jax
import jax.numpy as jnp
from jax import lax
from jax.experimental import pallas as pl
from jax.experimental.pallas import tpu as pltpu
from jax.sharding import PartitionSpec as P

DAMP = 0.7
F32 = jnp.float32
LOW, HIGH = 7, 10
X0 = LOW
ROWS = LOW + 16 + HIGH
HALF = ((0, 0), (0, 1), (1, -1), (1, 0), (1, 1))
FULL = tuple((dy, dz) for dy in (-1, 0, 1) for dz in (-1, 0, 1))
HI = lax.Precision.HIGHEST
BY = (4, 2, 4, 4, 1, 1, 1, 1)


def neg(s):
    return (-s[0], -s[1])


def shift(v, dy, dz, sy=1, sz=1):
    rows, lanes = v.shape
    if dy:
        v = pltpu.roll(v, (-dy * sy) % rows, 0)
    if dz:
        v = pltpu.roll(v, (-dz * sz) % lanes, 1)
    return v


def rows_loop(first, last, body, by):
    def group(start, count):
        stores = []
        for k in range(count):
            stores += body(start + k)
        for ref, index, value in stores:
            ref[index] = value

    count = last - first
    whole = count // by
    if whole == 1:
        group(first, by)
    elif whole > 1:

        def step(n, _):
            group(first + n * by, by)
            return 0

        lax.fori_loop(0, whole, step, 0)
    if count % by:
        group(first + whole * by, count % by)


def inverse(v):
    return pl.reciprocal(v, approx=True)


def iota(shape, dim):
    return lax.broadcasted_iota(jnp.int32, shape, dim)


def depth_order(transposed):
    z = iota((128, 128), 1 if transposed else 0)
    c = iota((128, 128), 0 if transposed else 1)
    source = jnp.where(c < 64, 2 * c, 2 * c - 127)
    return jnp.where(z == source, 1.0, 0.0).astype(F32)


def pack_kernel(mat_ref, rhs_ref, own_ref, fl_ref):
    fl_ref[...] = mat_ref[...].astype(F32)
    order = depth_order(False)
    for q, ref in ((0, fl_ref), (2, rhs_ref)):
        for parity in range(2):
            part = ref[:, pl.ds(parity, 8, stride=2), :].reshape(128, 128)
            part = jnp.dot(part, order, precision=HI, preferred_element_type=F32)
            own_ref[:, q + parity] = part.reshape(16, 8, 128)


def widen_kernel(pos_ref, own_ref, swap_ref, other_ref, wide_ref, to_swap_ref, to_other_ref):
    even_x, even_y = pos_ref[4] == 0, pos_ref[5] == 0
    row = iota((16, 8, 128), 1)
    for q in range(4):
        above = jnp.where(even_y, swap_ref[:, q], other_ref[:, q])
        below = jnp.where(even_y, other_ref[:, q], swap_ref[:, q])
        extra = jnp.where(row < 5, above, below)
        if q == 3:
            below_odd = jnp.where(even_y, other_ref[:, 1], swap_ref[:, 1])
            extra = jnp.where(row == 4, below_odd, extra)
        wide_ref[:, q, 0:8] = own_ref[:, q]
        wide_ref[:, q, 8:16] = extra
    start = jnp.where(even_x, 16 - HIGH, 0)

    def copy(i, _):
        to_swap_ref[i] = wide_ref[start + i]
        to_other_ref[i] = wide_ref[(16 - HIGH) - start + i]
        return 0

    lax.fori_loop(0, HIGH, copy, 0)


def pick(index, table):
    b0 = (index & 1) == 1
    b1 = (index & 2) == 2
    b2 = (index & 4) == 4
    q = [jnp.where(b0, table[2 * n + 1], table[2 * n]) for n in range(4)]
    q = [jnp.where(b1, q[2 * n + 1], q[2 * n]) for n in range(2)]
    return jnp.where(b2, q[1], q[0])


def collapse_line(tm, t0, tp, l, lc, move, want):
    h, hc = 1.0 - l, 1.0 - lc
    out = {}
    hcp = move(hc, 1)
    lcm = move(lc, -1)
    if 0 in want:
        low = move(h * (hc * t0 + tp), -1)
        high = move(l * (lc * t0 + tm), 1)
        out[0] = t0 + low + high + tm * move(hc, -1) + tp * move(lc, 1)
    if 1 in want:
        out[1] = move(l * (hc * t0 + tp), 1) + tp * hcp
    if -1 in want:
        out[-1] = move(h * (lc * t0 + tm), -1) + tm * lcm
    return out


def collapse_rows(d0, d1, d2, c0, c1, c2, a0, a2, sy, sz, upper):
    h0 = 1.0 - a0
    diag, up = {}, {}
    for s in HALF:
        a2s = shift(a2, *s, sy, sz)
        h0s = 1.0 - shift(a0, *s, sy, sz)
        t10 = shift(c0[neg(s)], *s, sy, sz)
        t21 = shift(c1[neg(s)], *s, sy, sz)
        diag[s] = (
            d1[s]
            + h0 * (h0s * d0[s] + c0[s])
            + h0s * t10
            + a2 * (a2s * d2[s] + t21)
            + a2s * c1[s]
        )
    if upper:
        for s in FULL:
            h2s = 1.0 - shift(a2, *s, sy, sz)
            d2s = d2[s] if s in HALF else shift(d2[neg(s)], *s, sy, sz)
            up[s] = a2 * (h2s * d2s + c2[s]) + h2s * c1[s]
    return diag, up


def apply27(e0, e1, e1_before, u_before, u, u_after):
    total = e0[(0, 0)] * u
    back = {}
    for dy in (-1, 0, 1):
        for dz in (-1, 0, 1):
            s = (dy, dz)
            total = total + e1[s] * shift(u_after, dy, dz)
            if s in HALF and s != (0, 0):
                total = total + e0[s] * shift(u, dy, dz)
    for dy in (-1, 0, 1):
        row = None
        for dz in (-1, 0, 1):
            s = (dy, dz)
            product = e1_before[s] * u_before
            if s in HALF and s != (0, 0):
                product = product + e0[s] * u
            product = shift(product, 0, -dz)
            row = product if row is None else row + product
        total = total + shift(row, -dy, 0)
    return total


def halves(n, shape):
    return iota(shape, 1) < n


def main_kernel(tab_ref, pos_ref, *refs):
    ins = refs[:3]
    fine_ref, mid_ref, low_ref = refs[3:6]
    (D, S, B, OP, CX, CYE, CYO, CZL, CZU, WZ, WY, DG, DI, U1, U2, T, AL, SM, CM,
     WZP, WYP, C0, C1, E0, E1, UM, UN, Z0, Z1, L15, CMP, MD, MS) = refs[6:]
    sh = (16, 128)
    lane = iota(sh, 1)
    subl = iota(sh, 0)
    lt64 = lane < 64
    x_first = pos_ref[0] == 0
    x_last = pos_ref[1] == 1
    y_first = pos_ref[2] == 0
    y_last = pos_ref[3] == 1
    yc = jnp.where(y_first, 0, -1)
    yd = jnp.where(y_last, 8, -1)
    keep_y = jnp.where((subl == yc) | (subl == yd), 0.0, 1.0)
    keep_zl = jnp.where(lane == 0, 0.0, 1.0)
    keep_zu = jnp.where(lane == 127, 0.0, 1.0)
    two_y, two_zl, two_zu = 2.0 * keep_y, 2.0 * keep_zl, 2.0 * keep_zu
    keep_wz = jnp.where((lane == 0) | (lane >= 64), 0.0, 1.0)

    def keep_x(x):
        cut = (x_first & (x == 0)) | (x_last & (x == 16))
        return jnp.where(cut, 0.0, 1.0).astype(F32)

    def r64(v):
        return pltpu.roll(v, 64, 1)

    def z_lower(v):
        return jnp.where(lt64, pltpu.roll(v, 65, 1), r64(v))

    def z_upper(v):
        return jnp.where(lt64, r64(v), pltpu.roll(v, 63, 1))

    def y_next(v):
        return pltpu.roll(v, 15, 0)

    def y_prev(v):
        return pltpu.roll(v, 1, 0)

    tsh = (8, 128)
    den = [jnp.full(tsh, tab_ref[n], F32) for n in range(8)]
    vel = [jnp.full(tsh, tab_ref[8 + n], F32) for n in range(8)]
    sft = [3.0 / (d * v * v) for d, v in zip(den, vel)]
    s8 = iota(tsh, 0)

    even_x = pos_ref[4] == 0

    def segment(first, count, get, by):
        def body(i):
            r = first + i
            v = get(i)
            stores = []
            for p in range(2):
                half = []
                for t in range(2):
                    rows = slice(8 * t, 8 * t + 8)
                    m = v[p][rows].astype(jnp.int32)
                    d = pick(m, den)
                    half.append(d)
                    stores.append((S, (r, p, rows), pick(m, sft)))
                dd = jnp.concatenate(half, 0)
                stores.append((D, (r, p), dd))
                stores.append((B, (r, p), v[2 + p]))
                if p == 1:
                    dd = y_prev(dd)
                    special = pick(v[3][8:16].astype(jnp.int32), den)
                    stores.append((OP, (r, slice(0, 8)), dd[0:8]))
                    extra = jnp.where(s8 == 5, pltpu.roll(special, 1, 0), dd[8:16])
                    stores.append((OP, (r, slice(8, 16)), extra))
            return stores

        rows_loop(0, count, body, by)

    wide_ref, swap_ref, other_ref = ins
    skip = HIGH - LOW
    segment(0, LOW, lambda i: jnp.where(even_x, other_ref[i + skip], swap_ref[i + skip]), BY[0])
    segment(LOW, 16, lambda i: wide_ref[i], BY[0])
    segment(LOW + 16, HIGH, lambda i: jnp.where(even_x, swap_ref[i], other_ref[i]), BY[0])

    def x_coupling(r, p):
        return (2.0 * keep_x(r - X0)) * inverse(D[r, p] + D[r - 1, p])

    for p in range(2):
        CX[1, p] = x_coupling(1, p)

    def coefficients(r):
        de, do, op = D[r, 0], D[r, 1], OP[r]
        sy_m, sy_p = de + op, de + do
        cye = two_y * inverse(sy_m)
        cyo = 2.0 * inverse(sy_p)
        stores = [
            (CYE, r, cye), (CYO, r, cyo), (WY, r, keep_y * sy_p * inverse(sy_m + sy_p)),
        ]
        for p in range(2):
            d = D[r, p]
            lo, up = d + z_lower(d), d + z_upper(d)
            czl = two_zl * inverse(lo)
            czu = two_zu * inverse(up)
            cxl, cxu = x_coupling(r, p), x_coupling(r + 1, p)
            ylo, yup = (cye, cyo) if p == 0 else (cyo, y_next(cye))
            diag = S[r, p] + cxl + cxu + ylo + yup + czl + czu
            di = DAMP * inverse(diag)
            stores += [
                (CZL, (r, p), czl), (CZU, (r, p), czu), (WZ, (r, p), keep_wz * up * inverse(lo + up)),
                (CX, (r + 1, p), cxu), (DG, (r, p), diag), (DI, (r, p), di), (U1, (r, p), di * B[r, p]),
            ]
        return stores

    rows_loop(1, ROWS - 1, coefficients, BY[1])

    def neighbours(U, r):
        e, o = U[r, 0], U[r, 1]
        cye, cyo = CYE[r], CYO[r]
        out = []
        for p in range(2):
            u = (e, o)[p]
            if p == 0:
                along_y = cye * y_prev(o) + cyo * o
            else:
                along_y = cyo * e + y_next(cye * e)
            out.append(
                CX[r, p] * U[r - 1, p]
                + CX[r + 1, p] * U[r + 1, p]
                + along_y
                + CZL[r, p] * z_lower(u)
                + CZU[r, p] * z_upper(u)
            )
        return out

    def second(r):
        around = neighbours(U1, r)
        return [
            (U2, (r, p), U1[r, p] + DI[r, p] * ((1.0 - DAMP) * B[r, p] + around[p])) for p in range(2)
        ]

    rows_loop(2, ROWS - 2, second, BY[2])
    order = depth_order(True)
    for p in range(2):
        part = U2[X0 : X0 + 16, p, 0:8].reshape(128, 128)
        part = jnp.dot(part, order, precision=HI, preferred_element_type=F32)
        fine_ref[:, pl.ds(p, 8, stride=2), :] = part.reshape(16, 8, 128)

    def residual(r):
        around = neighbours(U2, r)
        t = []
        for p in range(2):
            v = B[r, p] - DG[r, p] * U2[r, p] + around[p]
            lowered = WZ[r, p] * v
            t.append(v + r64(v - lowered) + pltpu.roll(lowered, 63, 1))
        te = t[0] * WY[r]
        return [(T, r, t[1] + (t[0] - te) + y_next(te))]

    rows_loop(3, ROWS - 3, residual, BY[3])

    def x_weights(n):
        r = 3 + 2 * n
        d = D[r, 1]
        lo, up = d + D[r - 1, 1], d + D[r + 1, 1]
        return [(AL, n, keep_x(r - X0) * up * inverse(lo + up))]

    rows_loop(0, 14, x_weights, 7)

    def restrict_x(n):
        r = 3 + 2 * n
        return [(SM, n, T[r + 1] + (1.0 - AL[n]) * T[r] + AL[n + 1] * T[r + 2])]

    rows_loop(0, 13, restrict_x, 7)

    def mean_mid(n):
        r = 3 + 2 * n
        total = inverse(D[r, 0]) + inverse(D[r, 1]) + inverse(D[r + 1, 0]) + inverse(D[r + 1, 1])
        return [(CM, n, 0.125 * (total + r64(total)))]

    rows_loop(0, 13, mean_mid, 7)

    def even_part(qa, qb):
        return jnp.where(lt64, qa, r64(qb))

    def odd_part(qa, qb):
        return jnp.where(lt64, r64(qa), qb)

    def pair_weights(n):
        r = 3 + n
        return [(WZP, (n, p), even_part(WZ[r, p], WZ[r + 12, p])) for p in range(2)] + [
            (WYP, n, odd_part(WY[r], WY[r + 12]))
        ]

    rows_loop(0, 16, pair_weights, 4)

    def z1(v):
        return pltpu.roll(v, 127, 1)

    def z_collapse_lateral(c_e, c_o, wa, wb):
        ha, hb = 1.0 - wa, 1.0 - wb
        wc = wa * c_e
        return {
            0: c_o + ha * hb * c_e + z1(wc * wb),
            1: z1(wc * hb),
            -1: (c_e - wc) * wb,
        }

    def build(n):
        stores = []
        r = 3 + n
        q = r + 12
        cen, xup = [], []
        for p in range(2):
            wl = WZP[n, p]
            wh = 1.0 - wl
            dge, dgo = even_part(DG[r, p], DG[q, p]), odd_part(DG[r, p], DG[q, p])
            cze, czo = -even_part(CZL[r, p], CZL[q, p]), -odd_part(CZL[r, p], CZL[q, p])
            wd = wl * dge
            c = dgo + wh * (wh * dge + 2.0 * czo) + z1(wl * (wd + 2.0 * cze))
            m = wh * (wd + cze) + wl * czo
            cen.append({-1: m, 0: c, 1: z1(m)})
            cxe = -even_part(CX[r + 1, p], CX[q + 1, p])
            cxo = -odd_part(CX[r + 1, p], CX[q + 1, p])
            xup.append(z_collapse_lateral(cxe, cxo, wl, WZP[n + 1, p]))
        we, wo = WZP[n, 0], WZP[n, 1]
        F = z_collapse_lateral(-even_part(CYO[r], CYO[q]), -odd_part(CYO[r], CYO[q]), we, wo)
        H = z_collapse_lateral(-even_part(CYE[r], CYE[q]), -odd_part(CYE[r], CYE[q]), we, y_prev(wo))
        vl = WYP[n]
        vh = 1.0 - vl
        ul = WYP[n + 1]
        be, bo = cen
        vls = {d: shift(vl, 0, d) for d in (-1, 0, 1)}
        vhs = {d: 1.0 - vls[d] for d in (-1, 0, 1)}
        uls = {d: shift(ul, 0, d) for d in (-1, 0, 1)}
        uhs = {d: 1.0 - uls[d] for d in (-1, 0, 1)}
        Ht = {d: shift(H[-d], 0, d) for d in (-1, 0, 1)}
        Ft = {d: shift(F[-d], 0, d) for d in (0, 1)}
        for d in (0, 1):
            v = (
                bo[d]
                + vh * (vhs[d] * be[d] + F[d])
                + vhs[d] * Ft[d]
                + y_next(vl * (vls[d] * be[d] + H[d]) + vls[d] * Ht[d])
            )
            stores.append((C0, (n, HALF.index((0, d))), v))
        for d in (-1, 0, 1):
            v = y_next(vl * (vhs[d] * be[d] + F[d]) + vhs[d] * Ht[d])
            stores.append((C0, (n, HALF.index((1, d))), v))
        xe, xo = xup
        for d in (-1, 0, 1):
            lx = vl * xe[d]
            hx = xe[d] - lx
            stores += [
                (C1, (n, FULL.index((0, d))), xo[d] + hx * uhs[d] + y_next(lx * uls[d])),
                (C1, (n, FULL.index((1, d))), y_next(lx * uhs[d])),
                (C1, (n, FULL.index((-1, d))), hx * uls[d]),
            ]
        return stores

    rows_loop(0, 15, build, BY[4])

    def half_of(ref, n):
        return {s: ref[n, j] for j, s in enumerate(HALF)}

    def full_of(ref, n):
        return {s: ref[n, j] for j, s in enumerate(FULL)}

    def join6(n, ref):
        return odd_part(ref[n], ref[n + 6])

    def first_dim(a):
        n = 2 * a
        diag, up = collapse_rows(
            half_of(C0, n), half_of(C0, n + 1), half_of(C0, n + 2),
            full_of(C1, n), full_of(C1, n + 1), full_of(C1, n + 2),
            join6(a, AL), join6(a + 1, AL), 1, 1, True,
        )
        return [(E0, (a, j), diag[s]) for j, s in enumerate(HALF)] + [
            (E1, (a + 1, j), up[s]) for j, s in enumerate(FULL)
        ]

    rows_loop(0, 7, first_dim, BY[5])
    for j in range(9):
        E1[0, j] = r64(E1[6, j])
        E1[7, j] = r64(E1[1, j])

    def mid_first(a):
        di = DAMP * inverse(E0[a, 0])
        source = join6(a, SM)
        return [(MD, a, di), (MS, a, source), (UM, a + 1, di * source)]

    rows_loop(0, 7, mid_first, 7)
    UM[0] = r64(UM[6])
    UM[8] = r64(UM[2])

    def a1(U, a):
        return apply27(half_of(E0, a), full_of(E1, a + 1), full_of(E1, a), U[a], U[a + 1], U[a + 2])

    def mid_second(a):
        return [(UN, a + 1, UM[a + 1] + MD[a] * (MS[a] - a1(UM, a)))]

    rows_loop(0, 7, mid_second, BY[6])
    UN[0] = r64(UN[6])
    UN[8] = r64(UN[2])
    for i in range(4):
        mid_ref[i] = UN[i + 3, 0:8, 0:64]
        mid_ref[i + 4] = r64(UN[i + 1])[0:8, 0:64]

    def mid_residual(a):
        return [(UM, a + 1, MS[a] - a1(UN, a))]

    rows_loop(0, 7, mid_residual, BY[6])

    def at(b, ref, j=None):
        if j is None:
            return jnp.where(lt64, ref[b + 2], ref[b])
        return jnp.where(lt64, ref[b + 2, j], ref[b, j])

    def at1(b, j=None):
        if j is None:
            return jnp.where(lt64, UM[b + 3], UM[b + 1])
        return jnp.where(lt64, E1[b + 3, j], E1[b + 1, j])

    def cm(b):
        return jnp.where(lt64, CM[b + 2], CM[b + 6])

    edge_z = jnp.where((lane == 0) | (lane == 64), 0.0, 1.0)

    def weight(g, before, after, keep):
        lo, up = before * (g + after), after * (g + before)
        return keep * lo * inverse(lo + up)

    def mid_z(b):
        g = cm(b)
        return weight(g, pltpu.roll(g, 1, 1), pltpu.roll(g, 127, 1), edge_z)

    def mid_y(b):
        g = cm(b)
        return weight(g, y_prev(g), y_next(g), keep_y)

    def mid_x(b):
        ka = jnp.where(x_first & (b == 0), 0.0, 1.0).astype(F32)
        kb = jnp.where(x_last & (b == 4), 0.0, 1.0).astype(F32)
        return weight(cm(b), cm(b - 1), cm(b + 1), jnp.where(lt64, ka, kb))

    def move_z(v, n):
        return shift(v, 0, n)

    def move_y(v, n):
        return shift(v, n, 0)

    def build_low(b):
        stores = []
        e0 = {s: at(b, E0, j) for j, s in enumerate(HALF)}
        e1 = {s: at1(b, j) for j, s in enumerate(FULL)}
        lz = (mid_z(b), mid_z(b + 1))
        z0, zz1 = {}, {}
        for dx in (0, 1):
            source, out = ((e0, z0), (e1, zz1))[dx]
            for dy in (-1, 0, 1):
                if dx == 0 and dy == -1:
                    continue
                lc = move_y(lz[dx], dy)
                if dx == 0 and dy == 0:
                    t0, tp = source[(0, 0)], source[(0, 1)]
                    tm = move_z(tp, -1)
                    want = (0, 1)
                else:
                    tm, t0, tp = (source[(dy, d)] for d in (-1, 0, 1))
                    want = (-1, 0, 1)
                for d, v in collapse_line(tm, t0, tp, lz[0], lc, move_z, want).items():
                    out[(dy, d)] = v
        ly = (mid_y(b), mid_y(b + 1))
        for d in (-1, 0, 1):
            lc = shift(ly[0], 0, d, 1, 2)
            want = (0, 1) if d >= 0 else (1,)
            t0 = z0[(0, d)] if d >= 0 else shift(z0[(0, 1)], 0, -1, 1, 2)
            tp = z0[(1, d)]
            tm = shift(z0[(1, -d)], -1, d, 1, 2)
            for dy, v in collapse_line(tm, t0, tp, ly[0], lc, move_y, want).items():
                stores.append((Z0, (b, HALF.index((dy, d))), v))
            lc = shift(ly[1], 0, d, 1, 2)
            tm, t0, tp = (zz1[(dy, d)] for dy in (-1, 0, 1))
            for dy, v in collapse_line(tm, t0, tp, ly[0], lc, move_y, (-1, 0, 1)).items():
                stores.append((Z1, (b, FULL.index((dy, d))), v))
        v = at1(b)
        lv = lz[0] * v
        v = v + move_z(v - lv, -1) + move_z(lv, 1)
        lv = ly[0] * v
        return stores + [(UN, b, v + move_y(v - lv, -1) + move_y(lv, 1))]

    rows_loop(0, 5, build_low, BY[7])

    for i in range(2):
        b = 2 * i
        w0, w2 = mid_x(b), mid_x(b + 2)
        diag, up = collapse_rows(
            half_of(Z0, b), half_of(Z0, b + 1), half_of(Z0, b + 2),
            full_of(Z1, b), full_of(Z1, b + 1), full_of(Z1, b + 2),
            w0, w2, 2, 2, True,
        )
        for j, s in enumerate(HALF):
            L15[i, j] = diag[s][0:8]
        for j, s in enumerate(FULL):
            L15[i, 5 + j] = up[s][0:8]
        L15[i, 14] = (UN[b + 1] + (1.0 - w0) * UN[b] + w2 * UN[b + 2])[0:8]
    src, dst = iota((128, 128), 0), iota((128, 128), 1)
    total = None
    for i in range(2):
        row, z = dst // 32, dst % 32
        hit = (src // 64 == row // 2) & (row % 2 == i) & (src % 64 == 2 * z + 1)
        part = jnp.dot(L15[i].reshape(120, 128), jnp.where(hit, 1.0, 0.0).astype(F32),
                       precision=HI, preferred_element_type=F32)
        total = part if total is None else total + part
    CMP[...] = total
    low_ref[0:60] = CMP[pl.ds(1, 60, stride=2), :]
    low_ref[60:64] = jnp.zeros((4, 128), F32)


def low_widen_kernel(pos_ref, own_ref, swap_ref, other_ref, wide_ref):
    even = pos_ref[5] == 0
    for j in range(15):
        rows = slice(4 * j, 4 * j + 4)
        own, one, two = own_ref[rows], swap_ref[rows], other_ref[rows]
        above, below = jnp.where(even, one, two), jnp.where(even, two, one)
        wide_ref[j] = jnp.concatenate([own, above, own, below], 0)


def low_kernel(pos_ref, own_ref, swap_ref, other_ref, out_ref, E, SRC, UA, UB):
    even = pos_ref[4] == 0
    for j in range(15):
        own, one, two = own_ref[j], swap_ref[j], other_ref[j]
        for b, v in enumerate((jnp.where(even, two, one), own, jnp.where(even, one, two))):
            if j < 14:
                E[b, j] = v
            else:
                SRC[b] = v
    lane = iota((16, 128), 1)
    last = lane >= 96
    first = lane < 32

    def after(get, b):
        here = pltpu.roll(get(b), 96, 1)
        there = pltpu.roll(get(min(b + 1, 2)), 96, 1)
        return jnp.where(last, there, here)

    def before(get, b):
        here = pltpu.roll(get(b), 32, 1)
        there = pltpu.roll(get(max(b - 1, 0)), 32, 1)
        return jnp.where(first, there, here)

    for b in range(3):
        UA[b] = DAMP * SRC[b] / E[b, 0]
    cur, nxt = UA, UB
    for sweep in range(3):
        blocks = (0, 1, 2) if sweep < 2 else (1,)
        for b in blocks:
            u_after = after(lambda c: cur[c], b)
            e0 = {s: E[b, j] for j, s in enumerate(HALF)}
            u = cur[b]
            total = e0[(0, 0)] * u
            for s in FULL:
                total = total + E[b, 5 + FULL.index(s)] * shift(u_after, *s)
                if s in HALF and s != (0, 0):
                    total = total + e0[s] * shift(u, *s)
            for dy in (-1, 0, 1):
                row = None
                for dz in (-1, 0, 1):
                    s = (dy, dz)
                    j = 5 + FULL.index(s)
                    product = before(lambda c: E[c, j] * cur[c], b)
                    if s in HALF and s != (0, 0):
                        product = product + e0[s] * u
                    product = shift(product, 0, -dz)
                    row = product if row is None else row + product
                total = total + shift(row, -dy, 0)
            nxt[b] = u + DAMP * ((SRC[b] - total) / e0[(0, 0)])
        if sweep < 2:
            cur, nxt = nxt, cur
    result = nxt[1]
    for i in range(4):
        out_ref[i] = pltpu.roll(result, (128 - 32 * i) % 128, 1)[0:4, 0:32] if i else result[0:4, 0:32]


def partners(axis, to_swap, to_other):
    n = lax.axis_size(axis)
    swap = [(i, i ^ 1) for i in range(n)]
    other = [(i, (i - 1 if i % 2 == 0 else i + 1) % n) for i in range(n)]
    return lax.ppermute(to_swap, axis, swap), lax.ppermute(to_other, axis, other)


def per_device(material, velocity, density, right_side):
    shape = jax.ShapeDtypeStruct
    params = pltpu.CompilerParams(vmem_limit_bytes=48 * 1024 * 1024)
    smem, vmem = pl.BlockSpec(memory_space=pltpu.SMEM), pl.BlockSpec(memory_space=pltpu.VMEM)
    row_x, row_y = lax.axis_index("gx"), lax.axis_index("gy")
    position = jnp.stack(
        [
            row_x,
            (row_x == lax.axis_size("gx") - 1).astype(jnp.int32),
            row_y,
            (row_y == lax.axis_size("gy") - 1).astype(jnp.int32),
            row_x % 2,
            row_y % 2,
        ]
    ).astype(jnp.int32)
    tables = jnp.concatenate([density, velocity])
    own = pl.pallas_call(
        pack_kernel,
        out_shape=shape((16, 4, 8, 128), F32),
        scratch_shapes=[pltpu.VMEM((16, 16, 128), F32)],
        compiler_params=params,
        name="pack",
    )(material, right_side)
    near = partners("gy", own, own)
    wide, to_swap, to_other = pl.pallas_call(
        widen_kernel,
        in_specs=[smem] + [vmem] * 3,
        out_specs=[vmem] * 3,
        out_shape=(
            shape((16, 4, 16, 128), F32),
            shape((HIGH, 4, 16, 128), F32),
            shape((HIGH, 4, 16, 128), F32),
        ),
        compiler_params=params,
        name="widen",
    )(position, own, *near)
    near = partners("gx", to_swap, to_other)
    vm = lambda *s: pltpu.VMEM(s, F32)
    two, one = (ROWS, 2, 16, 128), (ROWS, 16, 128)
    fine, mid, sent = pl.pallas_call(
        main_kernel,
        in_specs=[smem, smem] + [vmem] * 3,
        out_specs=[vmem] * 3,
        out_shape=(
            shape((16, 16, 128), F32),
            shape((8, 8, 64), F32),
            shape((64, 128), F32),
        ),
        scratch_shapes=[
            vm(*two), vm(*two), vm(*two), vm(*one), vm(*two), vm(*one), vm(*one), vm(*two), vm(*two),
            vm(*two), vm(*one), vm(*two), vm(*two), vm(*two), vm(*two), vm(*one),
            vm(14, 16, 128), vm(13, 16, 128), vm(13, 16, 128),
            vm(16, 2, 16, 128), vm(16, 16, 128), vm(15, 5, 16, 128), vm(15, 9, 16, 128),
            vm(7, 5, 16, 128), vm(8, 9, 16, 128), vm(9, 16, 128), vm(9, 16, 128),
            vm(5, 5, 16, 128), vm(5, 9, 16, 128), vm(2, 15, 8, 128), vm(120, 128), vm(7, 16, 128), vm(7, 16, 128),
        ],
        compiler_params=params,
        name="levels",
    )(tables, position, wide, *near)
    near = partners("gy", sent, sent)
    low = pl.pallas_call(
        low_widen_kernel,
        in_specs=[smem] + [vmem] * 3,
        out_specs=vmem,
        out_shape=shape((15, 16, 128), F32),
        compiler_params=params,
        name="low_widen",
    )(position, sent, *near)
    near = partners("gx", low, low)
    coarse = pl.pallas_call(
        low_kernel,
        in_specs=[smem] + [vmem] * 3,
        out_specs=vmem,
        out_shape=shape((4, 4, 32), F32),
        scratch_shapes=[vm(3, 14, 16, 128), vm(3, 16, 128), vm(3, 16, 128), vm(3, 16, 128)],
        compiler_params=params,
        name="coarse",
    )(position, low, *near)
    return fine, mid, coarse


def solution(mesh):
    return jax.shard_map(
        per_device,
        mesh=mesh,
        in_specs=(P("gx", "gy", None), P(), P(), P("gx", "gy", None)),
        out_specs=(P("gx", "gy", None), P("gx", "gy", None), P("gx", "gy", None)),
        check_vma=False,
    )
```

```python
import jax
import jax.numpy as jnp
from jax import lax
from jax.experimental import pallas as pl
from jax.experimental.pallas import tpu as pltpu
from jax.sharding import PartitionSpec as P

DAMP = 0.7
F32 = jnp.float32
LOW, HIGH = 7, 10
X0 = LOW
ROWS = LOW + 16 + HIGH
HALF = ((0, 0), (0, 1), (1, -1), (1, 0), (1, 1))
FULL = tuple((dy, dz) for dy in (-1, 0, 1) for dz in (-1, 0, 1))
HI = lax.Precision.HIGHEST
BY = (4, 3, 8, 6, 2, 2, 7, 5)


def neg(s):
    return (-s[0], -s[1])


def shift(v, dy, dz, sy=1, sz=1):
    rows, lanes = v.shape
    if dy:
        v = pltpu.roll(v, (-dy * sy) % rows, 0)
    if dz:
        v = pltpu.roll(v, (-dz * sz) % lanes, 1)
    return v


def rows_loop(first, last, body, by):
    def group(start, count):
        stores = []
        for k in range(count):
            stores += body(start + k)
        for ref, index, value in stores:
            ref[index] = value

    count = last - first
    whole = count // by
    if whole == 1:
        group(first, by)
    elif whole > 1:

        def step(n, _):
            group(first + n * by, by)
            return 0

        lax.fori_loop(0, whole, step, 0)
    if count % by:
        group(first + whole * by, count % by)


def inverse(v):
    return pl.reciprocal(v, approx=True)


def iota(shape, dim):
    return lax.broadcasted_iota(jnp.int32, shape, dim)


def depth_order(transposed):
    z = iota((128, 128), 1 if transposed else 0)
    c = iota((128, 128), 0 if transposed else 1)
    source = jnp.where(c < 64, 2 * c, 2 * c - 127)
    return jnp.where(z == source, 1.0, 0.0).astype(F32)


def pack_kernel(pos_ref, mat_ref, rhs_ref, own_ref, to_swap_ref, to_other_ref, fl_ref):
    order = depth_order(False)
    fl_ref[...] = mat_ref[...].astype(F32)
    for q, ref in ((0, fl_ref), (2, rhs_ref)):
        for parity in range(2):
            part = ref[:, pl.ds(parity, 8, stride=2), :].reshape(128, 128)
            precision = HI if q else None
            part = jnp.dot(part, order, precision=precision, preferred_element_type=F32)
            own_ref[:, q + parity] = part.reshape(16, 8, 128)
    even_y = pos_ref[5] == 0

    def send(i, _):
        for n in range(2):
            for q in range(4):
                up, down = own_ref[2 * i + n, q, 3:8], own_ref[2 * i + n, q, 0:5]
                at = slice(20 * n + 5 * q, 20 * n + 5 * q + 5)
                to_swap_ref[i, at] = jnp.where(even_y, up, down)
                to_other_ref[i, at] = jnp.where(even_y, down, up)
        return 0

    lax.fori_loop(0, 8, send, 0, unroll=True)


def widen_kernel(pos_ref, own_ref, swap_ref, other_ref, wide_ref, to_swap_ref, to_other_ref):
    even_x, even_y = pos_ref[4] == 0, pos_ref[5] == 0
    wide_ref[:, :, 0:8] = own_ref[...]

    def receive(i, _):
        for n in range(2):
            for q in range(4):
                at = slice(20 * n + 5 * q, 20 * n + 5 * q + 5)
                one, two = swap_ref[i, at], other_ref[i, at]
                above, below = jnp.where(even_y, one, two), jnp.where(even_y, two, one)
                wide_ref[2 * i + n, q, 8:13] = above
                wide_ref[2 * i + n, q, 13:16] = below[2:5]
                if q == 1:
                    special = below[1:2]
                if q == 3:
                    wide_ref[2 * i + n, q, 12:13] = special
        return 0

    lax.fori_loop(0, 8, receive, 0, unroll=True)
    start = jnp.where(even_x, 16 - HIGH, 0)

    def copy(i, _):
        to_swap_ref[i] = wide_ref[start + i]
        to_other_ref[i] = wide_ref[(16 - HIGH) - start + i]
        return 0

    lax.fori_loop(0, HIGH, copy, 0, unroll=True)


def pick(index, table):
    b0 = (index & 1) == 1
    b1 = (index & 2) == 2
    b2 = (index & 4) == 4
    q = [jnp.where(b0, table[2 * n + 1], table[2 * n]) for n in range(4)]
    q = [jnp.where(b1, q[2 * n + 1], q[2 * n]) for n in range(2)]
    return jnp.where(b2, q[1], q[0])


def collapse_line(tm, t0, tp, l, lc, move, want):
    h, hc = 1.0 - l, 1.0 - lc
    out = {}
    hcp = move(hc, 1)
    lcm = move(lc, -1)
    if 0 in want:
        low = move(h * (hc * t0 + tp), -1)
        high = move(l * (lc * t0 + tm), 1)
        out[0] = t0 + low + high + tm * move(hc, -1) + tp * move(lc, 1)
    if 1 in want:
        out[1] = move(l * (hc * t0 + tp), 1) + tp * hcp
    if -1 in want:
        out[-1] = move(h * (lc * t0 + tm), -1) + tm * lcm
    return out


def collapse_rows(d0, d1, d2, c0, c1, c2, a0, a2, sy, sz, upper):
    h0 = 1.0 - a0
    diag, up = {}, {}
    for s in HALF:
        a2s = shift(a2, *s, sy, sz)
        h0s = 1.0 - shift(a0, *s, sy, sz)
        t10 = shift(c0[neg(s)], *s, sy, sz)
        t21 = shift(c1[neg(s)], *s, sy, sz)
        diag[s] = (
            d1[s]
            + h0 * (h0s * d0[s] + c0[s])
            + h0s * t10
            + a2 * (a2s * d2[s] + t21)
            + a2s * c1[s]
        )
    if upper:
        for s in FULL:
            h2s = 1.0 - shift(a2, *s, sy, sz)
            d2s = d2[s] if s in HALF else shift(d2[neg(s)], *s, sy, sz)
            up[s] = a2 * (h2s * d2s + c2[s]) + h2s * c1[s]
    return diag, up


def apply27(e0, e1, e1_before, u_before, u, u_after):
    total = e0[(0, 0)] * u
    back = {}
    for dy in (-1, 0, 1):
        for dz in (-1, 0, 1):
            s = (dy, dz)
            total = total + e1[s] * shift(u_after, dy, dz)
            if s in HALF and s != (0, 0):
                total = total + e0[s] * shift(u, dy, dz)
    for dy in (-1, 0, 1):
        row = None
        for dz in (-1, 0, 1):
            s = (dy, dz)
            product = e1_before[s] * u_before
            if s in HALF and s != (0, 0):
                product = product + e0[s] * u
            product = shift(product, 0, -dz)
            row = product if row is None else row + product
        total = total + shift(row, -dy, 0)
    return total


def halves(n, shape):
    return iota(shape, 1) < n


def main_kernel(tab_ref, pos_ref, *refs):
    ins = refs[:3]
    fine_ref, mid_ref, low_ref = refs[3:6]
    (D, S, B, OP, CX, CYE, CYO, CZL, CZU, WZ, WY, DG, DI, U1, U2, T, AL, SM, CM,
     WZP, WYP, C0, C1, E0, E1, UM, UN, Z0, Z1, L15, CMP, MD, MS) = refs[6:]
    sh = (16, 128)
    lane = iota(sh, 1)
    subl = iota(sh, 0)
    lt64 = lane < 64
    x_first = pos_ref[0] == 0
    x_last = pos_ref[1] == 1
    y_first = pos_ref[2] == 0
    y_last = pos_ref[3] == 1
    yc = jnp.where(y_first, 0, -1)
    yd = jnp.where(y_last, 8, -1)
    keep_y = jnp.where((subl == yc) | (subl == yd), 0.0, 1.0)
    keep_zl = jnp.where(lane == 0, 0.0, 1.0)
    keep_zu = jnp.where(lane == 127, 0.0, 1.0)
    two_y, two_zl, two_zu = 2.0 * keep_y, 2.0 * keep_zl, 2.0 * keep_zu
    keep_wz = jnp.where((lane == 0) | (lane >= 64), 0.0, 1.0)

    def keep_x(x):
        cut = (x_first & (x == 0)) | (x_last & (x == 16))
        return jnp.where(cut, 0.0, 1.0).astype(F32)

    def r64(v):
        return pltpu.roll(v, 64, 1)

    def z_lower(v):
        return jnp.where(lt64, pltpu.roll(v, 65, 1), r64(v))

    def z_upper(v):
        return jnp.where(lt64, r64(v), pltpu.roll(v, 63, 1))

    def y_next(v):
        return pltpu.roll(v, 15, 0)

    def y_prev(v):
        return pltpu.roll(v, 1, 0)

    tsh = (8, 128)
    den = [jnp.full(tsh, tab_ref[n], F32) for n in range(8)]
    vel = [jnp.full(tsh, tab_ref[8 + n], F32) for n in range(8)]
    sft = [3.0 / (d * v * v) for d, v in zip(den, vel)]
    s8 = iota(tsh, 0)

    even_x = pos_ref[4] == 0

    def segment(first, count, get, by):
        def body(i):
            r = first + i
            v = get(i)
            stores = []
            for p in range(2):
                half = []
                for t in range(2):
                    rows = slice(8 * t, 8 * t + 8)
                    m = v[p][rows].astype(jnp.int32)
                    d = pick(m, den)
                    half.append(d)
                    stores.append((S, (r, p, rows), pick(m, sft)))
                dd = jnp.concatenate(half, 0)
                stores.append((D, (r, p), dd))
                stores.append((B, (r, p), v[2 + p]))
                if p == 1:
                    dd = y_prev(dd)
                    special = pick(v[3][8:16].astype(jnp.int32), den)
                    stores.append((OP, (r, slice(0, 8)), dd[0:8]))
                    extra = jnp.where(s8 == 5, pltpu.roll(special, 1, 0), dd[8:16])
                    stores.append((OP, (r, slice(8, 16)), extra))
            return stores

        rows_loop(0, count, body, by)

    wide_ref, swap_ref, other_ref = ins
    skip = HIGH - LOW
    segment(0, LOW, lambda i: jnp.where(even_x, other_ref[i + skip], swap_ref[i + skip]), BY[0])
    segment(LOW, 16, lambda i: wide_ref[i], BY[0])
    segment(LOW + 16, HIGH, lambda i: jnp.where(even_x, swap_ref[i], other_ref[i]), BY[0])

    def x_coupling(r, p):
        return (2.0 * keep_x(r - X0)) * inverse(D[r, p] + D[r - 1, p])

    for p in range(2):
        CX[1, p] = x_coupling(1, p)

    def coefficients(r):
        de, do, op = D[r, 0], D[r, 1], OP[r]
        sy_m, sy_p = de + op, de + do
        cye = two_y * inverse(sy_m)
        cyo = 2.0 * inverse(sy_p)
        stores = [
            (CYE, r, cye), (CYO, r, cyo), (WY, r, keep_y * sy_p * inverse(sy_m + sy_p)),
        ]
        for p in range(2):
            d = D[r, p]
            lo, up = d + z_lower(d), d + z_upper(d)
            czl = two_zl * inverse(lo)
            czu = two_zu * inverse(up)
            cxl, cxu = x_coupling(r, p), x_coupling(r + 1, p)
            ylo, yup = (cye, cyo) if p == 0 else (cyo, y_next(cye))
            diag = S[r, p] + cxl + cxu + ylo + yup + czl + czu
            di = DAMP * inverse(diag)
            stores += [
                (CZL, (r, p), czl), (CZU, (r, p), czu), (WZ, (r, p), keep_wz * up * inverse(lo + up)),
                (CX, (r + 1, p), cxu), (DG, (r, p), diag), (DI, (r, p), di), (U1, (r, p), di * B[r, p]),
            ]
        return stores

    rows_loop(1, ROWS - 1, coefficients, BY[1])

    def neighbours(U, r):
        e, o = U[r, 0], U[r, 1]
        cye, cyo = CYE[r], CYO[r]
        out = []
        for p in range(2):
            u = (e, o)[p]
            if p == 0:
                along_y = cye * y_prev(o) + cyo * o
            else:
                along_y = cyo * e + y_next(cye * e)
            out.append(
                CX[r, p] * U[r - 1, p]
                + CX[r + 1, p] * U[r + 1, p]
                + along_y
                + CZL[r, p] * z_lower(u)
                + CZU[r, p] * z_upper(u)
            )
        return out

    def second(r):
        around = neighbours(U1, r)
        return [
            (U2, (r, p), U1[r, p] + DI[r, p] * ((1.0 - DAMP) * B[r, p] + around[p])) for p in range(2)
        ]

    rows_loop(2, ROWS - 2, second, BY[2])
    order = depth_order(True)
    for p in range(2):
        part = U2[X0 : X0 + 16, p, 0:8].reshape(128, 128)
        part = jnp.dot(part, order, precision=HI, preferred_element_type=F32)
        fine_ref[:, pl.ds(p, 8, stride=2), :] = part.reshape(16, 8, 128)

    def residual(r):
        around = neighbours(U2, r)
        t = []
        for p in range(2):
            v = B[r, p] - DG[r, p] * U2[r, p] + around[p]
            lowered = WZ[r, p] * v
            t.append(v + r64(v - lowered) + pltpu.roll(lowered, 63, 1))
        te = t[0] * WY[r]
        return [(T, r, t[1] + (t[0] - te) + y_next(te))]

    rows_loop(3, ROWS - 3, residual, BY[3])

    def x_weights(n):
        r = 3 + 2 * n
        d = D[r, 1]
        lo, up = d + D[r - 1, 1], d + D[r + 1, 1]
        return [(AL, n, keep_x(r - X0) * up * inverse(lo + up))]

    rows_loop(0, 14, x_weights, 7)

    def restrict_x(n):
        r = 3 + 2 * n
        return [(SM, n, T[r + 1] + (1.0 - AL[n]) * T[r] + AL[n + 1] * T[r + 2])]

    rows_loop(0, 13, restrict_x, 7)

    def mean_mid(n):
        r = 3 + 2 * n
        total = inverse(D[r, 0]) + inverse(D[r, 1]) + inverse(D[r + 1, 0]) + inverse(D[r + 1, 1])
        return [(CM, n, 0.125 * (total + r64(total)))]

    rows_loop(0, 13, mean_mid, 7)

    def even_part(qa, qb):
        return jnp.where(lt64, qa, r64(qb))

    def odd_part(qa, qb):
        return jnp.where(lt64, r64(qa), qb)

    def pair_weights(n):
        r = 3 + n
        return [(WZP, (n, p), even_part(WZ[r, p], WZ[r + 12, p])) for p in range(2)] + [
            (WYP, n, odd_part(WY[r], WY[r + 12]))
        ]

    rows_loop(0, 16, pair_weights, 4)

    def z1(v):
        return pltpu.roll(v, 127, 1)

    def z_collapse_lateral(c_e, c_o, wa, wb):
        ha, hb = 1.0 - wa, 1.0 - wb
        wc = wa * c_e
        return {
            0: c_o + ha * hb * c_e + z1(wc * wb),
            1: z1(wc * hb),
            -1: (c_e - wc) * wb,
        }

    def build(n):
        stores = []
        r = 3 + n
        q = r + 12
        cen, xup = [], []
        for p in range(2):
            wl = WZP[n, p]
            wh = 1.0 - wl
            dge, dgo = even_part(DG[r, p], DG[q, p]), odd_part(DG[r, p], DG[q, p])
            cze, czo = -even_part(CZL[r, p], CZL[q, p]), -odd_part(CZL[r, p], CZL[q, p])
            wd = wl * dge
            c = dgo + wh * (wh * dge + 2.0 * czo) + z1(wl * (wd + 2.0 * cze))
            m = wh * (wd + cze) + wl * czo
            cen.append({-1: m, 0: c, 1: z1(m)})
            cxe = -even_part(CX[r + 1, p], CX[q + 1, p])
            cxo = -odd_part(CX[r + 1, p], CX[q + 1, p])
            xup.append(z_collapse_lateral(cxe, cxo, wl, WZP[n + 1, p]))
        we, wo = WZP[n, 0], WZP[n, 1]
        F = z_collapse_lateral(-even_part(CYO[r], CYO[q]), -odd_part(CYO[r], CYO[q]), we, wo)
        H = z_collapse_lateral(-even_part(CYE[r], CYE[q]), -odd_part(CYE[r], CYE[q]), we, y_prev(wo))
        vl = WYP[n]
        vh = 1.0 - vl
        ul = WYP[n + 1]
        be, bo = cen
        vls = {d: shift(vl, 0, d) for d in (-1, 0, 1)}
        vhs = {d: 1.0 - vls[d] for d in (-1, 0, 1)}
        uls = {d: shift(ul, 0, d) for d in (-1, 0, 1)}
        uhs = {d: 1.0 - uls[d] for d in (-1, 0, 1)}
        Ht = {d: shift(H[-d], 0, d) for d in (-1, 0, 1)}
        Ft = {d: shift(F[-d], 0, d) for d in (0, 1)}
        for d in (0, 1):
            v = (
                bo[d]
                + vh * (vhs[d] * be[d] + F[d])
                + vhs[d] * Ft[d]
                + y_next(vl * (vls[d] * be[d] + H[d]) + vls[d] * Ht[d])
            )
            stores.append((C0, (n, HALF.index((0, d))), v))
        for d in (-1, 0, 1):
            v = y_next(vl * (vhs[d] * be[d] + F[d]) + vhs[d] * Ht[d])
            stores.append((C0, (n, HALF.index((1, d))), v))
        xe, xo = xup
        for d in (-1, 0, 1):
            lx = vl * xe[d]
            hx = xe[d] - lx
            stores += [
                (C1, (n, FULL.index((0, d))), xo[d] + hx * uhs[d] + y_next(lx * uls[d])),
                (C1, (n, FULL.index((1, d))), y_next(lx * uhs[d])),
                (C1, (n, FULL.index((-1, d))), hx * uls[d]),
            ]
        return stores

    rows_loop(0, 15, build, BY[4])

    def half_of(ref, n):
        return {s: ref[n, j] for j, s in enumerate(HALF)}

    def full_of(ref, n):
        return {s: ref[n, j] for j, s in enumerate(FULL)}

    def join6(n, ref):
        return odd_part(ref[n], ref[n + 6])

    def first_dim(a):
        n = 2 * a
        diag, up = collapse_rows(
            half_of(C0, n), half_of(C0, n + 1), half_of(C0, n + 2),
            full_of(C1, n), full_of(C1, n + 1), full_of(C1, n + 2),
            join6(a, AL), join6(a + 1, AL), 1, 1, True,
        )
        return [(E0, (a, j), diag[s]) for j, s in enumerate(HALF)] + [
            (E1, (a + 1, j), up[s]) for j, s in enumerate(FULL)
        ]

    rows_loop(0, 7, first_dim, BY[5])
    for j in range(9):
        E1[0, j] = r64(E1[6, j])
        E1[7, j] = r64(E1[1, j])

    def mid_first(a):
        di = DAMP * inverse(E0[a, 0])
        source = join6(a, SM)
        return [(MD, a, di), (MS, a, source), (UM, a + 1, di * source)]

    rows_loop(0, 7, mid_first, 7)
    UM[0] = r64(UM[6])
    UM[8] = r64(UM[2])

    def a1(U, a):
        return apply27(half_of(E0, a), full_of(E1, a + 1), full_of(E1, a), U[a], U[a + 1], U[a + 2])

    def mid_second(a):
        return [(UN, a + 1, UM[a + 1] + MD[a] * (MS[a] - a1(UM, a)))]

    rows_loop(0, 7, mid_second, BY[6])
    UN[0] = r64(UN[6])
    UN[8] = r64(UN[2])
    for i in range(4):
        mid_ref[i] = UN[i + 3, 0:8, 0:64]
        mid_ref[i + 4] = r64(UN[i + 1])[0:8, 0:64]

    def mid_residual(a):
        return [(UM, a + 1, MS[a] - a1(UN, a))]

    rows_loop(0, 7, mid_residual, BY[6])

    def at(b, ref, j=None):
        if j is None:
            return jnp.where(lt64, ref[b + 2], ref[b])
        return jnp.where(lt64, ref[b + 2, j], ref[b, j])

    def at1(b, j=None):
        if j is None:
            return jnp.where(lt64, UM[b + 3], UM[b + 1])
        return jnp.where(lt64, E1[b + 3, j], E1[b + 1, j])

    def cm(b):
        return jnp.where(lt64, CM[b + 2], CM[b + 6])

    edge_z = jnp.where((lane == 0) | (lane == 64), 0.0, 1.0)

    def weight(g, before, after, keep):
        lo, up = before * (g + after), after * (g + before)
        return keep * lo * inverse(lo + up)

    def mid_z(b):
        g = cm(b)
        return weight(g, pltpu.roll(g, 1, 1), pltpu.roll(g, 127, 1), edge_z)

    def mid_y(b):
        g = cm(b)
        return weight(g, y_prev(g), y_next(g), keep_y)

    def mid_x(b):
        ka = jnp.where(x_first & (b == 0), 0.0, 1.0).astype(F32)
        kb = jnp.where(x_last & (b == 4), 0.0, 1.0).astype(F32)
        return weight(cm(b), cm(b - 1), cm(b + 1), jnp.where(lt64, ka, kb))

    def move_z(v, n):
        return shift(v, 0, n)

    def move_y(v, n):
        return shift(v, n, 0)

    def build_low(b):
        stores = []
        e0 = {s: at(b, E0, j) for j, s in enumerate(HALF)}
        e1 = {s: at1(b, j) for j, s in enumerate(FULL)}
        lz = (mid_z(b), mid_z(b + 1))
        z0, zz1 = {}, {}
        for dx in (0, 1):
            source, out = ((e0, z0), (e1, zz1))[dx]
            for dy in (-1, 0, 1):
                if dx == 0 and dy == -1:
                    continue
                lc = move_y(lz[dx], dy)
                if dx == 0 and dy == 0:
                    t0, tp = source[(0, 0)], source[(0, 1)]
                    tm = move_z(tp, -1)
                    want = (0, 1)
                else:
                    tm, t0, tp = (source[(dy, d)] for d in (-1, 0, 1))
                    want = (-1, 0, 1)
                for d, v in collapse_line(tm, t0, tp, lz[0], lc, move_z, want).items():
                    out[(dy, d)] = v
        ly = (mid_y(b), mid_y(b + 1))
        for d in (-1, 0, 1):
            lc = shift(ly[0], 0, d, 1, 2)
            want = (0, 1) if d >= 0 else (1,)
            t0 = z0[(0, d)] if d >= 0 else shift(z0[(0, 1)], 0, -1, 1, 2)
            tp = z0[(1, d)]
            tm = shift(z0[(1, -d)], -1, d, 1, 2)
            for dy, v in collapse_line(tm, t0, tp, ly[0], lc, move_y, want).items():
                stores.append((Z0, (b, HALF.index((dy, d))), v))
            lc = shift(ly[1], 0, d, 1, 2)
            tm, t0, tp = (zz1[(dy, d)] for dy in (-1, 0, 1))
            for dy, v in collapse_line(tm, t0, tp, ly[0], lc, move_y, (-1, 0, 1)).items():
                stores.append((Z1, (b, FULL.index((dy, d))), v))
        v = at1(b)
        lv = lz[0] * v
        v = v + move_z(v - lv, -1) + move_z(lv, 1)
        lv = ly[0] * v
        return stores + [(UN, b, v + move_y(v - lv, -1) + move_y(lv, 1))]

    rows_loop(0, 5, build_low, BY[7])

    for i in range(2):
        b = 2 * i
        w0, w2 = mid_x(b), mid_x(b + 2)
        diag, up = collapse_rows(
            half_of(Z0, b), half_of(Z0, b + 1), half_of(Z0, b + 2),
            full_of(Z1, b), full_of(Z1, b + 1), full_of(Z1, b + 2),
            w0, w2, 2, 2, True,
        )
        for j, s in enumerate(HALF):
            L15[i, j] = diag[s][0:8]
        for j, s in enumerate(FULL):
            L15[i, 5 + j] = up[s][0:8]
        L15[i, 14] = (UN[b + 1] + (1.0 - w0) * UN[b] + w2 * UN[b + 2])[0:8]
    src, dst = iota((128, 128), 0), iota((128, 128), 1)
    total = None
    for i in range(2):
        row, z = dst // 32, dst % 32
        hit = (src // 64 == row // 2) & (row % 2 == i) & (src % 64 == 2 * z + 1)
        part = jnp.dot(L15[i].reshape(120, 128), jnp.where(hit, 1.0, 0.0).astype(F32),
                       precision=HI, preferred_element_type=F32)
        total = part if total is None else total + part
    CMP[...] = total
    low_ref[0:60] = CMP[pl.ds(1, 60, stride=2), :]
    low_ref[60:64] = jnp.zeros((4, 128), F32)


def low_widen_kernel(pos_ref, own_ref, swap_ref, other_ref, wide_ref):
    even = pos_ref[5] == 0
    for j in range(15):
        rows = slice(4 * j, 4 * j + 4)
        own, one, two = own_ref[rows], swap_ref[rows], other_ref[rows]
        above, below = jnp.where(even, one, two), jnp.where(even, two, one)
        wide_ref[j] = jnp.concatenate([own, above, own, below], 0)


def low_kernel(pos_ref, own_ref, swap_ref, other_ref, out_ref, E, SRC):
    even = pos_ref[4] == 0
    for j in range(15):
        own, one, two = own_ref[j], swap_ref[j], other_ref[j]
        for b, v in enumerate((jnp.where(even, two, one), own, jnp.where(even, one, two))):
            if j < 14:
                E[b, j] = v
            else:
                SRC[b] = v
    lane = iota((16, 128), 1)
    last = lane >= 96
    first = lane < 32

    def after(rows, b):
        return pltpu.roll(jnp.where(first, rows[min(b + 1, 2)], rows[b]), 96, 1)

    def before(rows, b):
        return pltpu.roll(jnp.where(last, rows[max(b - 1, 0)], rows[b]), 32, 1)

    di = [DAMP * inverse(E[b, 0]) for b in range(3)]
    source = [SRC[b] for b in range(3)]
    cur = [di[b] * source[b] for b in range(3)]

    def lagged(products):
        return {
            dy: products[(dy, 0)] + shift(products[(dy, -1)], 0, 1) + shift(products[(dy, 1)], 0, -1)
            for dy in (-1, 0, 1)
        }

    for sweep in range(3):
        blocks = (0, 1, 2) if sweep < 2 else (1,)
        moved = [lagged({s: E[b, 5 + j] * cur[b] for j, s in enumerate(FULL)}) for b in range(3)]
        nxt = [None] * 3
        for b in blocks:
            u, u_after = cur[b], after(cur, b)
            total = E[b, 0] * u
            e0 = {s: E[b, j] for j, s in enumerate(HALF)}
            for dy in (-1, 0, 1):
                u_row, after_row = shift(u, dy, 0), shift(u_after, dy, 0)
                for dz in (-1, 0, 1):
                    s = (dy, dz)
                    total = total + E[b, 5 + FULL.index(s)] * shift(after_row, 0, dz)
                    if s in HALF and s != (0, 0):
                        total = total + e0[s] * shift(u_row, 0, dz)
                row = before([m[dy] for m in moved], b)
                if dy == 0:
                    row = row + shift(e0[(0, 1)] * u, 0, -1)
                if dy == 1:
                    row = row + e0[(1, 0)] * u + shift(e0[(1, -1)] * u, 0, 1) + shift(e0[(1, 1)] * u, 0, -1)
                total = total + shift(row, -dy, 0)
            nxt[b] = u + di[b] * (source[b] - total)
        cur = nxt
    result = cur[1]
    for i in range(4):
        out_ref[i] = pltpu.roll(result, (128 - 32 * i) % 128, 1)[0:4, 0:32] if i else result[0:4, 0:32]


def partners(axis, to_swap, to_other):
    n = lax.axis_size(axis)
    swap = [(i, i ^ 1) for i in range(n)]
    other = [(i, (i - 1 if i % 2 == 0 else i + 1) % n) for i in range(n)]
    return lax.ppermute(to_swap, axis, swap), lax.ppermute(to_other, axis, other)


def per_device(material, velocity, density, right_side):
    shape = jax.ShapeDtypeStruct
    params = pltpu.CompilerParams(vmem_limit_bytes=48 * 1024 * 1024)
    smem, vmem = pl.BlockSpec(memory_space=pltpu.SMEM), pl.BlockSpec(memory_space=pltpu.VMEM)
    row_x, row_y = lax.axis_index("gx"), lax.axis_index("gy")
    position = jnp.stack(
        [
            row_x,
            (row_x == lax.axis_size("gx") - 1).astype(jnp.int32),
            row_y,
            (row_y == lax.axis_size("gy") - 1).astype(jnp.int32),
            row_x % 2,
            row_y % 2,
        ]
    ).astype(jnp.int32)
    tables = jnp.concatenate([density, velocity])
    own, to_swap, to_other = pl.pallas_call(
        pack_kernel,
        in_specs=[smem, vmem, vmem],
        out_specs=[vmem] * 3,
        out_shape=(shape((16, 4, 8, 128), F32), shape((8, 40, 128), F32), shape((8, 40, 128), F32)),
        scratch_shapes=[
            pltpu.VMEM((16, 16, 128), F32),
        ],
        compiler_params=params,
        name="pack",
    )(position, material, right_side)
    near = partners("gy", to_swap, to_other)
    wide, to_swap, to_other = pl.pallas_call(
        widen_kernel,
        in_specs=[smem] + [vmem] * 3,
        out_specs=[vmem] * 3,
        out_shape=(
            shape((16, 4, 16, 128), F32),
            shape((HIGH, 4, 16, 128), F32),
            shape((HIGH, 4, 16, 128), F32),
        ),
        compiler_params=params,
        name="widen",
    )(position, own, *near)
    near = partners("gx", to_swap, to_other)
    vm = lambda *s: pltpu.VMEM(s, F32)
    two, one = (ROWS, 2, 16, 128), (ROWS, 16, 128)
    fine, mid, sent = pl.pallas_call(
        main_kernel,
        in_specs=[smem, smem] + [vmem] * 3,
        out_specs=[vmem] * 3,
        out_shape=(
            shape((16, 16, 128), F32),
            shape((8, 8, 64), F32),
            shape((64, 128), F32),
        ),
        scratch_shapes=[
            vm(*two), vm(*two), vm(*two), vm(*one), vm(*two), vm(*one), vm(*one), vm(*two), vm(*two),
            vm(*two), vm(*one), vm(*two), vm(*two), vm(*two), vm(*two), vm(*one),
            vm(14, 16, 128), vm(13, 16, 128), vm(13, 16, 128),
            vm(16, 2, 16, 128), vm(16, 16, 128), vm(15, 5, 16, 128), vm(15, 9, 16, 128),
            vm(7, 5, 16, 128), vm(8, 9, 16, 128), vm(9, 16, 128), vm(9, 16, 128),
            vm(5, 5, 16, 128), vm(5, 9, 16, 128), vm(2, 15, 8, 128), vm(120, 128), vm(7, 16, 128), vm(7, 16, 128),
        ],
        compiler_params=params,
        name="levels",
    )(tables, position, wide, *near)
    near = partners("gy", sent, sent)
    low = pl.pallas_call(
        low_widen_kernel,
        in_specs=[smem] + [vmem] * 3,
        out_specs=vmem,
        out_shape=shape((15, 16, 128), F32),
        compiler_params=params,
        name="low_widen",
    )(position, sent, *near)
    near = partners("gx", low, low)
    coarse = pl.pallas_call(
        low_kernel,
        in_specs=[smem] + [vmem] * 3,
        out_specs=vmem,
        out_shape=shape((4, 4, 32), F32),
        scratch_shapes=[vm(3, 14, 16, 128), vm(3, 16, 128)],
        compiler_params=params,
        name="coarse",
    )(position, low, *near)
    return fine, mid, coarse


def solution(mesh):
    return jax.shard_map(
        per_device,
        mesh=mesh,
        in_specs=(P("gx", "gy", None), P(), P(), P("gx", "gy", None)),
        out_specs=(P("gx", "gy", None), P("gx", "gy", None), P("gx", "gy", None)),
        check_vma=False,
    )
```

```python
import jax
import jax.numpy as jnp
from jax import lax
from jax.experimental import pallas as pl
from jax.experimental.pallas import tpu as pltpu
from jax.sharding import PartitionSpec as P

DAMP = 0.7
F32 = jnp.float32
LOW, HIGH = 7, 10
X0 = LOW
ROWS = LOW + 16 + HIGH
HALF = ((0, 0), (0, 1), (1, -1), (1, 0), (1, 1))
FULL = tuple((dy, dz) for dy in (-1, 0, 1) for dz in (-1, 0, 1))
HI = lax.Precision.HIGHEST
BY = (4, 3, 8, 6, 2, 2, 7, 5)


def neg(s):
    return (-s[0], -s[1])


def shift(v, dy, dz, sy=1, sz=1):
    rows, lanes = v.shape
    if dy:
        v = pltpu.roll(v, (-dy * sy) % rows, 0)
    if dz:
        v = pltpu.roll(v, (-dz * sz) % lanes, 1)
    return v


def rows_loop(first, last, body, by):
    def group(start, count):
        stores = []
        for k in range(count):
            stores += body(start + k)
        for ref, index, value in stores:
            ref[index] = value

    count = last - first
    whole = count // by
    if whole == 1:
        group(first, by)
    elif whole > 1:

        def step(n, _):
            group(first + n * by, by)
            return 0

        lax.fori_loop(0, whole, step, 0)
    if count % by:
        group(first + whole * by, count % by)


def inverse(v):
    return pl.reciprocal(v, approx=True)


def iota(shape, dim):
    return lax.broadcasted_iota(jnp.int32, shape, dim)


def depth_order(transposed):
    z = iota((128, 128), 1 if transposed else 0)
    c = iota((128, 128), 0 if transposed else 1)
    source = jnp.where(c < 64, 2 * c, 2 * c - 127)
    return jnp.where(z == source, 1.0, 0.0).astype(F32)


def pack_kernel(pos_ref, mat_ref, rhs_ref, own_ref, to_swap_ref, to_other_ref):
    order = depth_order(False)
    for q, ref in ((0, mat_ref), (2, rhs_ref)):
        for parity in range(2):
            part = ref[:, pl.ds(parity, 8, stride=2), :].reshape(128, 128)
            precision = HI if q else None
            part = jnp.dot(part, order, precision=precision, preferred_element_type=F32)
            own_ref[:, q + parity] = part.reshape(16, 8, 128)
    even_y = pos_ref[5] == 0

    def send(i, _):
        for n in range(2):
            for q in range(4):
                up, down = own_ref[2 * i + n, q, 3:8], own_ref[2 * i + n, q, 0:5]
                at = slice(20 * n + 5 * q, 20 * n + 5 * q + 5)
                to_swap_ref[i, at] = jnp.where(even_y, up, down)
                to_other_ref[i, at] = jnp.where(even_y, down, up)
        return 0

    lax.fori_loop(0, 8, send, 0, unroll=True)


def widen_kernel(pos_ref, own_ref, swap_ref, other_ref, wide_ref, to_swap_ref, to_other_ref):
    even_x, even_y = pos_ref[4] == 0, pos_ref[5] == 0
    wide_ref[:, :, 0:8] = own_ref[...]

    def receive(i, _):
        for n in range(2):
            for q in range(4):
                at = slice(20 * n + 5 * q, 20 * n + 5 * q + 5)
                one, two = swap_ref[i, at], other_ref[i, at]
                above, below = jnp.where(even_y, one, two), jnp.where(even_y, two, one)
                wide_ref[2 * i + n, q, 8:13] = above
                wide_ref[2 * i + n, q, 13:16] = below[2:5]
                if q == 1:
                    special = below[1:2]
                if q == 3:
                    wide_ref[2 * i + n, q, 12:13] = special
        return 0

    lax.fori_loop(0, 8, receive, 0, unroll=True)
    start = jnp.where(even_x, 16 - HIGH, 0)

    def copy(i, _):
        to_swap_ref[i] = wide_ref[start + i]
        to_other_ref[i] = wide_ref[(16 - HIGH) - start + i]
        return 0

    lax.fori_loop(0, HIGH, copy, 0, unroll=True)


def pick(index, table):
    b0 = (index & 1) == 1
    b1 = (index & 2) == 2
    b2 = (index & 4) == 4
    q = [jnp.where(b0, table[2 * n + 1], table[2 * n]) for n in range(4)]
    q = [jnp.where(b1, q[2 * n + 1], q[2 * n]) for n in range(2)]
    return jnp.where(b2, q[1], q[0])


def collapse_line(tm, t0, tp, l, lc, move, want):
    h, hc = 1.0 - l, 1.0 - lc
    out = {}
    hcp = move(hc, 1)
    lcm = move(lc, -1)
    if 0 in want:
        low = move(h * (hc * t0 + tp), -1)
        high = move(l * (lc * t0 + tm), 1)
        out[0] = t0 + low + high + tm * move(hc, -1) + tp * move(lc, 1)
    if 1 in want:
        out[1] = move(l * (hc * t0 + tp), 1) + tp * hcp
    if -1 in want:
        out[-1] = move(h * (lc * t0 + tm), -1) + tm * lcm
    return out


def collapse_rows(d0, d1, d2, c0, c1, c2, a0, a2, sy, sz, upper):
    h0 = 1.0 - a0
    diag, up = {}, {}
    for s in HALF:
        a2s = shift(a2, *s, sy, sz)
        h0s = 1.0 - shift(a0, *s, sy, sz)
        t10 = shift(c0[neg(s)], *s, sy, sz)
        t21 = shift(c1[neg(s)], *s, sy, sz)
        diag[s] = (
            d1[s]
            + h0 * (h0s * d0[s] + c0[s])
            + h0s * t10
            + a2 * (a2s * d2[s] + t21)
            + a2s * c1[s]
        )
    if upper:
        for s in FULL:
            h2s = 1.0 - shift(a2, *s, sy, sz)
            d2s = d2[s] if s in HALF else shift(d2[neg(s)], *s, sy, sz)
            up[s] = a2 * (h2s * d2s + c2[s]) + h2s * c1[s]
    return diag, up


def apply27(e0, e1, e1_before, u_before, u, u_after):
    total = e0[(0, 0)] * u
    back = {}
    for dy in (-1, 0, 1):
        for dz in (-1, 0, 1):
            s = (dy, dz)
            total = total + e1[s] * shift(u_after, dy, dz)
            if s in HALF and s != (0, 0):
                total = total + e0[s] * shift(u, dy, dz)
    for dy in (-1, 0, 1):
        row = None
        for dz in (-1, 0, 1):
            s = (dy, dz)
            product = e1_before[s] * u_before
            if s in HALF and s != (0, 0):
                product = product + e0[s] * u
            product = shift(product, 0, -dz)
            row = product if row is None else row + product
        total = total + shift(row, -dy, 0)
    return total


def halves(n, shape):
    return iota(shape, 1) < n


CARRIED = ("D", "B", "CX", "CYE", "CYO", "CZL", "CZU", "WZ", "WY", "DG", "DI", "U1", "S", "OP", "CA0", "CA1", "CB0", "CB1")


class Fine:
    def __init__(self, tab_ref, pos_ref, arrays):
        for name, value in fine_work(tab_ref, pos_ref, **arrays).items():
            setattr(self, name, value)


def fine_work(tab_ref, pos_ref, D, S, B, OP, CX, CYE, CYO, CZL, CZU, WZ, WY, DG, DI, U1, CA0, CA1, CB0, CB1):
    sh = (16, 128)
    lane = iota(sh, 1)
    subl = iota(sh, 0)
    lt64 = lane < 64
    x_first = pos_ref[0] == 0
    x_last = pos_ref[1] == 1
    y_first = pos_ref[2] == 0
    y_last = pos_ref[3] == 1
    yc = jnp.where(y_first, 0, -1)
    yd = jnp.where(y_last, 8, -1)
    keep_y = jnp.where((subl == yc) | (subl == yd), 0.0, 1.0)
    keep_zl = jnp.where(lane == 0, 0.0, 1.0)
    keep_zu = jnp.where(lane == 127, 0.0, 1.0)
    two_y, two_zl, two_zu = 2.0 * keep_y, 2.0 * keep_zl, 2.0 * keep_zu
    keep_wz = jnp.where((lane == 0) | (lane >= 64), 0.0, 1.0)

    def keep_x(x):
        cut = (x_first & (x == 0)) | (x_last & (x == 16))
        return jnp.where(cut, 0.0, 1.0).astype(F32)

    def r64(v):
        return pltpu.roll(v, 64, 1)

    def z_lower(v):
        return jnp.where(lt64, pltpu.roll(v, 65, 1), r64(v))

    def z_upper(v):
        return jnp.where(lt64, r64(v), pltpu.roll(v, 63, 1))

    def y_next(v):
        return pltpu.roll(v, 15, 0)

    def y_prev(v):
        return pltpu.roll(v, 1, 0)

    tsh = (8, 128)
    den = [jnp.full(tsh, tab_ref[n], F32) for n in range(8)]
    vel = [jnp.full(tsh, tab_ref[8 + n], F32) for n in range(8)]
    sft = [3.0 / (d * v * v) for d, v in zip(den, vel)]
    s8 = iota(tsh, 0)

    even_x = pos_ref[4] == 0

    def segment(first, count, get, by):
        def body(i):
            r = first + i
            v = get(i)
            stores = []
            for p in range(2):
                half = []
                for t in range(2):
                    rows = slice(8 * t, 8 * t + 8)
                    m = v[p][rows].astype(jnp.int32)
                    d = pick(m, den)
                    half.append(d)
                    stores.append((S, (r, p, rows), pick(m, sft)))
                dd = jnp.concatenate(half, 0)
                stores.append((D, (r, p), dd))
                stores.append((B, (r, p), v[2 + p]))
                if p == 1:
                    dd = y_prev(dd)
                    special = pick(v[3][8:16].astype(jnp.int32), den)
                    stores.append((OP, (r, slice(0, 8)), dd[0:8]))
                    extra = jnp.where(s8 == 5, pltpu.roll(special, 1, 0), dd[8:16])
                    stores.append((OP, (r, slice(8, 16)), extra))
            return stores

        rows_loop(0, count, body, by)

    def x_coupling(r, p):
        return (2.0 * keep_x(r - X0)) * inverse(D[r, p] + D[r - 1, p])

    def coefficients(r):
        de, do, op = D[r, 0], D[r, 1], OP[r]
        sy_m, sy_p = de + op, de + do
        cye = two_y * inverse(sy_m)
        cyo = 2.0 * inverse(sy_p)
        stores = [
            (CYE, r, cye), (CYO, r, cyo), (WY, r, keep_y * sy_p * inverse(sy_m + sy_p)),
        ]
        for p in range(2):
            d = D[r, p]
            lo, up = d + z_lower(d), d + z_upper(d)
            czl = two_zl * inverse(lo)
            czu = two_zu * inverse(up)
            cxl, cxu = x_coupling(r, p), x_coupling(r + 1, p)
            ylo, yup = (cye, cyo) if p == 0 else (cyo, y_next(cye))
            diag = S[r, p] + cxl + cxu + ylo + yup + czl + czu
            di = DAMP * inverse(diag)
            stores += [
                (CZL, (r, p), czl), (CZU, (r, p), czu), (WZ, (r, p), keep_wz * up * inverse(lo + up)),
                (CX, (r + 1, p), cxu), (DG, (r, p), diag), (DI, (r, p), di), (U1, (r, p), di * B[r, p]),
            ]
        return stores

    def even_part(qa, qb):
        return jnp.where(lt64, qa, r64(qb))

    def odd_part(qa, qb):
        return jnp.where(lt64, r64(qa), qb)

    def z1(v):
        return pltpu.roll(v, 127, 1)

    def z_collapse_lateral(c_e, c_o, wa, wb):
        ha, hb = 1.0 - wa, 1.0 - wb
        wc = wa * c_e
        return {
            0: c_o + ha * hb * c_e + z1(wc * wb),
            1: z1(wc * hb),
            -1: (c_e - wc) * wb,
        }

    def build(xa, xb):
        stores = []
        r, q = xa + X0, xb + X0
        wz = [even_part(WZ[r, p], WZ[q, p]) for p in range(2)]
        wz_next = [even_part(WZ[r + 1, p], WZ[q + 1, p]) for p in range(2)]

        def put(refs, j, v):
            stores.extend(((refs[0], (xa + 4, j), v), (refs[1], (xb - 8, j), v)))

        cen, xup = [], []
        for p in range(2):
            wl = wz[p]
            wh = 1.0 - wl
            dge, dgo = even_part(DG[r, p], DG[q, p]), odd_part(DG[r, p], DG[q, p])
            cze, czo = -even_part(CZL[r, p], CZL[q, p]), -odd_part(CZL[r, p], CZL[q, p])
            wd = wl * dge
            c = dgo + wh * (wh * dge + 2.0 * czo) + z1(wl * (wd + 2.0 * cze))
            m = wh * (wd + cze) + wl * czo
            cen.append({-1: m, 0: c, 1: z1(m)})
            cxe = -even_part(CX[r + 1, p], CX[q + 1, p])
            cxo = -odd_part(CX[r + 1, p], CX[q + 1, p])
            xup.append(z_collapse_lateral(cxe, cxo, wl, wz_next[p]))
        we, wo = wz
        F = z_collapse_lateral(-even_part(CYO[r], CYO[q]), -odd_part(CYO[r], CYO[q]), we, wo)
        H = z_collapse_lateral(-even_part(CYE[r], CYE[q]), -odd_part(CYE[r], CYE[q]), we, y_prev(wo))
        vl = odd_part(WY[r], WY[q])
        vh = 1.0 - vl
        ul = odd_part(WY[r + 1], WY[q + 1])
        be, bo = cen
        vls = {d: shift(vl, 0, d) for d in (-1, 0, 1)}
        vhs = {d: 1.0 - vls[d] for d in (-1, 0, 1)}
        uls = {d: shift(ul, 0, d) for d in (-1, 0, 1)}
        uhs = {d: 1.0 - uls[d] for d in (-1, 0, 1)}
        Ht = {d: shift(H[-d], 0, d) for d in (-1, 0, 1)}
        Ft = {d: shift(F[-d], 0, d) for d in (0, 1)}
        for d in (0, 1):
            v = (
                bo[d]
                + vh * (vhs[d] * be[d] + F[d])
                + vhs[d] * Ft[d]
                + y_next(vl * (vls[d] * be[d] + H[d]) + vls[d] * Ht[d])
            )
            put((CA0, CB0), HALF.index((0, d)), v)
        for d in (-1, 0, 1):
            v = y_next(vl * (vhs[d] * be[d] + F[d]) + vhs[d] * Ht[d])
            put((CA0, CB0), HALF.index((1, d)), v)
        xe, xo = xup
        for d in (-1, 0, 1):
            lx = vl * xe[d]
            hx = xe[d] - lx
            put((CA1, CB1), FULL.index((0, d)), xo[d] + hx * uhs[d] + y_next(lx * uls[d]))
            put((CA1, CB1), FULL.index((1, d)), y_next(lx * uhs[d]))
            put((CA1, CB1), FULL.index((-1, d)), hx * uls[d])
        return stores

    return locals()


def inner_kernel(tab_ref, pos_ref, wide_ref, *refs):
    arrays = dict(zip(CARRIED, refs))
    f = Fine(tab_ref, pos_ref, arrays)
    f.segment(LOW, 16, lambda i: wide_ref[i], BY[0])
    rows_loop(X0 + 1, X0 + 15, f.coefficients, BY[1])
    rows_loop(1, 7, lambda x: f.build(x, x + 7), BY[4])


def main_kernel(tab_ref, pos_ref, swap_ref, other_ref, *refs):
    refs = refs[len(CARRIED) :]
    fine_ref, mid_ref, low_ref = refs[:3]
    arrays = dict(zip(CARRIED, refs[3 : 3 + len(CARRIED)]))
    (U2, T, AL, SM, CM,
     E0, E1, UM, UN, Z0, Z1, L15, CMP, MD, MS) = refs[3 + len(CARRIED) :]
    D, B, CX, CYE, CYO, CZL, CZU, WZ, WY, DG, DI, U1, _, _, CA0, CA1, CB0, CB1 = (
        arrays[n] for n in CARRIED
    )
    f = Fine(tab_ref, pos_ref, arrays)
    sh, lane, lt64, even_x = f.sh, f.lane, f.lt64, f.even_x
    r64, y_next, y_prev, z_lower, z_upper = f.r64, f.y_next, f.y_prev, f.z_lower, f.z_upper
    keep_x, keep_y, odd_part, x_first, x_last = f.keep_x, f.keep_y, f.odd_part, f.x_first, f.x_last
    skip = HIGH - LOW
    f.segment(0, LOW, lambda i: jnp.where(even_x, other_ref[i + skip], swap_ref[i + skip]), BY[0])
    f.segment(LOW + 16, HIGH, lambda i: jnp.where(even_x, swap_ref[i], other_ref[i]), BY[0])
    for p in range(2):
        CX[1, p] = f.x_coupling(1, p)
    rows_loop(1, X0 + 1, f.coefficients, BY[1])
    rows_loop(X0 + 15, ROWS - 1, f.coefficients, BY[1])

    def neighbours(U, r):
        e, o = U[r, 0], U[r, 1]
        cye, cyo = CYE[r], CYO[r]
        out = []
        for p in range(2):
            u = (e, o)[p]
            if p == 0:
                along_y = cye * y_prev(o) + cyo * o
            else:
                along_y = cyo * e + y_next(cye * e)
            out.append(
                CX[r, p] * U[r - 1, p]
                + CX[r + 1, p] * U[r + 1, p]
                + along_y
                + CZL[r, p] * z_lower(u)
                + CZU[r, p] * z_upper(u)
            )
        return out

    def second(r):
        around = neighbours(U1, r)
        return [
            (U2, (r, p), U1[r, p] + DI[r, p] * ((1.0 - DAMP) * B[r, p] + around[p])) for p in range(2)
        ]

    rows_loop(2, ROWS - 2, second, BY[2])
    order = depth_order(True)
    for p in range(2):
        part = U2[X0 : X0 + 16, p, 0:8].reshape(128, 128)
        part = jnp.dot(part, order, precision=HI, preferred_element_type=F32)
        fine_ref[:, pl.ds(p, 8, stride=2), :] = part.reshape(16, 8, 128)

    def residual(r):
        around = neighbours(U2, r)
        t = []
        for p in range(2):
            v = B[r, p] - DG[r, p] * U2[r, p] + around[p]
            lowered = WZ[r, p] * v
            t.append(v + r64(v - lowered) + pltpu.roll(lowered, 63, 1))
        te = t[0] * WY[r]
        return [(T, r, t[1] + (t[0] - te) + y_next(te))]

    rows_loop(3, ROWS - 3, residual, BY[3])

    def x_weights(n):
        r = 3 + 2 * n
        d = D[r, 1]
        lo, up = d + D[r - 1, 1], d + D[r + 1, 1]
        return [(AL, n, keep_x(r - X0) * up * inverse(lo + up))]

    rows_loop(0, 14, x_weights, 7)

    def restrict_x(n):
        r = 3 + 2 * n
        return [(SM, n, T[r + 1] + (1.0 - AL[n]) * T[r] + AL[n + 1] * T[r + 2])]

    rows_loop(0, 13, restrict_x, 7)

    def mean_mid(n):
        r = 3 + 2 * n
        total = inverse(D[r, 0]) + inverse(D[r, 1]) + inverse(D[r + 1, 0]) + inverse(D[r + 1, 1])
        return [(CM, n, 0.125 * (total + r64(total)))]

    rows_loop(0, 13, mean_mid, 7)

    rows_loop(-4, 1, lambda x: f.build(x, x + 18), BY[4])
    rows_loop(7, 11, lambda x: f.build(x, x + 12), BY[4])

    def both(first, second, n, j):
        return jnp.where(lt64, first[n, j], second[n, j])

    def half_of(ref, n):
        return {s: ref[n, j] for j, s in enumerate(HALF)}

    def full_of(ref, n):
        return {s: ref[n, j] for j, s in enumerate(FULL)}

    def join6(n, ref):
        return odd_part(ref[n], ref[n + 6])

    def first_dim(a):
        n = 2 * a
        diag, up = collapse_rows(
            *({s: both(CA0, CB0, n + k, j) for j, s in enumerate(HALF)} for k in range(3)),
            *({s: both(CA1, CB1, n + k, j) for j, s in enumerate(FULL)} for k in range(3)),
            join6(a, AL), join6(a + 1, AL), 1, 1, True,
        )
        return [(E0, (a, j), diag[s]) for j, s in enumerate(HALF)] + [
            (E1, (a + 1, j), up[s]) for j, s in enumerate(FULL)
        ]

    rows_loop(0, 7, first_dim, BY[5])
    for j in range(9):
        E1[0, j] = r64(E1[6, j])
        E1[7, j] = r64(E1[1, j])

    def mid_first(a):
        di = DAMP * inverse(E0[a, 0])
        source = join6(a, SM)
        return [(MD, a, di), (MS, a, source), (UM, a + 1, di * source)]

    rows_loop(0, 7, mid_first, 7)
    UM[0] = r64(UM[6])
    UM[8] = r64(UM[2])

    def a1(U, a):
        return apply27(half_of(E0, a), full_of(E1, a + 1), full_of(E1, a), U[a], U[a + 1], U[a + 2])

    def mid_second(a):
        return [(UN, a + 1, UM[a + 1] + MD[a] * (MS[a] - a1(UM, a)))]

    rows_loop(0, 7, mid_second, BY[6])
    UN[0] = r64(UN[6])
    UN[8] = r64(UN[2])
    for i in range(4):
        mid_ref[i] = UN[i + 3, 0:8, 0:64]
        mid_ref[i + 4] = r64(UN[i + 1])[0:8, 0:64]

    def mid_residual(a):
        return [(UM, a + 1, MS[a] - a1(UN, a))]

    rows_loop(0, 7, mid_residual, BY[6])

    def at(b, ref, j=None):
        if j is None:
            return jnp.where(lt64, ref[b + 2], ref[b])
        return jnp.where(lt64, ref[b + 2, j], ref[b, j])

    def at1(b, j=None):
        if j is None:
            return jnp.where(lt64, UM[b + 3], UM[b + 1])
        return jnp.where(lt64, E1[b + 3, j], E1[b + 1, j])

    def cm(b):
        return jnp.where(lt64, CM[b + 2], CM[b + 6])

    edge_z = jnp.where((lane == 0) | (lane == 64), 0.0, 1.0)

    def weight(g, before, after, keep):
        lo, up = before * (g + after), after * (g + before)
        return keep * lo * inverse(lo + up)

    def mid_z(b):
        g = cm(b)
        return weight(g, pltpu.roll(g, 1, 1), pltpu.roll(g, 127, 1), edge_z)

    def mid_y(b):
        g = cm(b)
        return weight(g, y_prev(g), y_next(g), keep_y)

    def mid_x(b):
        ka = jnp.where(x_first & (b == 0), 0.0, 1.0).astype(F32)
        kb = jnp.where(x_last & (b == 4), 0.0, 1.0).astype(F32)
        return weight(cm(b), cm(b - 1), cm(b + 1), jnp.where(lt64, ka, kb))

    def move_z(v, n):
        return shift(v, 0, n)

    def move_y(v, n):
        return shift(v, n, 0)

    def build_low(b):
        stores = []
        e0 = {s: at(b, E0, j) for j, s in enumerate(HALF)}
        e1 = {s: at1(b, j) for j, s in enumerate(FULL)}
        lz = (mid_z(b), mid_z(b + 1))
        z0, zz1 = {}, {}
        for dx in (0, 1):
            source, out = ((e0, z0), (e1, zz1))[dx]
            for dy in (-1, 0, 1):
                if dx == 0 and dy == -1:
                    continue
                lc = move_y(lz[dx], dy)
                if dx == 0 and dy == 0:
                    t0, tp = source[(0, 0)], source[(0, 1)]
                    tm = move_z(tp, -1)
                    want = (0, 1)
                else:
                    tm, t0, tp = (source[(dy, d)] for d in (-1, 0, 1))
                    want = (-1, 0, 1)
                for d, v in collapse_line(tm, t0, tp, lz[0], lc, move_z, want).items():
                    out[(dy, d)] = v
        ly = (mid_y(b), mid_y(b + 1))
        for d in (-1, 0, 1):
            lc = shift(ly[0], 0, d, 1, 2)
            want = (0, 1) if d >= 0 else (1,)
            t0 = z0[(0, d)] if d >= 0 else shift(z0[(0, 1)], 0, -1, 1, 2)
            tp = z0[(1, d)]
            tm = shift(z0[(1, -d)], -1, d, 1, 2)
            for dy, v in collapse_line(tm, t0, tp, ly[0], lc, move_y, want).items():
                stores.append((Z0, (b, HALF.index((dy, d))), v))
            lc = shift(ly[1], 0, d, 1, 2)
            tm, t0, tp = (zz1[(dy, d)] for dy in (-1, 0, 1))
            for dy, v in collapse_line(tm, t0, tp, ly[0], lc, move_y, (-1, 0, 1)).items():
                stores.append((Z1, (b, FULL.index((dy, d))), v))
        v = at1(b)
        lv = lz[0] * v
        v = v + move_z(v - lv, -1) + move_z(lv, 1)
        lv = ly[0] * v
        return stores + [(UN, b, v + move_y(v - lv, -1) + move_y(lv, 1))]

    rows_loop(0, 5, build_low, BY[7])

    for i in range(2):
        b = 2 * i
        w0, w2 = mid_x(b), mid_x(b + 2)
        diag, up = collapse_rows(
            half_of(Z0, b), half_of(Z0, b + 1), half_of(Z0, b + 2),
            full_of(Z1, b), full_of(Z1, b + 1), full_of(Z1, b + 2),
            w0, w2, 2, 2, True,
        )
        for j, s in enumerate(HALF):
            L15[i, j] = diag[s][0:8]
        for j, s in enumerate(FULL):
            L15[i, 5 + j] = up[s][0:8]
        L15[i, 14] = (UN[b + 1] + (1.0 - w0) * UN[b] + w2 * UN[b + 2])[0:8]
    src, dst = iota((128, 128), 0), iota((128, 128), 1)
    total = None
    for i in range(2):
        row, z = dst // 32, dst % 32
        hit = (src // 64 == row // 2) & (row % 2 == i) & (src % 64 == 2 * z + 1)
        part = jnp.dot(L15[i].reshape(120, 128), jnp.where(hit, 1.0, 0.0).astype(F32),
                       precision=HI, preferred_element_type=F32)
        total = part if total is None else total + part
    CMP[...] = total
    low_ref[0:60] = CMP[pl.ds(1, 60, stride=2), :]
    low_ref[60:64] = jnp.zeros((4, 128), F32)


def low_widen_kernel(pos_ref, own_ref, swap_ref, other_ref, wide_ref):
    even = pos_ref[5] == 0
    for j in range(15):
        rows = slice(4 * j, 4 * j + 4)
        own, one, two = own_ref[rows], swap_ref[rows], other_ref[rows]
        above, below = jnp.where(even, one, two), jnp.where(even, two, one)
        wide_ref[j] = jnp.concatenate([own, above, own, below], 0)


def low_kernel(pos_ref, own_ref, swap_ref, other_ref, out_ref, E, SRC):
    even = pos_ref[4] == 0
    for j in range(15):
        own, one, two = own_ref[j], swap_ref[j], other_ref[j]
        for b, v in enumerate((jnp.where(even, two, one), own, jnp.where(even, one, two))):
            if j < 14:
                E[b, j] = v
            else:
                SRC[b] = v
    lane = iota((16, 128), 1)
    last = lane >= 96
    first = lane < 32

    def after(rows, b):
        return pltpu.roll(jnp.where(first, rows[min(b + 1, 2)], rows[b]), 96, 1)

    def before(rows, b):
        return pltpu.roll(jnp.where(last, rows[max(b - 1, 0)], rows[b]), 32, 1)

    di = [DAMP * inverse(E[b, 0]) for b in range(3)]
    source = [SRC[b] for b in range(3)]
    cur = [di[b] * source[b] for b in range(3)]

    def lagged(products):
        return {
            dy: products[(dy, 0)] + shift(products[(dy, -1)], 0, 1) + shift(products[(dy, 1)], 0, -1)
            for dy in (-1, 0, 1)
        }

    for sweep in range(3):
        blocks = (0, 1, 2) if sweep < 2 else (1,)
        moved = [lagged({s: E[b, 5 + j] * cur[b] for j, s in enumerate(FULL)}) for b in range(3)]
        nxt = [None] * 3
        for b in blocks:
            u, u_after = cur[b], after(cur, b)
            total = E[b, 0] * u
            e0 = {s: E[b, j] for j, s in enumerate(HALF)}
            for dy in (-1, 0, 1):
                u_row, after_row = shift(u, dy, 0), shift(u_after, dy, 0)
                for dz in (-1, 0, 1):
                    s = (dy, dz)
                    total = total + E[b, 5 + FULL.index(s)] * shift(after_row, 0, dz)
                    if s in HALF and s != (0, 0):
                        total = total + e0[s] * shift(u_row, 0, dz)
                row = before([m[dy] for m in moved], b)
                if dy == 0:
                    row = row + shift(e0[(0, 1)] * u, 0, -1)
                if dy == 1:
                    row = row + e0[(1, 0)] * u + shift(e0[(1, -1)] * u, 0, 1) + shift(e0[(1, 1)] * u, 0, -1)
                total = total + shift(row, -dy, 0)
            nxt[b] = u + di[b] * (source[b] - total)
        cur = nxt
    result = cur[1]
    for i in range(4):
        out_ref[i] = pltpu.roll(result, (128 - 32 * i) % 128, 1)[0:4, 0:32] if i else result[0:4, 0:32]


def partners(axis, to_swap, to_other):
    n = lax.axis_size(axis)
    swap = [(i, i ^ 1) for i in range(n)]
    other = [(i, (i - 1 if i % 2 == 0 else i + 1) % n) for i in range(n)]
    return lax.ppermute(to_swap, axis, swap), lax.ppermute(to_other, axis, other)


def per_device(material, velocity, density, right_side):
    shape = jax.ShapeDtypeStruct
    params = pltpu.CompilerParams(vmem_limit_bytes=48 * 1024 * 1024)
    smem, vmem = pl.BlockSpec(memory_space=pltpu.SMEM), pl.BlockSpec(memory_space=pltpu.VMEM)
    row_x, row_y = lax.axis_index("gx"), lax.axis_index("gy")
    position = jnp.stack(
        [
            row_x,
            (row_x == lax.axis_size("gx") - 1).astype(jnp.int32),
            row_y,
            (row_y == lax.axis_size("gy") - 1).astype(jnp.int32),
            row_x % 2,
            row_y % 2,
        ]
    ).astype(jnp.int32)
    tables = jnp.concatenate([density, velocity])
    own, to_swap, to_other = pl.pallas_call(
        pack_kernel,
        in_specs=[smem, vmem, vmem],
        out_specs=[vmem] * 3,
        out_shape=(shape((16, 4, 8, 128), F32), shape((8, 40, 128), F32), shape((8, 40, 128), F32)),
        compiler_params=params,
        name="pack",
    )(position, material.astype(F32), right_side)
    near = partners("gy", to_swap, to_other)
    wide, to_swap, to_other = pl.pallas_call(
        widen_kernel,
        in_specs=[smem] + [vmem] * 3,
        out_specs=[vmem] * 3,
        out_shape=(
            shape((16, 4, 16, 128), F32),
            shape((HIGH, 4, 16, 128), F32),
            shape((HIGH, 4, 16, 128), F32),
        ),
        compiler_params=params,
        name="widen",
    )(position, own, *near)
    vm = lambda *s: pltpu.VMEM(s, F32)
    two, one = (ROWS, 2, 16, 128), (ROWS, 16, 128)
    carried = [two, two, two, one, one, two, two, two, one, two, two, two, two, one]
    carried += [(15, n, 16, 128) for n in (5, 9, 5, 9)]
    carried = [shape(c, F32) for c in carried]
    count = len(carried)
    inner = pl.pallas_call(
        inner_kernel,
        in_specs=[smem, smem, vmem],
        out_specs=[vmem] * count,
        out_shape=carried,
        compiler_params=pltpu.CompilerParams(vmem_limit_bytes=24 * 1024 * 1024),
        cost_estimate=pl.CostEstimate(flops=20_000_000, bytes_accessed=8_000_000, transcendentals=0),
        name="inner",
    )(tables, position, wide)
    to_swap, *inner = lax.optimization_barrier((to_swap, *inner))
    near = partners("gx", to_swap, to_other)
    fine, mid, sent = pl.pallas_call(
        main_kernel,
        in_specs=[smem, smem] + [vmem] * (2 + count),
        out_specs=[vmem] * (3 + count),
        out_shape=[
            shape((16, 16, 128), F32),
            shape((8, 8, 64), F32),
            shape((64, 128), F32),
        ] + carried,
        input_output_aliases={4 + n: 3 + n for n in range(count)},
        scratch_shapes=[
            vm(*two), vm(*one),
            vm(14, 16, 128), vm(13, 16, 128), vm(13, 16, 128),
            vm(7, 5, 16, 128), vm(8, 9, 16, 128), vm(9, 16, 128), vm(9, 16, 128),
            vm(5, 5, 16, 128), vm(5, 9, 16, 128), vm(2, 15, 8, 128), vm(120, 128), vm(7, 16, 128), vm(7, 16, 128),
        ],
        compiler_params=pltpu.CompilerParams(vmem_limit_bytes=24 * 1024 * 1024),
        name="levels",
    )(tables, position, *near, *inner)[:3]
    near = partners("gy", sent, sent)
    low = pl.pallas_call(
        low_widen_kernel,
        in_specs=[smem] + [vmem] * 3,
        out_specs=vmem,
        out_shape=shape((15, 16, 128), F32),
        compiler_params=params,
        name="low_widen",
    )(position, sent, *near)
    near = partners("gx", low, low)
    coarse = pl.pallas_call(
        low_kernel,
        in_specs=[smem] + [vmem] * 3,
        out_specs=vmem,
        out_shape=shape((4, 4, 32), F32),
        scratch_shapes=[vm(3, 14, 16, 128), vm(3, 16, 128)],
        compiler_params=params,
        name="coarse",
    )(position, low, *near)
    return fine, mid, coarse


def solution(mesh):
    return jax.shard_map(
        per_device,
        mesh=mesh,
        in_specs=(P("gx", "gy", None), P(), P(), P("gx", "gy", None)),
        out_specs=(P("gx", "gy", None), P("gx", "gy", None), P("gx", "gy", None)),
        check_vma=False,
    )
```

```python
import jax
import jax.numpy as jnp
from jax import lax
from jax.experimental import pallas as pl
from jax.experimental.pallas import tpu as pltpu
from jax.sharding import PartitionSpec as P

DAMP = 0.7
F32 = jnp.float32
LOW, HIGH = 7, 10
X0 = LOW
ROWS = LOW + 16 + HIGH
HALF = ((0, 0), (0, 1), (1, -1), (1, 0), (1, 1))
FULL = tuple((dy, dz) for dy in (-1, 0, 1) for dz in (-1, 0, 1))
HI = lax.Precision.HIGHEST
BY = (5, 5, 8, 6, 2, 2, 7, 5)


def neg(s):
    return (-s[0], -s[1])


def shift(v, dy, dz, sy=1, sz=1):
    rows, lanes = v.shape
    if dy:
        v = pltpu.roll(v, (-dy * sy) % rows, 0)
    if dz:
        v = pltpu.roll(v, (-dz * sz) % lanes, 1)
    return v


def rows_loop(first, last, body, by):
    def group(start, count):
        stores = []
        for k in range(count):
            stores += body(start + k)
        for ref, index, value in stores:
            ref[index] = value

    count = last - first
    whole = count // by
    if whole == 1:
        group(first, by)
    elif whole > 1:

        def step(n, _):
            group(first + n * by, by)
            return 0

        lax.fori_loop(0, whole, step, 0)
    if count % by:
        group(first + whole * by, count % by)


def inverse(v):
    return pl.reciprocal(v, approx=True)


def iota(shape, dim):
    return lax.broadcasted_iota(jnp.int32, shape, dim)


def depth_order(transposed):
    z = iota((128, 128), 1 if transposed else 0)
    c = iota((128, 128), 0 if transposed else 1)
    source = jnp.where(c < 64, 2 * c, 2 * c - 127)
    return jnp.where(z == source, 1.0, 0.0).astype(F32)


def pack_kernel(pos_ref, mat_ref, rhs_ref, own_ref, to_swap_ref, to_other_ref):
    order = depth_order(False)
    for q, ref in ((0, mat_ref), (2, rhs_ref)):
        for parity in range(2):
            part = ref[:, pl.ds(parity, 8, stride=2), :].reshape(128, 128)
            precision = HI if q else None
            part = jnp.dot(part, order, precision=precision, preferred_element_type=F32)
            own_ref[:, q + parity] = part.reshape(16, 8, 128)
    even_y = pos_ref[5] == 0

    def send(i, _):
        for n in range(2):
            for q in range(4):
                up, down = own_ref[2 * i + n, q, 3:8], own_ref[2 * i + n, q, 0:5]
                at = slice(20 * n + 5 * q, 20 * n + 5 * q + 5)
                to_swap_ref[i, at] = jnp.where(even_y, up, down)
                to_other_ref[i, at] = jnp.where(even_y, down, up)
        return 0

    lax.fori_loop(0, 8, send, 0, unroll=True)


def widen_kernel(pos_ref, own_ref, swap_ref, other_ref, wide_ref, to_swap_ref, to_other_ref):
    even_x, even_y = pos_ref[4] == 0, pos_ref[5] == 0
    wide_ref[:, :, 0:8] = own_ref[...]

    def receive(i, _):
        for n in range(2):
            for q in range(4):
                at = slice(20 * n + 5 * q, 20 * n + 5 * q + 5)
                one, two = swap_ref[i, at], other_ref[i, at]
                above, below = jnp.where(even_y, one, two), jnp.where(even_y, two, one)
                wide_ref[2 * i + n, q, 8:13] = above
                wide_ref[2 * i + n, q, 13:16] = below[2:5]
                if q == 1:
                    special = below[1:2]
                if q == 3:
                    wide_ref[2 * i + n, q, 12:13] = special
        return 0

    lax.fori_loop(0, 8, receive, 0, unroll=True)
    start = jnp.where(even_x, 16 - HIGH, 0)

    def copy(i, _):
        to_swap_ref[i] = wide_ref[start + i]
        to_other_ref[i] = wide_ref[(16 - HIGH) - start + i]
        return 0

    lax.fori_loop(0, HIGH, copy, 0, unroll=True)


def pick(index, table):
    b0 = (index & 1) == 1
    b1 = (index & 2) == 2
    b2 = (index & 4) == 4
    q = [jnp.where(b0, table[2 * n + 1], table[2 * n]) for n in range(4)]
    q = [jnp.where(b1, q[2 * n + 1], q[2 * n]) for n in range(2)]
    return jnp.where(b2, q[1], q[0])


def collapse_line(tm, t0, tp, l, lc, move, want):
    h, hc = 1.0 - l, 1.0 - lc
    out = {}
    hcp = move(hc, 1)
    lcm = move(lc, -1)
    if 0 in want:
        low = move(h * (hc * t0 + tp), -1)
        high = move(l * (lc * t0 + tm), 1)
        out[0] = t0 + low + high + tm * move(hc, -1) + tp * move(lc, 1)
    if 1 in want:
        out[1] = move(l * (hc * t0 + tp), 1) + tp * hcp
    if -1 in want:
        out[-1] = move(h * (lc * t0 + tm), -1) + tm * lcm
    return out


def collapse_rows(d0, d1, d2, c0, c1, c2, a0, a2, sy, sz, upper):
    h0 = 1.0 - a0
    diag, up = {}, {}
    for s in HALF:
        a2s = shift(a2, *s, sy, sz)
        h0s = 1.0 - shift(a0, *s, sy, sz)
        t10 = shift(c0[neg(s)], *s, sy, sz)
        t21 = shift(c1[neg(s)], *s, sy, sz)
        diag[s] = (
            d1[s]
            + h0 * (h0s * d0[s] + c0[s])
            + h0s * t10
            + a2 * (a2s * d2[s] + t21)
            + a2s * c1[s]
        )
    if upper:
        for s in FULL:
            h2s = 1.0 - shift(a2, *s, sy, sz)
            d2s = d2[s] if s in HALF else shift(d2[neg(s)], *s, sy, sz)
            up[s] = a2 * (h2s * d2s + c2[s]) + h2s * c1[s]
    return diag, up


def apply27(e0, e1, e1_before, u_before, u, u_after):
    total = e0[(0, 0)] * u
    back = {}
    for dy in (-1, 0, 1):
        for dz in (-1, 0, 1):
            s = (dy, dz)
            total = total + e1[s] * shift(u_after, dy, dz)
            if s in HALF and s != (0, 0):
                total = total + e0[s] * shift(u, dy, dz)
    for dy in (-1, 0, 1):
        row = None
        for dz in (-1, 0, 1):
            s = (dy, dz)
            product = e1_before[s] * u_before
            if s in HALF and s != (0, 0):
                product = product + e0[s] * u
            product = shift(product, 0, -dz)
            row = product if row is None else row + product
        total = total + shift(row, -dy, 0)
    return total


def halves(n, shape):
    return iota(shape, 1) < n


CARRIED = ("D", "B", "CX", "CYE", "CYO", "CZL", "CZU", "WZ", "WY", "DG", "DI", "U1", "S", "OP", "CA0", "CA1", "CB0", "CB1")


class Fine:
    def __init__(self, tab_ref, pos_ref, arrays):
        for name, value in fine_work(tab_ref, pos_ref, **arrays).items():
            setattr(self, name, value)


def fine_work(tab_ref, pos_ref, D, S, B, OP, CX, CYE, CYO, CZL, CZU, WZ, WY, DG, DI, U1, CA0, CA1, CB0, CB1):
    sh = (16, 128)
    lane = iota(sh, 1)
    subl = iota(sh, 0)
    lt64 = lane < 64
    x_first = pos_ref[0] == 0
    x_last = pos_ref[1] == 1
    y_first = pos_ref[2] == 0
    y_last = pos_ref[3] == 1
    yc = jnp.where(y_first, 0, -1)
    yd = jnp.where(y_last, 8, -1)
    keep_y = jnp.where((subl == yc) | (subl == yd), 0.0, 1.0)
    keep_zl = jnp.where(lane == 0, 0.0, 1.0)
    keep_zu = jnp.where(lane == 127, 0.0, 1.0)
    two_y, two_zl, two_zu = 2.0 * keep_y, 2.0 * keep_zl, 2.0 * keep_zu
    keep_wz = jnp.where((lane == 0) | (lane >= 64), 0.0, 1.0)

    def keep_x(x):
        cut = (x_first & (x == 0)) | (x_last & (x == 16))
        return jnp.where(cut, 0.0, 1.0).astype(F32)

    def r64(v):
        return pltpu.roll(v, 64, 1)

    def z_lower(v):
        return jnp.where(lt64, pltpu.roll(v, 65, 1), r64(v))

    def z_upper(v):
        return jnp.where(lt64, r64(v), pltpu.roll(v, 63, 1))

    def y_next(v):
        return pltpu.roll(v, 15, 0)

    def y_prev(v):
        return pltpu.roll(v, 1, 0)

    tsh = (8, 128)
    den = [jnp.full(tsh, tab_ref[n], F32) for n in range(8)]
    vel = [jnp.full(tsh, tab_ref[8 + n], F32) for n in range(8)]
    sft = [3.0 / (d * v * v) for d, v in zip(den, vel)]
    s8 = iota(tsh, 0)

    even_x = pos_ref[4] == 0

    def segment(first, count, get, by):
        def body(i):
            r = first + i
            v = get(i)
            stores = []
            for p in range(2):
                half = []
                for t in range(2):
                    rows = slice(8 * t, 8 * t + 8)
                    m = v[p][rows].astype(jnp.int32)
                    d = pick(m, den)
                    half.append(d)
                    stores.append((S, (r, p, rows), pick(m, sft)))
                dd = jnp.concatenate(half, 0)
                stores.append((D, (r, p), dd))
                stores.append((B, (r, p), v[2 + p]))
                if p == 1:
                    dd = y_prev(dd)
                    special = pick(v[3][8:16].astype(jnp.int32), den)
                    stores.append((OP, (r, slice(0, 8)), dd[0:8]))
                    extra = jnp.where(s8 == 5, pltpu.roll(special, 1, 0), dd[8:16])
                    stores.append((OP, (r, slice(8, 16)), extra))
            return stores

        rows_loop(0, count, body, by)

    def x_coupling(r, p):
        return (2.0 * keep_x(r - X0)) * inverse(D[r, p] + D[r - 1, p])

    def coefficients(r):
        de, do, op = D[r, 0], D[r, 1], OP[r]
        sy_m, sy_p = de + op, de + do
        cye = two_y * inverse(sy_m)
        cyo = 2.0 * inverse(sy_p)
        stores = [
            (CYE, r, cye), (CYO, r, cyo), (WY, r, keep_y * sy_p * inverse(sy_m + sy_p)),
        ]
        for p in range(2):
            d = D[r, p]
            lo, up = d + z_lower(d), d + z_upper(d)
            czl = two_zl * inverse(lo)
            czu = two_zu * inverse(up)
            cxl, cxu = x_coupling(r, p), x_coupling(r + 1, p)
            ylo, yup = (cye, cyo) if p == 0 else (cyo, y_next(cye))
            diag = S[r, p] + cxl + cxu + ylo + yup + czl + czu
            di = DAMP * inverse(diag)
            stores += [
                (CZL, (r, p), czl), (CZU, (r, p), czu), (WZ, (r, p), keep_wz * up * inverse(lo + up)),
                (CX, (r + 1, p), cxu), (DG, (r, p), diag), (DI, (r, p), di), (U1, (r, p), di * B[r, p]),
            ]
        return stores

    def even_part(qa, qb):
        return jnp.where(lt64, qa, r64(qb))

    def odd_part(qa, qb):
        return jnp.where(lt64, r64(qa), qb)

    def z1(v):
        return pltpu.roll(v, 127, 1)

    def z_collapse_lateral(c_e, c_o, wa, wb):
        ha, hb = 1.0 - wa, 1.0 - wb
        wc = wa * c_e
        return {
            0: c_o + ha * hb * c_e + z1(wc * wb),
            1: z1(wc * hb),
            -1: (c_e - wc) * wb,
        }

    def build(xa, xb):
        stores = []
        r, q = xa + X0, xb + X0
        wz = [even_part(WZ[r, p], WZ[q, p]) for p in range(2)]
        wz_next = [even_part(WZ[r + 1, p], WZ[q + 1, p]) for p in range(2)]

        def put(refs, j, v):
            stores.extend(((refs[0], (xa + 4, j), v), (refs[1], (xb - 8, j), v)))

        cen, xup = [], []
        for p in range(2):
            wl = wz[p]
            wh = 1.0 - wl
            dge, dgo = even_part(DG[r, p], DG[q, p]), odd_part(DG[r, p], DG[q, p])
            cze, czo = -even_part(CZL[r, p], CZL[q, p]), -odd_part(CZL[r, p], CZL[q, p])
            wd = wl * dge
            c = dgo + wh * (wh * dge + 2.0 * czo) + z1(wl * (wd + 2.0 * cze))
            m = wh * (wd + cze) + wl * czo
            cen.append({-1: m, 0: c, 1: z1(m)})
            cxe = -even_part(CX[r + 1, p], CX[q + 1, p])
            cxo = -odd_part(CX[r + 1, p], CX[q + 1, p])
            xup.append(z_collapse_lateral(cxe, cxo, wl, wz_next[p]))
        we, wo = wz
        F = z_collapse_lateral(-even_part(CYO[r], CYO[q]), -odd_part(CYO[r], CYO[q]), we, wo)
        H = z_collapse_lateral(-even_part(CYE[r], CYE[q]), -odd_part(CYE[r], CYE[q]), we, y_prev(wo))
        vl = odd_part(WY[r], WY[q])
        vh = 1.0 - vl
        ul = odd_part(WY[r + 1], WY[q + 1])
        be, bo = cen
        vls = {d: shift(vl, 0, d) for d in (-1, 0, 1)}
        vhs = {d: 1.0 - vls[d] for d in (-1, 0, 1)}
        uls = {d: shift(ul, 0, d) for d in (-1, 0, 1)}
        uhs = {d: 1.0 - uls[d] for d in (-1, 0, 1)}
        Ht = {d: shift(H[-d], 0, d) for d in (-1, 0, 1)}
        Ft = {d: shift(F[-d], 0, d) for d in (0, 1)}
        for d in (0, 1):
            v = (
                bo[d]
                + vh * (vhs[d] * be[d] + F[d])
                + vhs[d] * Ft[d]
                + y_next(vl * (vls[d] * be[d] + H[d]) + vls[d] * Ht[d])
            )
            put((CA0, CB0), HALF.index((0, d)), v)
        for d in (-1, 0, 1):
            v = y_next(vl * (vhs[d] * be[d] + F[d]) + vhs[d] * Ht[d])
            put((CA0, CB0), HALF.index((1, d)), v)
        xe, xo = xup
        for d in (-1, 0, 1):
            lx = vl * xe[d]
            hx = xe[d] - lx
            put((CA1, CB1), FULL.index((0, d)), xo[d] + hx * uhs[d] + y_next(lx * uls[d]))
            put((CA1, CB1), FULL.index((1, d)), y_next(lx * uhs[d]))
            put((CA1, CB1), FULL.index((-1, d)), hx * uls[d])
        return stores

    return locals()


def inner_kernel(tab_ref, pos_ref, wide_ref, *refs):
    arrays = dict(zip(CARRIED, refs))
    f = Fine(tab_ref, pos_ref, arrays)
    f.segment(LOW, 16, lambda i: wide_ref[i], BY[0])
    rows_loop(X0 + 1, X0 + 15, f.coefficients, BY[1])
    rows_loop(1, 7, lambda x: f.build(x, x + 7), BY[4])


def main_kernel(tab_ref, pos_ref, swap_ref, other_ref, *refs):
    refs = refs[len(CARRIED) :]
    fine_ref, mid_ref, low_ref = refs[:3]
    arrays = dict(zip(CARRIED, refs[3 : 3 + len(CARRIED)]))
    (U2, T, AL, SM, CM,
     E0, E1, UM, UN, Z0, Z1, L15, CMP, MD, MS) = refs[3 + len(CARRIED) :]
    D, B, CX, CYE, CYO, CZL, CZU, WZ, WY, DG, DI, U1, _, _, CA0, CA1, CB0, CB1 = (
        arrays[n] for n in CARRIED
    )
    f = Fine(tab_ref, pos_ref, arrays)
    sh, lane, lt64, even_x = f.sh, f.lane, f.lt64, f.even_x
    r64, y_next, y_prev, z_lower, z_upper = f.r64, f.y_next, f.y_prev, f.z_lower, f.z_upper
    keep_x, keep_y, odd_part, x_first, x_last = f.keep_x, f.keep_y, f.odd_part, f.x_first, f.x_last
    skip = HIGH - LOW
    f.segment(0, LOW, lambda i: jnp.where(even_x, other_ref[i + skip], swap_ref[i + skip]), BY[0])
    f.segment(LOW + 16, HIGH, lambda i: jnp.where(even_x, swap_ref[i], other_ref[i]), BY[0])
    for p in range(2):
        CX[1, p] = f.x_coupling(1, p)
    rows_loop(1, X0 + 1, f.coefficients, BY[1])
    rows_loop(X0 + 15, ROWS - 1, f.coefficients, BY[1])

    def neighbours(U, r):
        e, o = U[r, 0], U[r, 1]
        cye, cyo = CYE[r], CYO[r]
        out = []
        for p in range(2):
            u = (e, o)[p]
            if p == 0:
                along_y = cye * y_prev(o) + cyo * o
            else:
                along_y = cyo * e + y_next(cye * e)
            out.append(
                CX[r, p] * U[r - 1, p]
                + CX[r + 1, p] * U[r + 1, p]
                + along_y
                + CZL[r, p] * z_lower(u)
                + CZU[r, p] * z_upper(u)
            )
        return out

    def second(r):
        around = neighbours(U1, r)
        return [
            (U2, (r, p), U1[r, p] + DI[r, p] * ((1.0 - DAMP) * B[r, p] + around[p])) for p in range(2)
        ]

    rows_loop(2, ROWS - 2, second, BY[2])
    for p in range(2):
        fine_ref[:, p] = U2[X0 : X0 + 16, p, 0:8]

    def residual(r):
        around = neighbours(U2, r)
        t = []
        for p in range(2):
            v = B[r, p] - DG[r, p] * U2[r, p] + around[p]
            lowered = WZ[r, p] * v
            t.append(v + r64(v - lowered) + pltpu.roll(lowered, 63, 1))
        te = t[0] * WY[r]
        return [(T, r, t[1] + (t[0] - te) + y_next(te))]

    rows_loop(3, ROWS - 3, residual, BY[3])

    def x_weights(n):
        r = 3 + 2 * n
        d = D[r, 1]
        lo, up = d + D[r - 1, 1], d + D[r + 1, 1]
        return [(AL, n, keep_x(r - X0) * up * inverse(lo + up))]

    rows_loop(0, 14, x_weights, 7)

    def restrict_x(n):
        r = 3 + 2 * n
        return [(SM, n, T[r + 1] + (1.0 - AL[n]) * T[r] + AL[n + 1] * T[r + 2])]

    rows_loop(0, 13, restrict_x, 7)

    def mean_mid(n):
        r = 3 + 2 * n
        total = inverse(D[r, 0]) + inverse(D[r, 1]) + inverse(D[r + 1, 0]) + inverse(D[r + 1, 1])
        return [(CM, n, 0.125 * (total + r64(total)))]

    rows_loop(0, 13, mean_mid, 7)

    rows_loop(-4, 1, lambda x: f.build(x, x + 18), BY[4])
    rows_loop(7, 11, lambda x: f.build(x, x + 12), BY[4])

    def both(first, second, n, j):
        return jnp.where(lt64, first[n, j], second[n, j])

    def half_of(ref, n):
        return {s: ref[n, j] for j, s in enumerate(HALF)}

    def full_of(ref, n):
        return {s: ref[n, j] for j, s in enumerate(FULL)}

    def join6(n, ref):
        return odd_part(ref[n], ref[n + 6])

    def first_dim(a):
        n = 2 * a
        diag, up = collapse_rows(
            *({s: both(CA0, CB0, n + k, j) for j, s in enumerate(HALF)} for k in range(3)),
            *({s: both(CA1, CB1, n + k, j) for j, s in enumerate(FULL)} for k in range(3)),
            join6(a, AL), join6(a + 1, AL), 1, 1, True,
        )
        return [(E0, (a, j), diag[s]) for j, s in enumerate(HALF)] + [
            (E1, (a + 1, j), up[s]) for j, s in enumerate(FULL)
        ]

    rows_loop(0, 7, first_dim, BY[5])
    for j in range(9):
        E1[0, j] = r64(E1[6, j])
        E1[7, j] = r64(E1[1, j])

    def mid_first(a):
        di = DAMP * inverse(E0[a, 0])
        source = join6(a, SM)
        return [(MD, a, di), (MS, a, source), (UM, a + 1, di * source)]

    rows_loop(0, 7, mid_first, 7)
    UM[0] = r64(UM[6])
    UM[8] = r64(UM[2])

    def a1(U, a):
        return apply27(half_of(E0, a), full_of(E1, a + 1), full_of(E1, a), U[a], U[a + 1], U[a + 2])

    def mid_second(a):
        return [(UN, a + 1, UM[a + 1] + MD[a] * (MS[a] - a1(UM, a)))]

    rows_loop(0, 7, mid_second, BY[6])
    UN[0] = r64(UN[6])
    UN[8] = r64(UN[2])
    for i in range(4):
        mid_ref[i] = UN[i + 3, 0:8]
        mid_ref[i + 4] = UN[i + 1, 0:8]

    def mid_residual(a):
        return [(UM, a + 1, MS[a] - a1(UN, a))]

    rows_loop(0, 7, mid_residual, BY[6])

    def at(b, ref, j=None):
        if j is None:
            return jnp.where(lt64, ref[b + 2], ref[b])
        return jnp.where(lt64, ref[b + 2, j], ref[b, j])

    def at1(b, j=None):
        if j is None:
            return jnp.where(lt64, UM[b + 3], UM[b + 1])
        return jnp.where(lt64, E1[b + 3, j], E1[b + 1, j])

    def cm(b):
        return jnp.where(lt64, CM[b + 2], CM[b + 6])

    edge_z = jnp.where((lane == 0) | (lane == 64), 0.0, 1.0)

    def weight(g, before, after, keep):
        lo, up = before * (g + after), after * (g + before)
        return keep * lo * inverse(lo + up)

    def mid_z(b):
        g = cm(b)
        return weight(g, pltpu.roll(g, 1, 1), pltpu.roll(g, 127, 1), edge_z)

    def mid_y(b):
        g = cm(b)
        return weight(g, y_prev(g), y_next(g), keep_y)

    def mid_x(b):
        ka = jnp.where(x_first & (b == 0), 0.0, 1.0).astype(F32)
        kb = jnp.where(x_last & (b == 4), 0.0, 1.0).astype(F32)
        return weight(cm(b), cm(b - 1), cm(b + 1), jnp.where(lt64, ka, kb))

    def move_z(v, n):
        return shift(v, 0, n)

    def move_y(v, n):
        return shift(v, n, 0)

    def build_low(b):
        stores = []
        e0 = {s: at(b, E0, j) for j, s in enumerate(HALF)}
        e1 = {s: at1(b, j) for j, s in enumerate(FULL)}
        lz = (mid_z(b), mid_z(b + 1))
        z0, zz1 = {}, {}
        for dx in (0, 1):
            source, out = ((e0, z0), (e1, zz1))[dx]
            for dy in (-1, 0, 1):
                if dx == 0 and dy == -1:
                    continue
                lc = move_y(lz[dx], dy)
                if dx == 0 and dy == 0:
                    t0, tp = source[(0, 0)], source[(0, 1)]
                    tm = move_z(tp, -1)
                    want = (0, 1)
                else:
                    tm, t0, tp = (source[(dy, d)] for d in (-1, 0, 1))
                    want = (-1, 0, 1)
                for d, v in collapse_line(tm, t0, tp, lz[0], lc, move_z, want).items():
                    out[(dy, d)] = v
        ly = (mid_y(b), mid_y(b + 1))
        for d in (-1, 0, 1):
            lc = shift(ly[0], 0, d, 1, 2)
            want = (0, 1) if d >= 0 else (1,)
            t0 = z0[(0, d)] if d >= 0 else shift(z0[(0, 1)], 0, -1, 1, 2)
            tp = z0[(1, d)]
            tm = shift(z0[(1, -d)], -1, d, 1, 2)
            for dy, v in collapse_line(tm, t0, tp, ly[0], lc, move_y, want).items():
                stores.append((Z0, (b, HALF.index((dy, d))), v))
            lc = shift(ly[1], 0, d, 1, 2)
            tm, t0, tp = (zz1[(dy, d)] for dy in (-1, 0, 1))
            for dy, v in collapse_line(tm, t0, tp, ly[0], lc, move_y, (-1, 0, 1)).items():
                stores.append((Z1, (b, FULL.index((dy, d))), v))
        v = at1(b)
        lv = lz[0] * v
        v = v + move_z(v - lv, -1) + move_z(lv, 1)
        lv = ly[0] * v
        return stores + [(UN, b, v + move_y(v - lv, -1) + move_y(lv, 1))]

    rows_loop(0, 5, build_low, BY[7])

    for i in range(2):
        b = 2 * i
        w0, w2 = mid_x(b), mid_x(b + 2)
        diag, up = collapse_rows(
            half_of(Z0, b), half_of(Z0, b + 1), half_of(Z0, b + 2),
            full_of(Z1, b), full_of(Z1, b + 1), full_of(Z1, b + 2),
            w0, w2, 2, 2, True,
        )
        for j, s in enumerate(HALF):
            L15[i, j] = diag[s][0:8]
        for j, s in enumerate(FULL):
            L15[i, 5 + j] = up[s][0:8]
        L15[i, 14] = (UN[b + 1] + (1.0 - w0) * UN[b] + w2 * UN[b + 2])[0:8]
    src, dst = iota((128, 128), 0), iota((128, 128), 1)
    total = None
    for i in range(2):
        row, z = dst // 32, dst % 32
        hit = (src // 64 == row // 2) & (row % 2 == i) & (src % 64 == 2 * z + 1)
        part = jnp.dot(L15[i].reshape(120, 128), jnp.where(hit, 1.0, 0.0).astype(F32),
                       precision=HI, preferred_element_type=F32)
        total = part if total is None else total + part
    CMP[...] = total
    low_ref[0:60] = CMP[pl.ds(1, 60, stride=2), :]
    low_ref[60:64] = jnp.zeros((4, 128), F32)


def finish_kernel(fine_in, mid_in, fine_ref, mid_ref):
    order = depth_order(True)
    for p in range(2):
        part = jnp.dot(fine_in[:, p].reshape(128, 128), order, precision=HI, preferred_element_type=F32)
        fine_ref[:, pl.ds(p, 8, stride=2), :] = part.reshape(16, 8, 128)
    for i in range(4):
        mid_ref[i] = mid_in[i, :, 0:64]
        mid_ref[i + 4] = pltpu.roll(mid_in[i + 4], 64, 1)[:, 0:64]


def low_widen_kernel(pos_ref, own_ref, swap_ref, other_ref, wide_ref):
    even = pos_ref[5] == 0
    for j in range(15):
        rows = slice(4 * j, 4 * j + 4)
        own, one, two = own_ref[rows], swap_ref[rows], other_ref[rows]
        above, below = jnp.where(even, one, two), jnp.where(even, two, one)
        wide_ref[j] = jnp.concatenate([own, above, own, below], 0)


def low_kernel(pos_ref, own_ref, swap_ref, other_ref, out_ref, E, SRC):
    even = pos_ref[4] == 0
    for j in range(15):
        own, one, two = own_ref[j], swap_ref[j], other_ref[j]
        for b, v in enumerate((jnp.where(even, two, one), own, jnp.where(even, one, two))):
            if j < 14:
                E[b, j] = v
            else:
                SRC[b] = v
    lane = iota((16, 128), 1)
    last = lane >= 96
    first = lane < 32

    def after(rows, b):
        return pltpu.roll(jnp.where(first, rows[min(b + 1, 2)], rows[b]), 96, 1)

    def before(rows, b):
        return pltpu.roll(jnp.where(last, rows[max(b - 1, 0)], rows[b]), 32, 1)

    di = [DAMP * inverse(E[b, 0]) for b in range(3)]
    source = [SRC[b] for b in range(3)]
    cur = [di[b] * source[b] for b in range(3)]

    def lagged(products):
        return {
            dy: products[(dy, 0)] + shift(products[(dy, -1)], 0, 1) + shift(products[(dy, 1)], 0, -1)
            for dy in (-1, 0, 1)
        }

    for sweep in range(3):
        blocks = (0, 1, 2) if sweep < 2 else (1,)
        moved = [lagged({s: E[b, 5 + j] * cur[b] for j, s in enumerate(FULL)}) for b in range(3)]
        nxt = [None] * 3
        for b in blocks:
            u, u_after = cur[b], after(cur, b)
            total = E[b, 0] * u
            e0 = {s: E[b, j] for j, s in enumerate(HALF)}
            for dy in (-1, 0, 1):
                u_row, after_row = shift(u, dy, 0), shift(u_after, dy, 0)
                for dz in (-1, 0, 1):
                    s = (dy, dz)
                    total = total + E[b, 5 + FULL.index(s)] * shift(after_row, 0, dz)
                    if s in HALF and s != (0, 0):
                        total = total + e0[s] * shift(u_row, 0, dz)
                row = before([m[dy] for m in moved], b)
                if dy == 0:
                    row = row + shift(e0[(0, 1)] * u, 0, -1)
                if dy == 1:
                    row = row + e0[(1, 0)] * u + shift(e0[(1, -1)] * u, 0, 1) + shift(e0[(1, 1)] * u, 0, -1)
                total = total + shift(row, -dy, 0)
            nxt[b] = u + di[b] * (source[b] - total)
        cur = nxt
    result = cur[1]
    for i in range(4):
        out_ref[i] = pltpu.roll(result, (128 - 32 * i) % 128, 1)[0:4, 0:32] if i else result[0:4, 0:32]


def partners(axis, to_swap, to_other):
    n = lax.axis_size(axis)
    swap = [(i, i ^ 1) for i in range(n)]
    other = [(i, (i - 1 if i % 2 == 0 else i + 1) % n) for i in range(n)]
    far = lax.ppermute(to_other, axis, other)
    return lax.ppermute(to_swap, axis, swap), far


def per_device(material, velocity, density, right_side):
    shape = jax.ShapeDtypeStruct
    params = pltpu.CompilerParams(vmem_limit_bytes=48 * 1024 * 1024)
    smem, vmem = pl.BlockSpec(memory_space=pltpu.SMEM), pl.BlockSpec(memory_space=pltpu.VMEM)
    row_x, row_y = lax.axis_index("gx"), lax.axis_index("gy")
    position = jnp.stack(
        [
            row_x,
            (row_x == lax.axis_size("gx") - 1).astype(jnp.int32),
            row_y,
            (row_y == lax.axis_size("gy") - 1).astype(jnp.int32),
            row_x % 2,
            row_y % 2,
        ]
    ).astype(jnp.int32)
    tables = jnp.concatenate([density, velocity])
    own, to_swap, to_other = pl.pallas_call(
        pack_kernel,
        in_specs=[smem, vmem, vmem],
        out_specs=[vmem] * 3,
        out_shape=(shape((16, 4, 8, 128), F32), shape((8, 40, 128), F32), shape((8, 40, 128), F32)),
        compiler_params=params,
        name="pack",
    )(position, material.astype(F32), right_side)
    near = partners("gy", to_swap, to_other)
    wide, to_swap, to_other = pl.pallas_call(
        widen_kernel,
        in_specs=[smem] + [vmem] * 3,
        out_specs=[vmem] * 3,
        out_shape=(
            shape((16, 4, 16, 128), F32),
            shape((HIGH, 4, 16, 128), F32),
            shape((HIGH, 4, 16, 128), F32),
        ),
        compiler_params=params,
        name="widen",
    )(position, own, *near)
    vm = lambda *s: pltpu.VMEM(s, F32)
    two, one = (ROWS, 2, 16, 128), (ROWS, 16, 128)
    carried = [two, two, two, one, one, two, two, two, one, two, two, two, two, one]
    carried += [(15, n, 16, 128) for n in (5, 9, 5, 9)]
    carried = [shape(c, F32) for c in carried]
    count = len(carried)
    inner = pl.pallas_call(
        inner_kernel,
        in_specs=[smem, smem, vmem],
        out_specs=[vmem] * count,
        out_shape=carried,
        compiler_params=pltpu.CompilerParams(vmem_limit_bytes=24 * 1024 * 1024),
        cost_estimate=pl.CostEstimate(flops=20_000_000, bytes_accessed=8_000_000, transcendentals=0),
        name="inner",
    )(tables, position, wide)
    to_swap, *inner = lax.optimization_barrier((to_swap, *inner))
    near = partners("gx", to_swap, to_other)
    fine, mid, sent = pl.pallas_call(
        main_kernel,
        in_specs=[smem, smem] + [vmem] * (2 + count),
        out_specs=[vmem] * (3 + count),
        out_shape=[
            shape((16, 2, 8, 128), F32),
            shape((8, 8, 128), F32),
            shape((64, 128), F32),
        ] + carried,
        input_output_aliases={4 + n: 3 + n for n in range(count)},
        scratch_shapes=[
            vm(*two), vm(*one),
            vm(14, 16, 128), vm(13, 16, 128), vm(13, 16, 128),
            vm(7, 5, 16, 128), vm(8, 9, 16, 128), vm(9, 16, 128), vm(9, 16, 128),
            vm(5, 5, 16, 128), vm(5, 9, 16, 128), vm(2, 15, 8, 128), vm(120, 128), vm(7, 16, 128), vm(7, 16, 128),
        ],
        compiler_params=pltpu.CompilerParams(vmem_limit_bytes=24 * 1024 * 1024),
        name="levels",
    )(tables, position, *near, *inner)[:3]
    near = partners("gy", sent, sent)
    low = pl.pallas_call(
        low_widen_kernel,
        in_specs=[smem] + [vmem] * 3,
        out_specs=vmem,
        out_shape=shape((15, 16, 128), F32),
        compiler_params=params,
        name="low_widen",
    )(position, sent, *near)
    fine, mid = pl.pallas_call(
        finish_kernel,
        in_specs=[vmem] * 2,
        out_specs=[vmem] * 2,
        out_shape=(shape((16, 16, 128), F32), shape((8, 8, 64), F32)),
        compiler_params=params,
        name="finish",
    )(fine, mid)
    near = partners("gx", low, low)
    coarse = pl.pallas_call(
        low_kernel,
        in_specs=[smem] + [vmem] * 3,
        out_specs=vmem,
        out_shape=shape((4, 4, 32), F32),
        scratch_shapes=[vm(3, 14, 16, 128), vm(3, 16, 128)],
        compiler_params=params,
        name="coarse",
    )(position, low, *near)
    return fine, mid, coarse


def solution(mesh):
    return jax.shard_map(
        per_device,
        mesh=mesh,
        in_specs=(P("gx", "gy", None), P(), P(), P("gx", "gy", None)),
        out_specs=(P("gx", "gy", None), P("gx", "gy", None), P("gx", "gy", None)),
        check_vma=False,
    )
```

```python
import jax
import jax.numpy as jnp
from jax import lax
from jax.experimental import pallas as pl
from jax.experimental.pallas import tpu as pltpu
from jax.sharding import PartitionSpec as P

DAMP = 0.7
F32 = jnp.float32
LOW, HIGH = 7, 10
X0 = LOW
ROWS = LOW + 16 + HIGH
HALF = ((0, 0), (0, 1), (1, -1), (1, 0), (1, 1))
FULL = tuple((dy, dz) for dy in (-1, 0, 1) for dz in (-1, 0, 1))
HI = lax.Precision.HIGHEST
BY = (5, 5, 15, 9, 2, 4, 7, 5)


def neg(s):
    return (-s[0], -s[1])


def shift(v, dy, dz, sy=1, sz=1):
    rows, lanes = v.shape
    if dy:
        v = pltpu.roll(v, (-dy * sy) % rows, 0)
    if dz:
        v = pltpu.roll(v, (-dz * sz) % lanes, 1)
    return v


def rows_loop(first, last, body, by):
    def group(start, count):
        stores = []
        for k in range(count):
            stores += body(start + k)
        for ref, index, value in stores:
            ref[index] = value

    count = last - first
    whole = count // by
    if whole == 1:
        group(first, by)
    elif whole > 1:

        def step(n, _):
            group(first + n * by, by)
            return 0

        lax.fori_loop(0, whole, step, 0)
    if count % by:
        group(first + whole * by, count % by)


def inverse(v):
    return pl.reciprocal(v, approx=True)


def iota(shape, dim):
    return lax.broadcasted_iota(jnp.int32, shape, dim)


def depth_order(transposed):
    z = iota((128, 128), 1 if transposed else 0)
    c = iota((128, 128), 0 if transposed else 1)
    source = jnp.where(c < 64, 2 * c, 2 * c - 127)
    return jnp.where(z == source, 1.0, 0.0).astype(F32)


def pack_kernel(pos_ref, mat_ref, rhs_ref, own_ref, to_swap_ref, to_other_ref):
    order = depth_order(False)
    for q, ref in ((0, mat_ref), (2, rhs_ref)):
        for parity in range(2):
            part = ref[:, pl.ds(parity, 8, stride=2), :].reshape(128, 128)
            precision = HI if q else None
            part = jnp.dot(part, order, precision=precision, preferred_element_type=F32)
            own_ref[:, q + parity] = part.reshape(16, 8, 128)
    even_y = pos_ref[5] == 0

    def send(i, _):
        for n in range(2):
            for q in range(4):
                up, down = own_ref[2 * i + n, q, 3:8], own_ref[2 * i + n, q, 0:5]
                at = slice(20 * n + 5 * q, 20 * n + 5 * q + 5)
                to_swap_ref[i, at] = jnp.where(even_y, up, down)
                to_other_ref[i, at] = jnp.where(even_y, down, up)
        return 0

    lax.fori_loop(0, 8, send, 0, unroll=True)


def widen_kernel(pos_ref, own_ref, swap_ref, other_ref, wide_ref, to_swap_ref, to_other_ref):
    even_x, even_y = pos_ref[4] == 0, pos_ref[5] == 0
    wide_ref[:, :, 0:8] = own_ref[...]

    def receive(i, _):
        for n in range(2):
            for q in range(4):
                at = slice(20 * n + 5 * q, 20 * n + 5 * q + 5)
                one, two = swap_ref[i, at], other_ref[i, at]
                above, below = jnp.where(even_y, one, two), jnp.where(even_y, two, one)
                wide_ref[2 * i + n, q, 8:13] = above
                wide_ref[2 * i + n, q, 13:16] = below[2:5]
                if q == 1:
                    special = below[1:2]
                if q == 3:
                    wide_ref[2 * i + n, q, 12:13] = special
        return 0

    lax.fori_loop(0, 8, receive, 0, unroll=True)
    start = jnp.where(even_x, 16 - HIGH, 0)

    def copy(i, _):
        to_swap_ref[i] = wide_ref[start + i]
        to_other_ref[i] = wide_ref[(16 - HIGH) - start + i]
        return 0

    lax.fori_loop(0, HIGH, copy, 0, unroll=True)


def pick(index, table):
    b0 = (index & 1) == 1
    b1 = (index & 2) == 2
    b2 = (index & 4) == 4
    q = [jnp.where(b0, table[2 * n + 1], table[2 * n]) for n in range(4)]
    q = [jnp.where(b1, q[2 * n + 1], q[2 * n]) for n in range(2)]
    return jnp.where(b2, q[1], q[0])


def collapse_line(tm, t0, tp, l, lc, move, want):
    h, hc = 1.0 - l, 1.0 - lc
    out = {}
    hcp = move(hc, 1)
    lcm = move(lc, -1)
    if 0 in want:
        low = move(h * (hc * t0 + tp), -1)
        high = move(l * (lc * t0 + tm), 1)
        out[0] = t0 + low + high + tm * move(hc, -1) + tp * move(lc, 1)
    if 1 in want:
        out[1] = move(l * (hc * t0 + tp), 1) + tp * hcp
    if -1 in want:
        out[-1] = move(h * (lc * t0 + tm), -1) + tm * lcm
    return out


def collapse_rows(d0, d1, d2, c0, c1, c2, a0, a2, sy, sz, upper):
    h0 = 1.0 - a0
    diag, up = {}, {}
    for s in HALF:
        a2s = shift(a2, *s, sy, sz)
        h0s = 1.0 - shift(a0, *s, sy, sz)
        t10 = shift(c0[neg(s)], *s, sy, sz)
        t21 = shift(c1[neg(s)], *s, sy, sz)
        diag[s] = (
            d1[s]
            + h0 * (h0s * d0[s] + c0[s])
            + h0s * t10
            + a2 * (a2s * d2[s] + t21)
            + a2s * c1[s]
        )
    if upper:
        for s in FULL:
            h2s = 1.0 - shift(a2, *s, sy, sz)
            d2s = d2[s] if s in HALF else shift(d2[neg(s)], *s, sy, sz)
            up[s] = a2 * (h2s * d2s + c2[s]) + h2s * c1[s]
    return diag, up


def apply27(e0, e1, e1_before, u_before, u, u_after):
    total = e0[(0, 0)] * u
    back = {}
    for dy in (-1, 0, 1):
        for dz in (-1, 0, 1):
            s = (dy, dz)
            total = total + e1[s] * shift(u_after, dy, dz)
            if s in HALF and s != (0, 0):
                total = total + e0[s] * shift(u, dy, dz)
    for dy in (-1, 0, 1):
        row = None
        for dz in (-1, 0, 1):
            s = (dy, dz)
            product = e1_before[s] * u_before
            if s in HALF and s != (0, 0):
                product = product + e0[s] * u
            product = shift(product, 0, -dz)
            row = product if row is None else row + product
        total = total + shift(row, -dy, 0)
    return total


def halves(n, shape):
    return iota(shape, 1) < n


CARRIED = ("D", "B", "CX", "CYE", "CYO", "CZL", "CZU", "WZ", "WY", "DG", "DI", "U1", "S", "OP", "CA0", "CA1", "CB0", "CB1")


class Fine:
    def __init__(self, tab_ref, pos_ref, arrays):
        for name, value in fine_work(tab_ref, pos_ref, **arrays).items():
            setattr(self, name, value)


def fine_work(tab_ref, pos_ref, D, S, B, OP, CX, CYE, CYO, CZL, CZU, WZ, WY, DG, DI, U1, CA0, CA1, CB0, CB1):
    sh = (16, 128)
    lane = iota(sh, 1)
    subl = iota(sh, 0)
    lt64 = lane < 64
    x_first = pos_ref[0] == 0
    x_last = pos_ref[1] == 1
    y_first = pos_ref[2] == 0
    y_last = pos_ref[3] == 1
    yc = jnp.where(y_first, 0, -1)
    yd = jnp.where(y_last, 8, -1)
    keep_y = jnp.where((subl == yc) | (subl == yd), 0.0, 1.0)
    keep_zl = jnp.where(lane == 0, 0.0, 1.0)
    keep_zu = jnp.where(lane == 127, 0.0, 1.0)
    two_y, two_zl, two_zu = 2.0 * keep_y, 2.0 * keep_zl, 2.0 * keep_zu
    keep_wz = jnp.where((lane == 0) | (lane >= 64), 0.0, 1.0)

    def keep_x(x):
        cut = (x_first & (x == 0)) | (x_last & (x == 16))
        return jnp.where(cut, 0.0, 1.0).astype(F32)

    def r64(v):
        return pltpu.roll(v, 64, 1)

    def z_lower(v):
        return jnp.where(lt64, pltpu.roll(v, 65, 1), r64(v))

    def z_upper(v):
        return jnp.where(lt64, r64(v), pltpu.roll(v, 63, 1))

    def y_next(v):
        return pltpu.roll(v, 15, 0)

    def y_prev(v):
        return pltpu.roll(v, 1, 0)

    tsh = (8, 128)
    den = [jnp.full(tsh, tab_ref[n], F32) for n in range(8)]
    vel = [jnp.full(tsh, tab_ref[8 + n], F32) for n in range(8)]
    sft = [3.0 / (d * v * v) for d, v in zip(den, vel)]
    s8 = iota(tsh, 0)

    even_x = pos_ref[4] == 0

    def segment(first, count, get, by):
        def body(i):
            r = first + i
            v = get(i)
            stores = []
            for p in range(2):
                half = []
                for t in range(2):
                    rows = slice(8 * t, 8 * t + 8)
                    m = v[p][rows].astype(jnp.int32)
                    d = pick(m, den)
                    half.append(d)
                    stores.append((S, (r, p, rows), pick(m, sft)))
                dd = jnp.concatenate(half, 0)
                stores.append((D, (r, p), dd))
                stores.append((B, (r, p), v[2 + p]))
                if p == 1:
                    dd = y_prev(dd)
                    special = pick(v[3][8:16].astype(jnp.int32), den)
                    stores.append((OP, (r, slice(0, 8)), dd[0:8]))
                    extra = jnp.where(s8 == 5, pltpu.roll(special, 1, 0), dd[8:16])
                    stores.append((OP, (r, slice(8, 16)), extra))
            return stores

        rows_loop(0, count, body, by)

    def x_coupling(r, p):
        return (2.0 * keep_x(r - X0)) * inverse(D[r, p] + D[r - 1, p])

    def coefficients(r):
        de, do, op = D[r, 0], D[r, 1], OP[r]
        sy_m, sy_p = de + op, de + do
        cye = two_y * inverse(sy_m)
        cyo = 2.0 * inverse(sy_p)
        stores = [
            (CYE, r, cye), (CYO, r, cyo), (WY, r, keep_y * sy_p * inverse(sy_m + sy_p)),
        ]
        for p in range(2):
            d = D[r, p]
            lo, up = d + z_lower(d), d + z_upper(d)
            czl = two_zl * inverse(lo)
            czu = two_zu * inverse(up)
            cxl, cxu = x_coupling(r, p), x_coupling(r + 1, p)
            ylo, yup = (cye, cyo) if p == 0 else (cyo, y_next(cye))
            diag = S[r, p] + cxl + cxu + ylo + yup + czl + czu
            di = DAMP * inverse(diag)
            stores += [
                (CZL, (r, p), czl), (CZU, (r, p), czu), (WZ, (r, p), keep_wz * up * inverse(lo + up)),
                (CX, (r + 1, p), cxu), (DG, (r, p), diag), (DI, (r, p), di), (U1, (r, p), di * B[r, p]),
            ]
        return stores

    def even_part(qa, qb):
        return jnp.where(lt64, qa, r64(qb))

    def odd_part(qa, qb):
        return jnp.where(lt64, r64(qa), qb)

    def z1(v):
        return pltpu.roll(v, 127, 1)

    def z_collapse_lateral(c_e, c_o, wa, wb):
        ha, hb = 1.0 - wa, 1.0 - wb
        wc = wa * c_e
        return {
            0: c_o + ha * hb * c_e + z1(wc * wb),
            1: z1(wc * hb),
            -1: (c_e - wc) * wb,
        }

    def build(xa, xb):
        stores = []
        r, q = xa + X0, xb + X0
        wz = [even_part(WZ[r, p], WZ[q, p]) for p in range(2)]
        wz_next = [even_part(WZ[r + 1, p], WZ[q + 1, p]) for p in range(2)]

        def put(refs, j, v):
            stores.extend(((refs[0], (xa + 4, j), v), (refs[1], (xb - 8, j), v)))

        cen, xup = [], []
        for p in range(2):
            wl = wz[p]
            wh = 1.0 - wl
            dge, dgo = even_part(DG[r, p], DG[q, p]), odd_part(DG[r, p], DG[q, p])
            cze, czo = -even_part(CZL[r, p], CZL[q, p]), -odd_part(CZL[r, p], CZL[q, p])
            wd = wl * dge
            c = dgo + wh * (wh * dge + 2.0 * czo) + z1(wl * (wd + 2.0 * cze))
            m = wh * (wd + cze) + wl * czo
            cen.append({-1: m, 0: c, 1: z1(m)})
            cxe = -even_part(CX[r + 1, p], CX[q + 1, p])
            cxo = -odd_part(CX[r + 1, p], CX[q + 1, p])
            xup.append(z_collapse_lateral(cxe, cxo, wl, wz_next[p]))
        we, wo = wz
        F = z_collapse_lateral(-even_part(CYO[r], CYO[q]), -odd_part(CYO[r], CYO[q]), we, wo)
        H = z_collapse_lateral(-even_part(CYE[r], CYE[q]), -odd_part(CYE[r], CYE[q]), we, y_prev(wo))
        vl = odd_part(WY[r], WY[q])
        vh = 1.0 - vl
        ul = odd_part(WY[r + 1], WY[q + 1])
        be, bo = cen
        vls = {d: shift(vl, 0, d) for d in (-1, 0, 1)}
        vhs = {d: 1.0 - vls[d] for d in (-1, 0, 1)}
        uls = {d: shift(ul, 0, d) for d in (-1, 0, 1)}
        uhs = {d: 1.0 - uls[d] for d in (-1, 0, 1)}
        Ht = {d: shift(H[-d], 0, d) for d in (-1, 0, 1)}
        Ft = {d: shift(F[-d], 0, d) for d in (0, 1)}
        for d in (0, 1):
            v = (
                bo[d]
                + vh * (vhs[d] * be[d] + F[d])
                + vhs[d] * Ft[d]
                + y_next(vl * (vls[d] * be[d] + H[d]) + vls[d] * Ht[d])
            )
            put((CA0, CB0), HALF.index((0, d)), v)
        for d in (-1, 0, 1):
            v = y_next(vl * (vhs[d] * be[d] + F[d]) + vhs[d] * Ht[d])
            put((CA0, CB0), HALF.index((1, d)), v)
        xe, xo = xup
        for d in (-1, 0, 1):
            lx = vl * xe[d]
            hx = xe[d] - lx
            put((CA1, CB1), FULL.index((0, d)), xo[d] + hx * uhs[d] + y_next(lx * uls[d]))
            put((CA1, CB1), FULL.index((1, d)), y_next(lx * uhs[d]))
            put((CA1, CB1), FULL.index((-1, d)), hx * uls[d])
        return stores

    return locals()


def inner_kernel(tab_ref, pos_ref, wide_ref, *refs):
    arrays = dict(zip(CARRIED, refs))
    f = Fine(tab_ref, pos_ref, arrays)
    f.segment(LOW, 16, lambda i: wide_ref[i], BY[0])
    rows_loop(X0 + 1, X0 + 15, f.coefficients, BY[1])
    rows_loop(1, 7, lambda x: f.build(x, x + 7), BY[4])


def main_kernel(tab_ref, pos_ref, swap_ref, other_ref, *refs):
    refs = refs[len(CARRIED) :]
    fine_ref, mid_ref, low_ref = refs[:3]
    arrays = dict(zip(CARRIED, refs[3 : 3 + len(CARRIED)]))
    (U2, T, AL, SM, CM,
     E0, E1, UM, UN, Z0, Z1, L15, CMP, MD, MS) = refs[3 + len(CARRIED) :]
    D, B, CX, CYE, CYO, CZL, CZU, WZ, WY, DG, DI, U1, _, _, CA0, CA1, CB0, CB1 = (
        arrays[n] for n in CARRIED
    )
    f = Fine(tab_ref, pos_ref, arrays)
    sh, lane, lt64, even_x = f.sh, f.lane, f.lt64, f.even_x
    r64, y_next, y_prev, z_lower, z_upper = f.r64, f.y_next, f.y_prev, f.z_lower, f.z_upper
    keep_x, keep_y, odd_part, x_first, x_last = f.keep_x, f.keep_y, f.odd_part, f.x_first, f.x_last
    skip = HIGH - LOW
    f.segment(0, LOW, lambda i: jnp.where(even_x, other_ref[i + skip], swap_ref[i + skip]), BY[0])
    f.segment(LOW + 16, HIGH, lambda i: jnp.where(even_x, swap_ref[i], other_ref[i]), BY[0])
    for p in range(2):
        CX[1, p] = f.x_coupling(1, p)
    rows_loop(1, X0 + 1, f.coefficients, BY[1])
    rows_loop(X0 + 15, ROWS - 1, f.coefficients, BY[1])

    def neighbours(U, r):
        e, o = U[r, 0], U[r, 1]
        cye, cyo = CYE[r], CYO[r]
        out = []
        for p in range(2):
            u = (e, o)[p]
            if p == 0:
                along_y = cye * y_prev(o) + cyo * o
            else:
                along_y = cyo * e + y_next(cye * e)
            out.append(
                CX[r, p] * U[r - 1, p]
                + CX[r + 1, p] * U[r + 1, p]
                + along_y
                + CZL[r, p] * z_lower(u)
                + CZU[r, p] * z_upper(u)
            )
        return out

    def second(r):
        around = neighbours(U1, r)
        return [
            (U2, (r, p), U1[r, p] + DI[r, p] * ((1.0 - DAMP) * B[r, p] + around[p])) for p in range(2)
        ]

    rows_loop(2, ROWS - 2, second, BY[2])
    for p in range(2):
        fine_ref[:, p] = U2[X0 : X0 + 16, p, 0:8]

    def residual(r):
        around = neighbours(U2, r)
        t = []
        for p in range(2):
            v = B[r, p] - DG[r, p] * U2[r, p] + around[p]
            lowered = WZ[r, p] * v
            t.append(v + r64(v - lowered) + pltpu.roll(lowered, 63, 1))
        te = t[0] * WY[r]
        return [(T, r, t[1] + (t[0] - te) + y_next(te))]

    rows_loop(3, ROWS - 3, residual, BY[3])

    def x_weights(n):
        r = 3 + 2 * n
        d = D[r, 1]
        lo, up = d + D[r - 1, 1], d + D[r + 1, 1]
        return [(AL, n, keep_x(r - X0) * up * inverse(lo + up))]

    rows_loop(0, 14, x_weights, 7)

    def restrict_x(n):
        r = 3 + 2 * n
        return [(SM, n, T[r + 1] + (1.0 - AL[n]) * T[r] + AL[n + 1] * T[r + 2])]

    rows_loop(0, 13, restrict_x, 7)

    def mean_mid(n):
        r = 3 + 2 * n
        total = inverse(D[r, 0]) + inverse(D[r, 1]) + inverse(D[r + 1, 0]) + inverse(D[r + 1, 1])
        return [(CM, n, 0.125 * (total + r64(total)))]

    rows_loop(0, 13, mean_mid, 7)

    rows_loop(-4, 1, lambda x: f.build(x, x + 18), BY[4])
    rows_loop(7, 11, lambda x: f.build(x, x + 12), BY[4])

    def both(first, second, n, j):
        return jnp.where(lt64, first[n, j], second[n, j])

    def half_of(ref, n):
        return {s: ref[n, j] for j, s in enumerate(HALF)}

    def full_of(ref, n):
        return {s: ref[n, j] for j, s in enumerate(FULL)}

    def join6(n, ref):
        return odd_part(ref[n], ref[n + 6])

    def first_dim(a):
        n = 2 * a
        diag, up = collapse_rows(
            *({s: both(CA0, CB0, n + k, j) for j, s in enumerate(HALF)} for k in range(3)),
            *({s: both(CA1, CB1, n + k, j) for j, s in enumerate(FULL)} for k in range(3)),
            join6(a, AL), join6(a + 1, AL), 1, 1, True,
        )
        return [(E0, (a, j), diag[s]) for j, s in enumerate(HALF)] + [
            (E1, (a + 1, j), up[s]) for j, s in enumerate(FULL)
        ]

    rows_loop(0, 7, first_dim, BY[5])
    for j in range(9):
        E1[0, j] = r64(E1[6, j])
        E1[7, j] = r64(E1[1, j])

    def mid_first(a):
        di = DAMP * inverse(E0[a, 0])
        source = join6(a, SM)
        return [(MD, a, di), (MS, a, source), (UM, a + 1, di * source)]

    rows_loop(0, 7, mid_first, 7)
    UM[0] = r64(UM[6])
    UM[8] = r64(UM[2])

    def a1(U, a):
        return apply27(half_of(E0, a), full_of(E1, a + 1), full_of(E1, a), U[a], U[a + 1], U[a + 2])

    def mid_second(a):
        return [(UN, a + 1, UM[a + 1] + MD[a] * (MS[a] - a1(UM, a)))]

    rows_loop(0, 7, mid_second, BY[6])
    UN[0] = r64(UN[6])
    UN[8] = r64(UN[2])
    for i in range(4):
        mid_ref[i] = UN[i + 3, 0:8]
        mid_ref[i + 4] = UN[i + 1, 0:8]

    def mid_residual(a):
        return [(UM, a + 1, MS[a] - a1(UN, a))]

    rows_loop(0, 7, mid_residual, BY[6])

    def at(b, ref, j=None):
        if j is None:
            return jnp.where(lt64, ref[b + 2], ref[b])
        return jnp.where(lt64, ref[b + 2, j], ref[b, j])

    def at1(b, j=None):
        if j is None:
            return jnp.where(lt64, UM[b + 3], UM[b + 1])
        return jnp.where(lt64, E1[b + 3, j], E1[b + 1, j])

    def cm(b):
        return jnp.where(lt64, CM[b + 2], CM[b + 6])

    edge_z = jnp.where((lane == 0) | (lane == 64), 0.0, 1.0)

    def weight(g, before, after, keep):
        lo, up = before * (g + after), after * (g + before)
        return keep * lo * inverse(lo + up)

    def mid_z(b):
        g = cm(b)
        return weight(g, pltpu.roll(g, 1, 1), pltpu.roll(g, 127, 1), edge_z)

    def mid_y(b):
        g = cm(b)
        return weight(g, y_prev(g), y_next(g), keep_y)

    def mid_x(b):
        ka = jnp.where(x_first & (b == 0), 0.0, 1.0).astype(F32)
        kb = jnp.where(x_last & (b == 4), 0.0, 1.0).astype(F32)
        return weight(cm(b), cm(b - 1), cm(b + 1), jnp.where(lt64, ka, kb))

    def move_z(v, n):
        return shift(v, 0, n)

    def move_y(v, n):
        return shift(v, n, 0)

    def build_low(b):
        stores = []
        e0 = {s: at(b, E0, j) for j, s in enumerate(HALF)}
        e1 = {s: at1(b, j) for j, s in enumerate(FULL)}
        lz = (mid_z(b), mid_z(b + 1))
        z0, zz1 = {}, {}
        for dx in (0, 1):
            source, out = ((e0, z0), (e1, zz1))[dx]
            for dy in (-1, 0, 1):
                if dx == 0 and dy == -1:
                    continue
                lc = move_y(lz[dx], dy)
                if dx == 0 and dy == 0:
                    t0, tp = source[(0, 0)], source[(0, 1)]
                    tm = move_z(tp, -1)
                    want = (0, 1)
                else:
                    tm, t0, tp = (source[(dy, d)] for d in (-1, 0, 1))
                    want = (-1, 0, 1)
                for d, v in collapse_line(tm, t0, tp, lz[0], lc, move_z, want).items():
                    out[(dy, d)] = v
        ly = (mid_y(b), mid_y(b + 1))
        for d in (-1, 0, 1):
            lc = shift(ly[0], 0, d, 1, 2)
            want = (0, 1) if d >= 0 else (1,)
            t0 = z0[(0, d)] if d >= 0 else shift(z0[(0, 1)], 0, -1, 1, 2)
            tp = z0[(1, d)]
            tm = shift(z0[(1, -d)], -1, d, 1, 2)
            for dy, v in collapse_line(tm, t0, tp, ly[0], lc, move_y, want).items():
                stores.append((Z0, (b, HALF.index((dy, d))), v))
            lc = shift(ly[1], 0, d, 1, 2)
            tm, t0, tp = (zz1[(dy, d)] for dy in (-1, 0, 1))
            for dy, v in collapse_line(tm, t0, tp, ly[0], lc, move_y, (-1, 0, 1)).items():
                stores.append((Z1, (b, FULL.index((dy, d))), v))
        v = at1(b)
        lv = lz[0] * v
        v = v + move_z(v - lv, -1) + move_z(lv, 1)
        lv = ly[0] * v
        return stores + [(UN, b, v + move_y(v - lv, -1) + move_y(lv, 1))]

    rows_loop(0, 5, build_low, BY[7])

    for i in range(2):
        b = 2 * i
        w0, w2 = mid_x(b), mid_x(b + 2)
        diag, up = collapse_rows(
            half_of(Z0, b), half_of(Z0, b + 1), half_of(Z0, b + 2),
            full_of(Z1, b), full_of(Z1, b + 1), full_of(Z1, b + 2),
            w0, w2, 2, 2, True,
        )
        for j, s in enumerate(HALF):
            L15[i, j] = diag[s][0:8]
        for j, s in enumerate(FULL):
            L15[i, 5 + j] = up[s][0:8]
        L15[i, 14] = (UN[b + 1] + (1.0 - w0) * UN[b] + w2 * UN[b + 2])[0:8]
    src, dst = iota((128, 128), 0), iota((128, 128), 1)
    total = None
    for i in range(2):
        row, z = dst // 32, dst % 32
        hit = (src // 64 == row // 2) & (row % 2 == i) & (src % 64 == 2 * z + 1)
        part = jnp.dot(L15[i].reshape(120, 128), jnp.where(hit, 1.0, 0.0).astype(F32),
                       precision=HI, preferred_element_type=F32)
        total = part if total is None else total + part
    CMP[...] = total
    low_ref[0:60] = CMP[pl.ds(1, 60, stride=2), :]
    low_ref[60:64] = jnp.zeros((4, 128), F32)


def finish_kernel(fine_in, mid_in, fine_ref, mid_ref):
    order = depth_order(True)
    for p in range(2):
        part = jnp.dot(fine_in[:, p].reshape(128, 128), order, precision=HI, preferred_element_type=F32)
        fine_ref[:, pl.ds(p, 8, stride=2), :] = part.reshape(16, 8, 128)
    for i in range(4):
        mid_ref[i] = mid_in[i, :, 0:64]
        mid_ref[i + 4] = pltpu.roll(mid_in[i + 4], 64, 1)[:, 0:64]


def low_widen_kernel(pos_ref, own_ref, swap_ref, other_ref, wide_ref):
    even = pos_ref[5] == 0
    for j in range(15):
        rows = slice(4 * j, 4 * j + 4)
        own, one, two = own_ref[rows], swap_ref[rows], other_ref[rows]
        above, below = jnp.where(even, one, two), jnp.where(even, two, one)
        wide_ref[j] = jnp.concatenate([own, above, own, below], 0)


def low_kernel(pos_ref, own_ref, swap_ref, other_ref, out_ref, E, SRC):
    even = pos_ref[4] == 0
    for j in range(15):
        own, one, two = own_ref[j], swap_ref[j], other_ref[j]
        for b, v in enumerate((jnp.where(even, two, one), own, jnp.where(even, one, two))):
            if j < 14:
                E[b, j] = v
            else:
                SRC[b] = v
    lane = iota((16, 128), 1)
    last = lane >= 96
    first = lane < 32

    def after(rows, b):
        return pltpu.roll(jnp.where(first, rows[min(b + 1, 2)], rows[b]), 96, 1)

    def before(rows, b):
        return pltpu.roll(jnp.where(last, rows[max(b - 1, 0)], rows[b]), 32, 1)

    di = [DAMP * inverse(E[b, 0]) for b in range(3)]
    source = [SRC[b] for b in range(3)]
    cur = [di[b] * source[b] for b in range(3)]

    def lagged(products):
        return {
            dy: products[(dy, 0)] + shift(products[(dy, -1)], 0, 1) + shift(products[(dy, 1)], 0, -1)
            for dy in (-1, 0, 1)
        }

    for sweep in range(3):
        blocks = (0, 1, 2) if sweep < 2 else (1,)
        moved = [lagged({s: E[b, 5 + j] * cur[b] for j, s in enumerate(FULL)}) for b in range(3)]
        nxt = [None] * 3
        for b in blocks:
            u, u_after = cur[b], after(cur, b)
            total = E[b, 0] * u
            e0 = {s: E[b, j] for j, s in enumerate(HALF)}
            for dy in (-1, 0, 1):
                u_row, after_row = shift(u, dy, 0), shift(u_after, dy, 0)
                for dz in (-1, 0, 1):
                    s = (dy, dz)
                    total = total + E[b, 5 + FULL.index(s)] * shift(after_row, 0, dz)
                    if s in HALF and s != (0, 0):
                        total = total + e0[s] * shift(u_row, 0, dz)
                row = before([m[dy] for m in moved], b)
                if dy == 0:
                    row = row + shift(e0[(0, 1)] * u, 0, -1)
                if dy == 1:
                    row = row + e0[(1, 0)] * u + shift(e0[(1, -1)] * u, 0, 1) + shift(e0[(1, 1)] * u, 0, -1)
                total = total + shift(row, -dy, 0)
            nxt[b] = u + di[b] * (source[b] - total)
        cur = nxt
    result = cur[1]
    for i in range(4):
        out_ref[i] = pltpu.roll(result, (128 - 32 * i) % 128, 1)[0:4, 0:32] if i else result[0:4, 0:32]


def partners(axis, to_swap, to_other):
    n = lax.axis_size(axis)
    swap = [(i, i ^ 1) for i in range(n)]
    other = [(i, (i - 1 if i % 2 == 0 else i + 1) % n) for i in range(n)]
    far = lax.ppermute(to_other, axis, other)
    return lax.ppermute(to_swap, axis, swap), far


def per_device(material, velocity, density, right_side):
    shape = jax.ShapeDtypeStruct
    params = pltpu.CompilerParams(vmem_limit_bytes=48 * 1024 * 1024)
    smem, vmem = pl.BlockSpec(memory_space=pltpu.SMEM), pl.BlockSpec(memory_space=pltpu.VMEM)
    row_x, row_y = lax.axis_index("gx"), lax.axis_index("gy")
    position = jnp.stack(
        [
            row_x,
            (row_x == lax.axis_size("gx") - 1).astype(jnp.int32),
            row_y,
            (row_y == lax.axis_size("gy") - 1).astype(jnp.int32),
            row_x % 2,
            row_y % 2,
        ]
    ).astype(jnp.int32)
    tables = jnp.concatenate([density, velocity])
    own, to_swap, to_other = pl.pallas_call(
        pack_kernel,
        in_specs=[smem, vmem, vmem],
        out_specs=[vmem] * 3,
        out_shape=(shape((16, 4, 8, 128), F32), shape((8, 40, 128), F32), shape((8, 40, 128), F32)),
        compiler_params=params,
        name="pack",
    )(position, material.astype(F32), right_side)
    near = partners("gy", to_swap, to_other)
    wide, to_swap, to_other = pl.pallas_call(
        widen_kernel,
        in_specs=[smem] + [vmem] * 3,
        out_specs=[vmem] * 3,
        out_shape=(
            shape((16, 4, 16, 128), F32),
            shape((HIGH, 4, 16, 128), F32),
            shape((HIGH, 4, 16, 128), F32),
        ),
        compiler_params=params,
        name="widen",
    )(position, own, *near)
    vm = lambda *s: pltpu.VMEM(s, F32)
    two, one = (ROWS, 2, 16, 128), (ROWS, 16, 128)
    carried = [two, two, two, one, one, two, two, two, one, two, two, two, two, one]
    carried += [(15, n, 16, 128) for n in (5, 9, 5, 9)]
    carried = [shape(c, F32) for c in carried]
    count = len(carried)
    inner = pl.pallas_call(
        inner_kernel,
        in_specs=[smem, smem, vmem],
        out_specs=[vmem] * count,
        out_shape=carried,
        compiler_params=pltpu.CompilerParams(vmem_limit_bytes=24 * 1024 * 1024),
        cost_estimate=pl.CostEstimate(flops=20_000_000, bytes_accessed=8_000_000, transcendentals=0),
        name="inner",
    )(tables, position, wide)
    to_swap, *inner = lax.optimization_barrier((to_swap, *inner))
    near = partners("gx", to_swap, to_other)
    fine, mid, sent = pl.pallas_call(
        main_kernel,
        in_specs=[smem, smem] + [vmem] * (2 + count),
        out_specs=[vmem] * (3 + count),
        out_shape=[
            shape((16, 2, 8, 128), F32),
            shape((8, 8, 128), F32),
            shape((64, 128), F32),
        ] + carried,
        input_output_aliases={4 + n: 3 + n for n in range(count)},
        scratch_shapes=[
            vm(*two), vm(*one),
            vm(14, 16, 128), vm(13, 16, 128), vm(13, 16, 128),
            vm(7, 5, 16, 128), vm(8, 9, 16, 128), vm(9, 16, 128), vm(9, 16, 128),
            vm(5, 5, 16, 128), vm(5, 9, 16, 128), vm(2, 15, 8, 128), vm(120, 128), vm(7, 16, 128), vm(7, 16, 128),
        ],
        compiler_params=pltpu.CompilerParams(vmem_limit_bytes=24 * 1024 * 1024),
        name="levels",
    )(tables, position, *near, *inner)[:3]
    near = partners("gy", sent, sent)
    low = pl.pallas_call(
        low_widen_kernel,
        in_specs=[smem] + [vmem] * 3,
        out_specs=vmem,
        out_shape=shape((15, 16, 128), F32),
        compiler_params=params,
        name="low_widen",
    )(position, sent, *near)
    fine, mid = pl.pallas_call(
        finish_kernel,
        in_specs=[vmem] * 2,
        out_specs=[vmem] * 2,
        out_shape=(shape((16, 16, 128), F32), shape((8, 8, 64), F32)),
        compiler_params=params,
        name="finish",
    )(fine, mid)
    near = partners("gx", low, low)
    coarse = pl.pallas_call(
        low_kernel,
        in_specs=[smem] + [vmem] * 3,
        out_specs=vmem,
        out_shape=shape((4, 4, 32), F32),
        scratch_shapes=[vm(3, 14, 16, 128), vm(3, 16, 128)],
        compiler_params=params,
        name="coarse",
    )(position, low, *near)
    return fine, mid, coarse


def solution(mesh):
    return jax.shard_map(
        per_device,
        mesh=mesh,
        in_specs=(P("gx", "gy", None), P(), P(), P("gx", "gy", None)),
        out_specs=(P("gx", "gy", None), P("gx", "gy", None), P("gx", "gy", None)),
        check_vma=False,
    )
```
